128 devices in a mesh: seq: 32 (over x, z, core), dp: 4 (over y).
Axes of the slice: x: 4, y: 4, z: 4, core: 2. Of those that a mesh axis runs over, the one named last changes fastest.
Arguments:
- tokens: bfloat16 [4, 6144, 640], P('dp', 'seq'), may hold values from -6 to 6
- lengths: int32 [4, 2], P('dp'), may hold values from 2048 to 4096, as said below
- w_query: bfloat16 [640, 1024], replicated, may hold values from -0.25 to 0.25
- w_key: bfloat16 [640, 256], replicated, may hold values from -0.25 to 0.25
- w_value: bfloat16 [640, 256], replicated, may hold values from -0.25 to 0.25
- w_output: bfloat16 [1024, 640], replicated, may hold values from -1.5 to 1.5
- w_gate: bfloat16 [640, 2048], replicated, may hold values from -0.25 to 0.25
- w_up: bfloat16 [640, 2048], replicated, may hold values from -0.25 to 0.25
- w_down: bfloat16 [2048, 640], replicated, may hold values from -0.125 to 0.125
- gain_attn: float32 [640], replicated, may hold values from 0.1 to 1.9
- gain_mlp: float32 [640], replicated, may hold values from 0.1 to 1.9
- out_grad: bfloat16 [4, 6144, 640], P('dp', 'seq'), may hold values from -6 to 6
Outputs:
- block_out: bfloat16 [4, 6144, 640], P('dp', 'seq')
- shared_kv: bfloat16 [4, 6144, 512], P('dp', 'seq')
- input_grad: float32 [4, 6144, 640], P('dp', 'seq')
- grad_query: float32 [640, 1024], replicated
- grad_key: float32 [640, 256], replicated
- grad_value: float32 [640, 256], replicated
- grad_proj: float32 [1024, 640], replicated
- grad_gate: float32 [640, 2048], replicated
- grad_up: float32 [640, 2048], replicated
- grad_down: float32 [2048, 640], replicated
- grad_gain_attn: float32 [640], replicated
- grad_gain_mlp: float32 [640], replicated
The draws below stay inside these ranges and needn't reach their ends.
Inputs may be any that keep to these rules, and one draw needn't show every extreme that they name: `lengths`: in each row, 1 entries are 2048 and 1 are 4096, in an order drawn for each row.
All inputs are finite; a program needn't handle non-finite values.
Results may differ from the reference program's by a relative error of at most 0.015.
Values may be sent and summed in bfloat16 or wider, within the bound.
No kernel may reach another device: no remote copies, remote signals or barrier semaphores. Data moves between devices by JAX's collectives and lax.ppermute only.
A program may use at most 128 MiB of HBM per device.

```python
import jax
import jax.numpy as jnp
from jax import lax

D = 640
HEADS = 4
HEAD_DIM = 256
FF = 2048
WINDOW = 1024
SHORT_LEN = 2048
PAIRS = 1
TOK_DEV = 192
GROUP_TOK = 6144
GROUPS = 4
N_SEQ = 32


def shuffle_row(row_key, base):
    return jax.random.permutation(row_key, base)


def draw_lengths(key, part):
    key = jax.random.fold_in(key, 11)
    base = jnp.concatenate([jnp.full((PAIRS,), SHORT_LEN, dtype=jnp.int32), jnp.full((PAIRS,), 2 * SHORT_LEN, dtype=jnp.int32)])
    row_keys = jax.random.split(key, GROUPS)
    return jax.vmap(shuffle_row, in_axes=(0, None))(row_keys, base).astype(jnp.int32)


def levels(own_key, shape, cuts, smallest, largest):
    gain, own = 1.0, jax.random.fold_in(own_key, 6)
    for dim, parts in cuts:
        steps = jnp.exp(jax.random.uniform(jax.random.fold_in(own, dim), (parts,), jnp.float32, smallest / len(cuts), largest / len(cuts)))
        gain = gain * jnp.repeat(steps, shape[dim] // parts).reshape([-1 if axis == dim else 1 for axis in range(len(shape))])
    return gain


def noise(stream_key, dims, scale, reach, shards=(), kind=jnp.bfloat16):
    factor_of = levels(stream_key, dims, shards, -0.22, 0.18) if shards else 1.0
    entries = jax.random.normal(stream_key, dims, jnp.float32) * scale * factor_of
    return jnp.minimum(jnp.maximum(entries, -reach), reach).astype(kind)


def setup_inputs(seed: int = 0) -> dict:
    keys = jax.random.split(jax.random.key(seed), 13)
    return {
        "tokens": noise(keys[0], (GROUPS, GROUP_TOK, D), 1.0, 6.0, ((0, 4), (1, 32))),
        "lengths": draw_lengths(jax.random.fold_in(keys[12], 71), 0),
        "w_query": noise(keys[2], (D, HEADS * HEAD_DIM), D ** -0.5, 0.25),
        "w_key": noise(keys[3], (D, HEAD_DIM), D ** -0.5, 0.25),
        "w_value": noise(keys[4], (D, HEAD_DIM), D ** -0.5, 0.25),
        "w_output": noise(keys[5], (HEADS * HEAD_DIM, D), (HEADS * HEAD_DIM * 16 // WINDOW) ** -0.5, 1.5),
        "w_gate": noise(keys[6], (D, FF), D ** -0.5, 0.25),
        "w_up": noise(keys[7], (D, FF), D ** -0.5, 0.25),
        "w_down": noise(keys[8], (FF, D), FF ** -0.5, 0.125),
        "gain_attn": jnp.clip(1.0 + 0.18 * jax.random.normal(keys[9], (D,), jnp.float32), 0.1, 1.9),
        "gain_mlp": jnp.clip(1.0 + 0.18 * jax.random.normal(keys[10], (D,), jnp.float32), 0.1, 1.9),
        "out_grad": noise(keys[11], (GROUPS, GROUP_TOK, D), 1.0, 6.0, ((0, 4), (1, 32))),
    }


@jax.custom_vjp
def low(v):
    return lax.optimization_barrier(v.astype(jnp.bfloat16)).astype(jnp.float32)

@jax.custom_vjp
def low_back(v):
    return v

def low_keep(v):
    return (low(v), None)

def low_pass(kept, grad):
    return (grad,)

def back_keep(v):
    return (v, None)

def back_low(kept, grad):
    return (low(grad),)
low.defvjp(low_keep, low_pass)
low_back.defvjp(back_keep, back_low)
epsilon = 1e-06
theta_base = 10000.0
masked_score = -1e+30

def product(left, right):
    return jnp.dot(left, right, precision=lax.Precision.HIGHEST, preferred_element_type=jnp.float32)

def rms_scale(values):
    return lax.rsqrt(lax.optimization_barrier(jnp.mean(values * values, axis=-1, keepdims=True)) + epsilon)

def rotary_tables(positions, head_dim):
    half_dim = head_dim // 2
    frequency = theta_base ** (-(jnp.arange(half_dim, dtype=jnp.float32) * 2.0 / head_dim))
    angles = positions.astype(jnp.float32)[:, None] * frequency[None, :]
    cosine_half = jnp.cos(angles)
    sine_half = jnp.sin(angles)
    return (jnp.concatenate([cosine_half, cosine_half], axis=1), jnp.concatenate([sine_half, sine_half], axis=1))

def rotate(values, cosine_table, sine_table):
    half_dim = values.shape[-1] // 2
    turned = jnp.concatenate([-values[..., half_dim:], values[..., :half_dim]], axis=-1)
    return values * cosine_table + turned * sine_table

def token_layout(lengths):
    pieces = lengths // N_SEQ
    offsets = jnp.cumsum(pieces, axis=1) - pieces
    starts = jnp.cumsum(lengths, axis=1) - lengths
    slot_index = jnp.arange(TOK_DEV, dtype=jnp.int32)
    member = lax.optimization_barrier(jnp.sum((slot_index[None, :, None] >= offsets[:, None, :]).astype(jnp.int32), axis=2)) - 1
    onehot = (member[:, :, None] == jnp.arange(2 * PAIRS, dtype=jnp.int32)[None, None, :]).astype(jnp.int32)
    own_piece = lax.optimization_barrier(jnp.sum(onehot * pieces[:, None, :], axis=2))
    own_offset = lax.optimization_barrier(jnp.sum(onehot * offsets[:, None, :], axis=2))
    own_start = lax.optimization_barrier(jnp.sum(onehot * starts[:, None, :], axis=2))
    devices = jnp.arange(N_SEQ, dtype=jnp.int32)
    position = devices[None, :, None] * own_piece[:, None, :] + (slot_index[None, :] - own_offset)[:, None, :]
    natural = own_start[:, None, :] + position
    member_full = jnp.broadcast_to(member[:, None, :], position.shape)
    return (member_full.reshape(GROUPS, GROUP_TOK).astype(jnp.int32), position.reshape(GROUPS, GROUP_TOK).astype(jnp.int32), natural.reshape(GROUPS, GROUP_TOK).astype(jnp.int32))

def attend(queries, key_rows, value_rows, member_nat, position_nat):
    row_count = queries.shape[0]
    block_rows = min(512, SHORT_LEN)
    block_count = row_count // block_rows
    score_scale = queries.shape[2] ** (-0.5)
    pad_keys = jnp.concatenate([jnp.zeros((WINDOW, key_rows.shape[1]), key_rows.dtype), key_rows], axis=0)
    pad_values = jnp.concatenate([jnp.zeros((WINDOW, value_rows.shape[1]), value_rows.dtype), value_rows], axis=0)
    pad_member = jnp.concatenate([jnp.full((WINDOW,), -1, jnp.int32), member_nat])
    pad_position = jnp.concatenate([jnp.zeros((WINDOW,), jnp.int32), position_nat])

    def one_block(number):
        first_row = (number * block_rows).astype(jnp.int32)
        query_block = lax.dynamic_slice_in_dim(queries, first_row, block_rows, 0)
        query_member = lax.dynamic_slice_in_dim(member_nat, first_row, block_rows, 0)
        query_position = lax.dynamic_slice_in_dim(position_nat, first_row, block_rows, 0)
        key_block = lax.dynamic_slice_in_dim(pad_keys, first_row, block_rows + WINDOW, 0)
        value_block = lax.dynamic_slice_in_dim(pad_values, first_row, block_rows + WINDOW, 0)
        key_member = lax.dynamic_slice_in_dim(pad_member, first_row, block_rows + WINDOW, 0)
        key_position = lax.dynamic_slice_in_dim(pad_position, first_row, block_rows + WINDOW, 0)
        raw_scores = jnp.einsum('qhd,kd->hqk', query_block, key_block, precision=lax.Precision.HIGHEST) * score_scale
        scores = low_back(raw_scores)
        distance = query_position[:, None] - key_position[None, :]
        allowed = (query_member[:, None] == key_member[None, :]) & (distance >= 0) & (distance < WINDOW)
        scores = jnp.where(allowed[None], scores, masked_score)
        row_max = lax.optimization_barrier(jnp.max(scores, axis=-1, keepdims=True))
        exponent = jnp.exp(scores - row_max)
        attn_probs = exponent / lax.optimization_barrier(jnp.sum(exponent, axis=-1, keepdims=True))
        return jnp.einsum('hqk,kd->qhd', low(attn_probs), value_block, precision=lax.Precision.HIGHEST)
    mixed = lax.map(jax.checkpoint(one_block), jnp.arange(block_count, dtype=jnp.int32))
    return mixed.reshape(row_count, queries.shape[1], queries.shape[2])

def reference(tokens, lengths, w_query, w_key, w_value, w_output, w_gate, w_up, w_down, gain_attn, gain_mlp, out_grad):
    member, position, natural = token_layout(lengths)
    inverse = jnp.argsort(natural, axis=1).astype(jnp.int32)
    group_ids = jnp.arange(GROUPS, dtype=jnp.int32)[:, None]
    member_nat = jnp.take_along_axis(member + group_ids * (2 * PAIRS), inverse, axis=1).reshape(-1)
    position_nat = jnp.take_along_axis(position, inverse, axis=1).reshape(-1)
    head_dim = w_key.shape[1]
    cosine_table, sine_table = rotary_tables(position_nat, head_dim)

    def to_natural(values):
        return jnp.take_along_axis(values, inverse[:, :, None], axis=1).reshape(GROUPS * GROUP_TOK, values.shape[2])

    def to_devices(values):
        return jnp.take_along_axis(values.reshape(GROUPS, GROUP_TOK, values.shape[1]), natural[:, :, None], axis=1)

    def forward(block_in, query_mat, key_mat, value_mat, output_mat, gate_mat, up_mat, down_mat, gain_first, gain_second):
        tokens_nat = to_natural(block_in)
        row_count = tokens_nat.shape[0]
        normed = low(tokens_nat * rms_scale(tokens_nat) * gain_first)
        query_raw = low_back(product(normed, query_mat))
        key_raw = low_back(product(normed, key_mat))
        value_raw = low_back(product(normed, value_mat))
        queries = low(rotate(query_raw.reshape(row_count, -1, head_dim), cosine_table[:, None, :], sine_table[:, None, :]))
        key_rows = low(rotate(key_raw, cosine_table, sine_table))
        value_rows = low(value_raw)
        mixed = attend(queries, key_rows, value_rows, member_nat, position_nat)
        mixed = low_back(low(mixed.reshape(row_count, -1)))
        resid = tokens_nat + low_back(product(mixed, output_mat))
        normed_mlp = low(resid * rms_scale(resid) * gain_second)
        gate = low_back(product(normed_mlp, gate_mat))
        upward = low_back(product(normed_mlp, up_mat))
        act = low(jax.nn.silu(gate) * upward)
        block_out = resid + product(act, down_mat)
        return (to_devices(block_out), to_devices(jnp.concatenate([key_rows, value_rows], axis=1)))
    block_out, pullback, shared_kv = jax.vjp(forward, tokens.astype(jnp.float32), w_query.astype(jnp.float32), w_key.astype(jnp.float32), w_value.astype(jnp.float32), w_output.astype(jnp.float32), w_gate.astype(jnp.float32), w_up.astype(jnp.float32), w_down.astype(jnp.float32), gain_attn, gain_mlp, has_aux=True)
    grads = pullback(out_grad.astype(jnp.float32))
    return (block_out.astype(jnp.bfloat16), shared_kv.astype(jnp.bfloat16), grads[0], grads[1], grads[2], grads[3], grads[4], grads[5], grads[6], grads[7], grads[8], grads[9])
```

```python
import jax
import jax.numpy as jnp
from jax import lax
from jax.experimental import pallas as pl
from jax.experimental.pallas import tpu as pltpu
from jax.sharding import Mesh, PartitionSpec as P

WINDOW = 1024
SHORT_LEN = 2048
D = 640
HEADS = 4
HD = 256
HALF = 128
FF = 2048
TOK = 192
SHORT = 64
LONG = 128
CHIPS = 16
NEAR = 4
FAR = 8
SIDE = (NEAR + 1) * TOK + (FAR - NEAR) * SHORT
GROUPS = SIDE // SHORT
KEYS_SHORT = 2 * (FAR + 1) * SHORT
KEYS_LONG = 2 * (NEAR + 1) * LONG
KEYS = KEYS_SHORT + KEYS_LONG
FF_CHUNK = 512

epsilon = 1e-06
theta_base = 10000.0
masked_score = -1e30

SEQ = ("x", "z", "core")
CHIP = ("x", "z")
RING = ("x", "z", "dp")
ALL = ("x", "z", "core", "dp")
B_ROWS = 8192

bf16 = jnp.bfloat16
f32 = jnp.float32


def mm(left, right):
    return jnp.dot(left, right, preferred_element_type=f32)


def mm_tn(left, right):
    return lax.dot_general(left, right, (((0,), (0,)), ((), ())), preferred_element_type=f32)


def mm_nt(left, right):
    return lax.dot_general(left, right, (((1,), (1,)), ((), ())), preferred_element_type=f32)


def window_groups():
    groups = []
    for behind in range(NEAR + 1):
        groups += [(behind, "short", 0), (behind, "long", 0), (behind, "long", 1)]
    groups += [(behind, "short", 0) for behind in range(NEAR + 1, FAR + 1)]
    return groups


def key_row(side, group):
    behind, kind, part = group
    if kind == "short":
        return side * (KEYS_SHORT // 2) + behind * SHORT
    return KEYS_SHORT + side * (KEYS_LONG // 2) + behind * LONG + part * SHORT


def mask_bias(kind, chip, core):
    rows, width, first_key = (SHORT, KEYS_SHORT, 0) if kind == "short" else (LONG, KEYS_LONG, 0)
    half = width // 2
    column = lax.broadcasted_iota(jnp.int32, (1, width), 1)
    other = (column >= half).astype(jnp.int32)
    inner = column - other * half
    shift = 6 if kind == "short" else 7
    behind = lax.shift_right_logical(inner, shift)
    rest = inner & (rows - 1)
    key_core = core + other * (1 - 2 * core)
    key_position = (2 * (chip - behind) + key_core) * rows + rest
    query_position = (2 * chip + core) * rows + lax.broadcasted_iota(jnp.int32, (rows, 1), 0)
    distance = query_position - key_position
    allowed = (key_position >= 0) & (distance >= 0) & (distance < WINDOW)
    return jnp.where(allowed, 0.0, masked_score).astype(f32)


def group_tables(cosb, sinb, cosr, sinr, index):
    cb, sb = cosb[index : index + 1, :], sinb[index : index + 1, :]
    cr, sr = cosr[...], sinr[...]
    return cb * cr - sb * sr, sb * cr + cb * sr


KINDS = (
    ("short", SHORT, 0, KEYS_SHORT, 0, 0),
    ("long", LONG, KEYS_SHORT, KEYS_LONG, HEADS * SHORT, SHORT),
)


def forward_kernel(
    info, cosb, sinb, cosr, sinr, ga, gm, win_h, og_h, wq_h, wk_h, wv_h, wo_h, wg_h, wu_h, wd_h,
    q_o, k_o, v_o, gmix_o, norm_o, gres_o, ggain_o, bo_h, skv_h, gg_h, gu_h, gd_h, gp_h,
    win, og, wq, wk, wv, wo, wg, wu, wd, kv, mixed, bo, skv, gg, gu, gd, gp, bias_s, bias_l, sems,
):
    chip, core, short_at, long_at = info[0], info[1], info[2], info[3]
    short_at = pl.multiple_of(short_at, SHORT)
    long_at = pl.multiple_of(long_at, SHORT)
    loads = {}
    for number, (name, source, target) in enumerate((
        ("win", win_h, win), ("wk", wk_h, wk), ("wv", wv_h, wv), ("wq", wq_h, wq), ("wo", wo_h, wo),
        ("ogs", og_h.at[pl.ds(short_at, SHORT)], og.at[pl.ds(0, SHORT)]),
        ("ogl", og_h.at[pl.ds(long_at, LONG)], og.at[pl.ds(SHORT, LONG)]),
        ("wg", wg_h, wg), ("wu", wu_h, wu), ("wd", wd_h, wd),
    )):
        loads[name] = pltpu.make_async_copy(source, target, sems.at[number])
        loads[name].start()
    stores = []

    def store(source, target):
        copy = pltpu.make_async_copy(source, target, sems.at[10 + len(stores)])
        copy.start()
        stores.append(copy)

    bias_s[...] = mask_bias("short", chip, core)
    bias_l[...] = mask_bias("long", chip, core)
    gain_a = ga[...]
    gain_m = gm[...]
    loads["win"].wait()

    def normalise(step, carry):
        rows = pl.ds(pl.multiple_of(step * SHORT, SHORT), SHORT)
        x = win[rows, :].astype(f32)
        scale = lax.rsqrt(jnp.mean(x * x, axis=-1, keepdims=True) + epsilon)
        norm_o[rows, :] = (x * scale * gain_a).astype(bf16)
        return carry

    lax.fori_loop(0, 2 * GROUPS, normalise, 0)
    loads["wk"].wait()
    loads["wv"].wait()
    for side in range(2):
        normed = norm_o[side * SIDE : (side + 1) * SIDE, :]
        kv[:, :HD] = mm(normed, wk[...])
        kv[:, HD:] = mm(normed, wv[...])
        for number, group in enumerate(window_groups()):
            rows = slice(number * SHORT, (number + 1) * SHORT)
            cos, sin = group_tables(cosb, sinb, cosr, sinr, side * GROUPS + number)
            low_half, high_half = kv[rows, :HALF], kv[rows, HALF:HD]
            at = key_row(side, group)
            k_o[at : at + SHORT, :HALF] = (low_half * cos - high_half * sin).astype(bf16)
            k_o[at : at + SHORT, HALF:] = (high_half * cos + low_half * sin).astype(bf16)
            v_o[at : at + SHORT, :] = kv[rows, HD:].astype(bf16)
            if side == 0 and number < 3:
                skv[rows, :HD] = k_o[at : at + SHORT, :]
                skv[rows, HD:] = v_o[at : at + SHORT, :]
    store(skv.at[pl.ds(0, SHORT)], skv_h.at[pl.ds(short_at, SHORT)])
    store(skv.at[pl.ds(SHORT, LONG)], skv_h.at[pl.ds(long_at, LONG)])

    loads["wq"].wait()
    query_raw = mm(norm_o[:TOK, :], wq[...])
    for number in range(3):
        rows = slice(number * SHORT, (number + 1) * SHORT)
        cos, sin = group_tables(cosb, sinb, cosr, sinr, number)
        for head in range(HEADS):
            low_half = query_raw[rows, head * HD : head * HD + HALF]
            high_half = query_raw[rows, head * HD + HALF : (head + 1) * HD]
            at = head * SHORT if number == 0 else HEADS * SHORT + head * LONG + (number - 1) * SHORT
            turned_low = (low_half * cos - high_half * sin).astype(bf16) * bf16(HD**-0.5)
            turned_high = (high_half * cos + low_half * sin).astype(bf16) * bf16(HD**-0.5)
            q_o[at : at + SHORT, :HALF] = turned_low
            q_o[at : at + SHORT, HALF:] = turned_high

    for kind, rows, key_at, width, query_at, row_at in KINDS:
        bias = bias_s if kind == "short" else bias_l
        for head in range(HEADS):
            queries = q_o[query_at + head * rows : query_at + (head + 1) * rows, :]
            scores = mm_nt(queries, k_o[key_at : key_at + width, :]) + bias[...]
            exponent = jnp.exp(scores - jnp.max(scores, axis=-1, keepdims=True))
            total = jnp.sum(exponent, axis=-1, keepdims=True)
            probs_low = (exponent / total).astype(bf16)
            mixed[row_at : row_at + rows, head * HD : (head + 1) * HD] = mm(
                probs_low, v_o[key_at : key_at + width, :]
            ).astype(bf16)

    loads["wo"].wait()
    resid = win[:TOK, :].astype(f32) + mm(mixed[...], wo[...])
    scale = lax.rsqrt(jnp.mean(resid * resid, axis=-1, keepdims=True) + epsilon)
    unit = resid * scale
    normed_mlp = (unit * gain_m).astype(bf16)
    for name in ("ogs", "ogl", "wg", "wu", "wd"):
        loads[name].wait()
    grad_out = og[...]
    block_out = resid
    grad_normed = jnp.zeros((TOK, D), f32)
    for chunk in range(FF // FF_CHUNK):
        cols = slice(chunk * FF_CHUNK, (chunk + 1) * FF_CHUNK)
        gate = mm(normed_mlp, wg[:, cols])
        up = mm(normed_mlp, wu[:, cols])
        sig = jax.nn.sigmoid(gate)
        silu = gate * sig
        act = (silu * up).astype(bf16)
        grad_act = mm_nt(grad_out, wd[cols, :])
        grad_gate = (grad_act * up * sig * (1.0 + gate * (1.0 - sig))).astype(bf16)
        grad_up = (grad_act * silu).astype(bf16)
        block_out = block_out + mm(act, wd[cols, :])
        grad_normed = grad_normed + mm_nt(grad_gate, wg[:, cols]) + mm_nt(grad_up, wu[:, cols])
        gd[cols, :] = mm_tn(act, grad_out).astype(bf16)
        gg[:, cols] = mm_tn(normed_mlp, grad_gate).astype(bf16)
        gu[:, cols] = mm_tn(normed_mlp, grad_up).astype(bf16)
        store(gd.at[pl.ds(chunk * FF_CHUNK, FF_CHUNK)], gd_h.at[pl.ds(chunk * FF_CHUNK, FF_CHUNK)])
    store(gg, gg_h)
    store(gu, gu_h)
    bo[...] = block_out.astype(bf16)
    store(bo.at[pl.ds(0, SHORT)], bo_h.at[pl.ds(short_at, SHORT)])
    store(bo.at[pl.ds(SHORT, LONG)], bo_h.at[pl.ds(long_at, LONG)])
    ggain_o[...] = jnp.sum(grad_normed * unit, axis=0, keepdims=True)
    scaled = grad_normed * gain_m
    grad_resid = grad_out.astype(f32) + scale * (
        scaled - unit * jnp.mean(scaled * unit, axis=-1, keepdims=True)
    )
    gres_o[...] = grad_resid
    grad_branch = grad_resid.astype(bf16)
    gp[...] = mm_tn(mixed[...], grad_branch).astype(bf16)
    store(gp, gp_h)
    grad_mixed = mm_nt(grad_branch, wo[...]).astype(bf16)
    for head in range(HEADS):
        cols = slice(head * HD, (head + 1) * HD)
        gmix_o[head * SHORT : (head + 1) * SHORT, :] = grad_mixed[:SHORT, cols]
        at = HEADS * SHORT + head * LONG
        gmix_o[at : at + LONG, :] = grad_mixed[SHORT:, cols]
    for copy in stores:
        copy.wait()


def backward_kernel(
    info, cosb, sinb, cosr, sinr, ggain, q, k, v, gmix, norm, wq,
    b_o, ret_o, gnq_o,
    probs_s, probs_l, gs_s, gs_l, bias_s, bias_l, gq,
):
    chip, core = info[0], info[1]
    bias_s[...] = mask_bias("short", chip, core)
    bias_l[...] = mask_bias("long", chip, core)
    for kind, rows, key_at, width, query_at, row_at in KINDS:
        bias, probs_all, gs_all = (bias_s, probs_s, gs_s) if kind == "short" else (bias_l, probs_l, gs_l)
        keys = k[key_at : key_at + width, :]
        values = v[key_at : key_at + width, :]
        for head in range(HEADS):
            here = slice(query_at + head * rows, query_at + (head + 1) * rows)
            scores = mm_nt(q[here, :], keys) + bias[...]
            exponent = jnp.exp(scores - jnp.max(scores, axis=-1, keepdims=True))
            probs = exponent / jnp.sum(exponent, axis=-1, keepdims=True)
            probs_all[head * rows : (head + 1) * rows, :] = probs.astype(bf16)
            grad_probs = mm_nt(gmix[here, :], values)
            inner = jnp.sum(probs * grad_probs, axis=-1, keepdims=True)
            grad_scores = (probs * (grad_probs - inner)).astype(bf16)
            gs_all[head * rows : (head + 1) * rows, :] = grad_scores
            grad_queries = mm(grad_scores, keys) * (HD**-0.5)
            for part in range(rows // SHORT):
                number = 0 if kind == "short" else 1 + part
                cos, sin = group_tables(cosb, sinb, cosr, sinr, number)
                low_half = grad_queries[part * SHORT : (part + 1) * SHORT, :HALF]
                high_half = grad_queries[part * SHORT : (part + 1) * SHORT, HALF:]
                at = row_at + part * SHORT
                gq[at : at + SHORT, head * HD : head * HD + HALF] = (
                    low_half * cos + high_half * sin
                ).astype(bf16)
                gq[at : at + SHORT, head * HD + HALF : (head + 1) * HD] = (
                    high_half * cos - low_half * sin
                ).astype(bf16)
        stack = slice(query_at, query_at + HEADS * rows)
        grad_keys = mm_tn(gs_all[...], q[stack, :])
        grad_values = mm_tn(probs_all[...], gmix[stack, :])
        for side in range(2):
            for number, group in enumerate(window_groups()):
                if group[1] != kind:
                    continue
                at = key_row(side, group) - key_at
                cos, sin = group_tables(cosb, sinb, cosr, sinr, side * GROUPS + number)
                low_half = grad_keys[at : at + SHORT, :HALF]
                high_half = grad_keys[at : at + SHORT, HALF:]
                to = side * SIDE + number * SHORT
                ret_o[to : to + SHORT, :HALF] = (low_half * cos + high_half * sin).astype(bf16)
                ret_o[to : to + SHORT, HALF:HD] = (high_half * cos - low_half * sin).astype(bf16)
                ret_o[to : to + SHORT, HD:] = grad_values[at : at + SHORT, :].astype(bf16)
    gnq_o[...] = mm_nt(gq[...], wq[...])
    for chunk in range(HEADS):
        grad_wq = mm_tn(norm[:TOK, :], gq[:, chunk * HD : (chunk + 1) * HD]).astype(bf16)
        for part in range(2):
            at = (2 * chunk + part) * D
            b_o[at : at + D, :] = grad_wq[:, part * HALF : (part + 1) * HALF]
    for chunk in range(2):
        grad_wkv = mm_tn(norm[...], ret_o[:, chunk * HD : (chunk + 1) * HD]).astype(bf16)
        for part in range(2):
            at = (8 + 2 * chunk + part) * D
            b_o[at : at + D, :] = grad_wkv[:, part * HALF : (part + 1) * HALF]
    b_o[12 * D :, :] = jnp.zeros((B_ROWS - 12 * D, HALF), bf16)
    for part in range(D // HALF):
        b_o[12 * D + 16 * part : 12 * D + 16 * part + 16, :] = jnp.broadcast_to(
            ggain[:, part * HALF : (part + 1) * HALF], (16, HALF)
        ).astype(bf16)


VMEM = pl.BlockSpec(memory_space=pltpu.VMEM)
SMEM = pl.BlockSpec(memory_space=pltpu.SMEM)
ANY = pl.BlockSpec(memory_space=pl.ANY)


def shape(dims, kind=bf16):
    return jax.ShapeDtypeStruct(dims, kind)


def run_forward(*operands):
    return pl.pallas_call(
        forward_kernel,
        in_specs=[SMEM] + [VMEM] * 6 + [ANY] * 9,
        out_specs=[VMEM] * 7 + [ANY] * 6,
        out_shape=[
            shape((HEADS * TOK, HD)), shape((KEYS, HD)), shape((KEYS, HD)), shape((HEADS * TOK, HD)),
            shape((2 * SIDE, D)), shape((TOK, D), f32), shape((1, D), f32),
            shape((TOK, D)), shape((TOK, 2 * HD)),
            shape((D, FF)), shape((D, FF)), shape((FF, D)), shape((HEADS * HD, D)),
        ],
        scratch_shapes=[
            pltpu.VMEM((2 * SIDE, D), bf16), pltpu.VMEM((TOK, D), bf16),
            pltpu.VMEM((D, HEADS * HD), bf16), pltpu.VMEM((D, HD), bf16), pltpu.VMEM((D, HD), bf16),
            pltpu.VMEM((HEADS * HD, D), bf16), pltpu.VMEM((D, FF), bf16), pltpu.VMEM((D, FF), bf16),
            pltpu.VMEM((FF, D), bf16),
            pltpu.VMEM((SIDE, 2 * HD), f32), pltpu.VMEM((TOK, HEADS * HD), bf16),
            pltpu.VMEM((TOK, D), bf16), pltpu.VMEM((TOK, 2 * HD), bf16),
            pltpu.VMEM((D, FF), bf16), pltpu.VMEM((D, FF), bf16), pltpu.VMEM((FF, D), bf16),
            pltpu.VMEM((HEADS * HD, D), bf16),
            pltpu.VMEM((SHORT, KEYS_SHORT), f32), pltpu.VMEM((LONG, KEYS_LONG), f32),
            pltpu.SemaphoreType.DMA((24,)),
        ],
        compiler_params=pltpu.CompilerParams(vmem_limit_bytes=58 * 2**20),
        cost_estimate=pl.CostEstimate(flops=10**10, bytes_accessed=4 * 10**7, transcendentals=10**6),
        name="forward",
    )(*operands)


def run_backward(*operands):
    return pl.pallas_call(
        backward_kernel,
        in_specs=[SMEM] + [VMEM] * 11,
        out_specs=[VMEM] * 3,
        out_shape=[shape((B_ROWS, HALF)), shape((2 * SIDE, 2 * HD)), shape((TOK, D), f32)],
        scratch_shapes=[
            pltpu.VMEM((HEADS * SHORT, KEYS_SHORT), bf16), pltpu.VMEM((HEADS * LONG, KEYS_LONG), bf16),
            pltpu.VMEM((HEADS * SHORT, KEYS_SHORT), bf16), pltpu.VMEM((HEADS * LONG, KEYS_LONG), bf16),
            pltpu.VMEM((SHORT, KEYS_SHORT), f32), pltpu.VMEM((LONG, KEYS_LONG), f32),
            pltpu.VMEM((TOK, HEADS * HD), bf16),
        ],
        compiler_params=pltpu.CompilerParams(vmem_limit_bytes=58 * 2**20),
        cost_estimate=pl.CostEstimate(flops=8 * 10**9, bytes_accessed=2 * 10**7, transcendentals=10**6),
        name="backward",
    )(*operands)


def shift_chips(array, by):
    pairs = [(i, i + by) for i in range(CHIPS) if 0 <= i + by < CHIPS]
    return lax.ppermute(array, CHIP, pairs)


def swap_cores(array):
    return lax.ppermute(array, "core", [(0, 1), (1, 0)])


def exchange(array, axes, count):
    parts = array.reshape((count, array.shape[0] // count) + array.shape[1:])
    return lax.all_to_all(parts, axes, 0, 0, tiled=True)


def spread(array, axes, count):
    copies = jnp.broadcast_to(array[None], (count,) + array.shape)
    got = lax.all_to_all(copies, axes, 0, 0, tiled=True)
    return got.reshape((count * array.shape[0],) + array.shape[1:])


def total_of(parts):
    return jnp.sum(parts.astype(f32), axis=0).astype(bf16)


def base_tables(chip, core):
    frequency = theta_base ** (-(jnp.arange(HALF, dtype=f32) * 2.0 / HD))
    positions = []
    for side in range(2):
        key_core = core if side == 0 else 1 - core
        for behind, kind, part in window_groups():
            piece = 2 * (chip - behind) + key_core
            positions.append(piece * SHORT if kind == "short" else piece * LONG + part * SHORT)
    base = jnp.stack(positions).astype(f32)[:, None] * frequency[None, :]
    rest = jnp.arange(SHORT, dtype=f32)[:, None] * frequency[None, :]
    return jnp.cos(base), jnp.sin(base), jnp.cos(rest), jnp.sin(rest)


def shards(
    tokens, lengths, w_query, w_key, w_value, w_output, w_gate, w_up, w_down, gain_attn, gain_mlp, out_grad
):
    core = lax.axis_index("core")
    chip = lax.axis_index(CHIP)
    short_first = lengths[0, 0] == SHORT_LEN
    short_at = jnp.where(short_first, 0, LONG).astype(jnp.int32)
    long_at = jnp.where(short_first, SHORT, 0).astype(jnp.int32)
    info = jnp.stack([chip, core, short_at, long_at]).astype(jnp.int32)

    def to_slots(rows):
        return jnp.where(
            short_first, rows, jnp.concatenate([rows[SHORT:], rows[:SHORT]], axis=0)
        )

    own = jnp.where(
        short_first, tokens[0], jnp.concatenate([tokens[0, LONG:], tokens[0, :LONG]], axis=0)
    )
    own_short = own[:SHORT]
    pieces = [own]
    for behind in range(1, FAR + 1):
        pieces.append(shift_chips(own if behind <= NEAR else own_short, behind))
    side_own = jnp.concatenate(pieces, axis=0)
    side_other = swap_cores(side_own)
    window = jnp.concatenate([side_own, side_other], axis=0)
    cosb, sinb, cosr, sinr = base_tables(chip, core)
    (
        q, k, v, gmix, norm, grad_resid, grad_gain_mlp,
        block_out, shared_kv, g_gate, g_up, g_down, g_proj,
    ) = run_forward(
        info, cosb, sinb, cosr, sinr, gain_attn[None], gain_mlp[None], window, out_grad[0],
        w_query, w_key, w_value, w_output, w_gate, w_up, w_down,
    )
    totals = lax.psum((g_gate, g_up, g_down, g_proj), ALL)

    packed, returned, grad_normed_q = run_backward(
        info, cosb, sinb, cosr, sinr, grad_gain_mlp, q, k, v, gmix, norm, w_query
    )
    part = total_of(exchange(packed, "core", 2))
    part = total_of(exchange(part, RING, 64))
    whole = spread(spread(part, RING, 64), "core", 2).astype(f32)
    blocks = [whole[i * D : (i + 1) * D] for i in range(12)]
    grad_query = jnp.concatenate(blocks[:8], axis=1)
    grad_key = jnp.concatenate(blocks[8:10], axis=1)
    grad_value = jnp.concatenate(blocks[10:], axis=1)
    tail = whole[12 * D :]
    total_gain_mlp = jnp.concatenate([tail[16 * i] for i in range(D // HALF)])
    total_gain_attn = (
        jnp.sum(grad_query * w_query.astype(f32), axis=1)
        + jnp.sum(grad_key * w_key.astype(f32), axis=1)
        + jnp.sum(grad_value * w_value.astype(f32), axis=1)
    ) / gain_attn

    mine = returned[:SIDE].astype(f32)
    theirs = swap_cores(returned[SIDE:])
    chip_sum = (mine + theirs.astype(f32)).astype(bf16)
    grad_kv = chip_sum[:TOK].astype(f32)
    for behind in range(1, FAR + 1):
        if behind <= NEAR:
            piece = chip_sum[behind * TOK : (behind + 1) * TOK]
            grad_kv = grad_kv + shift_chips(piece, -behind).astype(f32)
        else:
            at = (NEAR + 1) * TOK + (behind - NEAR - 1) * SHORT
            piece = shift_chips(chip_sum[at : at + SHORT], -behind).astype(f32)
            grad_kv = grad_kv + jnp.pad(piece, ((0, LONG), (0, 0)))
    grad_kv = grad_kv.astype(bf16)
    grad_normed = grad_normed_q + mm_nt(grad_kv[:, :HD], w_key) + mm_nt(grad_kv[:, HD:], w_value)
    wide = own.astype(f32)
    scale = lax.rsqrt(jnp.mean(wide * wide, axis=-1, keepdims=True) + epsilon)
    unit = wide * scale
    scaled = grad_normed * gain_attn
    input_grad = grad_resid + scale * (
        scaled - unit * jnp.mean(scaled * unit, axis=-1, keepdims=True)
    )
    return (
        block_out[None], shared_kv[None], to_slots(input_grad)[None],
        grad_query, grad_key, grad_value, totals[3].astype(f32),
        totals[0].astype(f32), totals[1].astype(f32), totals[2].astype(f32),
        total_gain_attn, total_gain_mlp,
    )


def solution(mesh):
    fine = Mesh(mesh.devices.reshape(4, 4, 2, 4), ALL)
    rows = P("dp", SEQ, None)
    return jax.shard_map(
        shards,
        mesh=fine,
        in_specs=(rows, P("dp", None)) + (P(),) * 9 + (rows,),
        out_specs=(rows, rows, rows) + (P(),) * 9,
        check_vma=False,
    )
```

```python
import jax
import jax.numpy as jnp
import numpy as np
from jax import lax
from jax.experimental import pallas as pl
from jax.experimental.pallas import tpu as pltpu
from jax.sharding import Mesh, PartitionSpec as P

WINDOW = 1024
SHORT_LEN = 2048
D = 640
HEADS = 4
HD = 256
HALF = 128
FF = 2048
TOK = 192
SHORT = 64
LONG = 128
CHIPS = 16
NEAR = 4
FAR = 8
SIDE = (NEAR + 1) * TOK + (FAR - NEAR) * SHORT
GROUPS = SIDE // SHORT
KEYS_SHORT = 2 * (FAR + 1) * SHORT
KEYS_LONG = 2 * (NEAR + 1) * LONG
KEYS = KEYS_SHORT + KEYS_LONG
FF_CHUNK = 512

epsilon = 1e-06
theta_base = 10000.0
masked_score = -1e30

SEQ = ("x", "z", "core")
CHIP = ("x", "z")
ALL = ("x", "z", "core", "dp")
HALF_FF = FF // 2
AT_GATE, AT_UP, AT_MIXED, AT_NORMED, AT_OUT, AT_BRANCH = 1024, 2048, 3072, 3584, 4224, 4864
ACTS = 5504
A_GATE, A_UP, A_DOWN, A_PROJ, A_GAIN, A_ROWS = 0, 5120, 10240, 15360, 17920, 18432
B_QUERY, B_KV, B_GAIN, B_ROWS = 0, 2560, 3840, 4096
DP = 4
A_DP = 6144
A_XZ = A_ROWS - A_DP
A_DP_PIECE, B_PIECE, A_XZ_PIECE = A_DP // DP, B_ROWS // DP, A_XZ // CHIPS
A_DP_BLOCK, B_BLOCK, A_XZ_BLOCK = A_DP_PIECE // CHIPS, B_PIECE // CHIPS, A_XZ_PIECE // DP
BLOCK = A_DP_BLOCK + B_BLOCK + A_XZ_BLOCK
XZ_FIRST = 208
JOINED = XZ_FIRST - A_DP_BLOCK - B_BLOCK
DP_FIRST = A_XZ_BLOCK - JOINED

bf16 = jnp.bfloat16
f32 = jnp.float32


def mm(left, right):
    return jnp.dot(left, right, preferred_element_type=f32)


def mm_tn(left, right):
    return lax.dot_general(left, right, (((0,), (0,)), ((), ())), preferred_element_type=f32)


def mm_nt(left, right):
    return lax.dot_general(left, right, (((1,), (1,)), ((), ())), preferred_element_type=f32)


def window_groups():
    groups = []
    for behind in range(NEAR + 1):
        groups += [(behind, "short", 0), (behind, "long", 0), (behind, "long", 1)]
    groups += [(behind, "short", 0) for behind in range(NEAR + 1, FAR + 1)]
    return groups


def key_row(side, group):
    behind, kind, part = group
    if kind == "short":
        return side * (KEYS_SHORT // 2) + behind * SHORT
    return KEYS_SHORT + side * (KEYS_LONG // 2) + behind * LONG + part * SHORT


def mask_bias(kind, chip, core):
    rows, width, first_key = (SHORT, KEYS_SHORT, 0) if kind == "short" else (LONG, KEYS_LONG, 0)
    half = width // 2
    column = lax.broadcasted_iota(jnp.int32, (1, width), 1)
    other = (column >= half).astype(jnp.int32)
    inner = column - other * half
    shift = 6 if kind == "short" else 7
    behind = lax.shift_right_logical(inner, shift)
    rest = inner & (rows - 1)
    key_core = core + other * (1 - 2 * core)
    key_position = (2 * (chip - behind) + key_core) * rows + rest
    query_position = (2 * chip + core) * rows + lax.broadcasted_iota(jnp.int32, (rows, 1), 0)
    distance = query_position - key_position
    allowed = (key_position >= 0) & (distance >= 0) & (distance < WINDOW)
    return jnp.where(allowed, 0.0, masked_score).astype(f32)


def group_tables(tables, chip, core, side, group):
    behind, kind, part = group
    piece = 2 * (chip - behind) + (core if side == 0 else 1 - core)
    at = jnp.maximum(piece if kind == "short" else 2 * piece + part, 0)
    cb, sb = tables[0, pl.ds(at, 1), :], tables[1, pl.ds(at, 1), :]
    cr, sr = tables[2], tables[3]
    return cb * cr - sb * sr, sb * cr + cb * sr


def rotary_tables():
    frequency = theta_base ** (-(np.arange(HALF) * 2.0 / HD))
    far = np.arange(SHORT)[:, None] * SHORT * frequency[None, :]
    near = np.arange(SHORT)[:, None] * frequency[None, :]
    return np.stack([np.cos(far), np.sin(far), np.cos(near), np.sin(near)]).astype(np.float32)


def place():
    return lax.axis_index("x") * 4 + lax.axis_index("z"), lax.axis_index("core")


def starts(lengths):
    short_first = (lengths[0, 0] == SHORT_LEN).astype(jnp.int32)
    return pl.multiple_of((1 - short_first) * LONG, SHORT), pl.multiple_of(short_first * SHORT, SHORT)


KINDS = (
    ("short", SHORT, 0, KEYS_SHORT, 0, 0),
    ("long", LONG, KEYS_SHORT, KEYS_LONG, HEADS * SHORT, SHORT),
)


def copies_of(pairs, sems, first=0):
    copies = [
        pltpu.make_async_copy(source, target, sems.at[first + number])
        for number, (source, target) in enumerate(pairs)
    ]
    for copy in copies:
        copy.start()
    return copies


class Stores:
    def __init__(self, sems):
        self.sems, self.copies = sems, []

    def start(self, source, target):
        self.copies += copies_of([(source, target)], self.sems, len(self.copies))

    def wait(self):
        for copy in self.copies:
            copy.wait()


def forward_kernel(
    lengths, tables, ga, gm, w0_h, w1_h, w2_h, w3_h, w4_h, w5_h, w6_h, w7_h, og_h, wq_h, wk_h, wv_h, wo_h, wg_h, wu_h, wd_h,
    ggain_o, q_h, k_h, v_h, gmix_h, norm_h, gres_h, bo_h, skv_h, keep_h, send_h,
    win, og, wq, wk, wv, wo, wg, wu, wd, norm, q, k, v, kv, scores_all, probs_all, mixed, gmix, gres,
    bo, skv, acts, bias_s, bias_l, win_sem, sems, out_sem,
):
    chip, core = place()
    short_at, long_at = starts(lengths)
    window_loads = []
    for side, (known, *rounds) in enumerate(((w0_h, w1_h, w2_h, w3_h), (w4_h, w5_h, w6_h, w7_h))):
        base = side * SIDE
        for source, first, behind in [(known, 0, 0), (known, TOK, NEAR)] + [(r, 0, n + 1) for n, r in enumerate(rounds)]:
            at = base + behind * TOK
            window_loads += [
                (source.at[pl.ds(first + short_at, SHORT)], win.at[pl.ds(at, SHORT)]),
                (source.at[pl.ds(first + long_at, LONG)], win.at[pl.ds(at + SHORT, LONG)]),
            ]
        for source, first, behind in [(known, 2 * TOK, FAR)] + [(r, TOK, NEAR + 1 + n) for n, r in enumerate(rounds)]:
            at = base + (NEAR + 1) * TOK + (behind - NEAR - 1) * SHORT
            window_loads.append((source.at[pl.ds(first, SHORT)], win.at[pl.ds(at, SHORT)]))
    window_loads = copies_of(window_loads, win_sem)
    names = ("wk", "wv", "wq", "wo", "ogs", "ogl", "wg", "wu", "wd")
    loads = dict(zip(names, copies_of((
        (wk_h, wk), (wv_h, wv), (wq_h, wq), (wo_h, wo),
        (og_h.at[pl.ds(short_at, SHORT)], og.at[pl.ds(0, SHORT)]),
        (og_h.at[pl.ds(long_at, LONG)], og.at[pl.ds(SHORT, LONG)]),
        (wg_h, wg), (wu_h, wu), (wd_h, wd),
    ), sems)))
    stores = Stores(out_sem)
    bias_s[...] = mask_bias("short", chip, core)
    bias_l[...] = mask_bias("long", chip, core)
    gain_a = ga[...].reshape(1, D)
    gain_m = gm[...].reshape(1, D)
    for copy in window_loads:
        copy.wait()

    def normalise(step, carry):
        rows = pl.ds(pl.multiple_of(step * SHORT, SHORT), SHORT)
        x = win[rows, :].astype(f32)
        scale = lax.rsqrt(jnp.mean(x * x, axis=-1, keepdims=True) + epsilon)
        norm[rows, :] = (x * scale * gain_a).astype(bf16)
        return carry

    lax.fori_loop(0, 2 * GROUPS, normalise, 0, unroll=2)
    stores.start(norm, norm_h)
    loads["wk"].wait()
    loads["wv"].wait()
    for side in range(2):
        normed = norm[side * SIDE : (side + 1) * SIDE, :]
        kv[:, :HD] = mm(normed, wk[...])
        kv[:, HD:] = mm(normed, wv[...])
        for number, group in enumerate(window_groups()):
            rows = slice(number * SHORT, (number + 1) * SHORT)
            cos, sin = group_tables(tables, chip, core, side, group)
            low_half, high_half = kv[rows, :HALF], kv[rows, HALF:HD]
            at = key_row(side, group)
            k[at : at + SHORT, :HALF] = (low_half * cos - high_half * sin).astype(bf16)
            k[at : at + SHORT, HALF:] = (high_half * cos + low_half * sin).astype(bf16)
            v[at : at + SHORT, :] = kv[rows, HD:].astype(bf16)
            if side == 0 and number < 3:
                skv[rows, :HD] = k[at : at + SHORT, :]
                skv[rows, HD:] = v[at : at + SHORT, :]
    stores.start(k, k_h)
    stores.start(v, v_h)
    stores.start(skv.at[pl.ds(0, SHORT)], skv_h.at[pl.ds(short_at, SHORT)])
    stores.start(skv.at[pl.ds(SHORT, LONG)], skv_h.at[pl.ds(long_at, LONG)])

    loads["wq"].wait()
    query_raw = mm(norm[:TOK, :], wq[...])
    for number in range(3):
        rows = slice(number * SHORT, (number + 1) * SHORT)
        cos, sin = group_tables(tables, chip, core, 0, window_groups()[number])
        for head in range(HEADS):
            low_half = query_raw[rows, head * HD : head * HD + HALF]
            high_half = query_raw[rows, head * HD + HALF : (head + 1) * HD]
            at = head * SHORT if number == 0 else HEADS * SHORT + head * LONG + (number - 1) * SHORT
            q[at : at + SHORT, :HALF] = (low_half * cos - high_half * sin).astype(bf16) * bf16(HD**-0.5)
            q[at : at + SHORT, HALF:] = (high_half * cos + low_half * sin).astype(bf16) * bf16(HD**-0.5)
    stores.start(q, q_h)

    for kind, rows, key_at, width, query_at, row_at in KINDS:
        bias = bias_s if kind == "short" else bias_l
        count = HEADS * rows
        scores_all[:count, :width] = mm_nt(q[query_at : query_at + count, :], k[key_at : key_at + width, :])
        for head in range(HEADS):
            here = slice(head * rows, (head + 1) * rows)
            scores = scores_all[here, :width] + bias[...]
            exponent = jnp.exp(scores - jnp.max(scores, axis=-1, keepdims=True))
            share = 1.0 / jnp.sum(exponent, axis=-1, keepdims=True)
            probs_all[here, :width] = (exponent * share).astype(bf16)
        mixed_all = mm(probs_all[:count, :width], v[key_at : key_at + width, :]).astype(bf16)
        for head in range(HEADS):
            mixed[row_at : row_at + rows, head * HD : (head + 1) * HD] = mixed_all[
                head * rows : (head + 1) * rows, :
            ]

    loads["wo"].wait()
    resid = win[:TOK, :].astype(f32) + mm(mixed[...], wo[...])
    scale = lax.rsqrt(jnp.mean(resid * resid, axis=-1, keepdims=True) + epsilon)
    unit = resid * scale
    normed_mlp = (unit * gain_m).astype(bf16)
    for name in ("ogs", "ogl", "wg", "wu", "wd"):
        loads[name].wait()
    grad_out = og[...]
    for half in range(2):
        acts[half, :, AT_MIXED:AT_NORMED] = mixed[:, half * 2 * HD : (half + 1) * 2 * HD]
        acts[half, :, AT_NORMED:AT_OUT] = normed_mlp
        acts[half, :, AT_OUT:AT_BRANCH] = grad_out
    block_out = resid
    grad_normed = jnp.zeros((TOK, D), f32)
    for chunk in range(FF // FF_CHUNK):
        cols = slice(chunk * FF_CHUNK, (chunk + 1) * FF_CHUNK)
        gate = mm(normed_mlp, wg[:, cols])
        up = mm(normed_mlp, wu[:, cols])
        sig = jax.nn.sigmoid(gate)
        silu = gate * sig
        act = (silu * up).astype(bf16)
        grad_act = mm_nt(grad_out, wd[cols, :])
        grad_gate = (grad_act * up * sig * (1.0 + gate * (1.0 - sig))).astype(bf16)
        grad_up = (grad_act * silu).astype(bf16)
        block_out = block_out + mm(act, wd[cols, :])
        grad_normed = grad_normed + mm_nt(grad_gate, wg[:, cols]) + mm_nt(grad_up, wu[:, cols])
        half, at = chunk // 2, (chunk % 2) * FF_CHUNK
        acts[half, :, at : at + FF_CHUNK] = act
        acts[half, :, AT_GATE + at : AT_GATE + at + FF_CHUNK] = grad_gate
        acts[half, :, AT_UP + at : AT_UP + at + FF_CHUNK] = grad_up
    stores.start(acts.at[1 - core, :, pl.ds(0, AT_BRANCH)], send_h.at[:, pl.ds(0, AT_BRANCH)])
    stores.start(acts.at[core, :, pl.ds(0, AT_BRANCH)], keep_h.at[:, pl.ds(0, AT_BRANCH)])
    ggain_o[...] = jnp.sum(grad_normed * unit, axis=0, keepdims=True)
    scaled = grad_normed * gain_m
    grad_resid = grad_out.astype(f32) + scale * (
        scaled - unit * jnp.mean(scaled * unit, axis=-1, keepdims=True)
    )
    grad_branch = grad_resid.astype(bf16)
    for half in range(2):
        acts[half, :, AT_BRANCH:] = grad_branch
    rest = pl.ds(AT_BRANCH, ACTS - AT_BRANCH)
    stores.start(acts.at[1 - core, :, rest], send_h.at[:, rest])
    stores.start(acts.at[core, :, rest], keep_h.at[:, rest])
    gres[...] = grad_resid
    stores.start(gres, gres_h)
    bo[...] = block_out.astype(bf16)
    stores.start(bo.at[pl.ds(0, SHORT)], bo_h.at[pl.ds(short_at, SHORT)])
    stores.start(bo.at[pl.ds(SHORT, LONG)], bo_h.at[pl.ds(long_at, LONG)])
    grad_mixed = mm_nt(grad_branch, wo[...]).astype(bf16)
    for head in range(HEADS):
        cols = slice(head * HD, (head + 1) * HD)
        gmix[head * SHORT : (head + 1) * SHORT, :] = grad_mixed[:SHORT, cols]
        at = HEADS * SHORT + head * LONG
        gmix[at : at + LONG, :] = grad_mixed[SHORT:, cols]
    stores.start(gmix, gmix_h)
    stores.wait()


def backward_kernel(
    tables, ga, q_h, k_h, v_h, gmix_h, norm_h, wq_h, wk_h, wv_h,
    gain_o, mine_h, other_h, gq_h, gnq_h,
    q, k, v, gmix, norm, wq, wk, wv, scores_all, gp_all, probs_all, gs_all, ret, gq, gnq, bias_s, bias_l,
    sems, out_sem,
):
    chip, core = place()
    loads = copies_of((
        (q_h, q), (k_h, k), (gmix_h, gmix), (v_h, v), (norm_h, norm), (wq_h, wq), (wk_h, wk), (wv_h, wv),
    ), sems)
    stores = Stores(out_sem)
    bias_s[...] = mask_bias("short", chip, core)
    bias_l[...] = mask_bias("long", chip, core)
    for copy in loads[:4]:
        copy.wait()
    for kind, rows, key_at, width, query_at, row_at in KINDS:
        bias = bias_s if kind == "short" else bias_l
        keys = k[key_at : key_at + width, :]
        count = HEADS * rows
        stack = slice(query_at, query_at + count)
        scores_all[:count, :width] = mm_nt(q[stack, :], keys)
        gp_all[:count, :width] = mm_nt(gmix[stack, :], v[key_at : key_at + width, :])
        for head in range(HEADS):
            here = slice(head * rows, (head + 1) * rows)
            scores = scores_all[here, :width] + bias[...]
            exponent = jnp.exp(scores - jnp.max(scores, axis=-1, keepdims=True))
            probs = exponent * (1.0 / jnp.sum(exponent, axis=-1, keepdims=True))
            probs_all[here, :width] = probs.astype(bf16)
            grad_probs = gp_all[here, :width]
            inner = jnp.sum(probs * grad_probs, axis=-1, keepdims=True)
            gs_all[here, :width] = (probs * (grad_probs - inner)).astype(bf16)
        grad_queries = mm(gs_all[:count, :width], keys) * (HD**-0.5)
        for head in range(HEADS):
            for part in range(rows // SHORT):
                number = 0 if kind == "short" else 1 + part
                cos, sin = group_tables(tables, chip, core, 0, window_groups()[number])
                at = head * rows + part * SHORT
                low_half = grad_queries[at : at + SHORT, :HALF]
                high_half = grad_queries[at : at + SHORT, HALF:]
                to = slice(row_at + part * SHORT, row_at + (part + 1) * SHORT)
                gq[to, head * HD : head * HD + HALF] = (low_half * cos + high_half * sin).astype(bf16)
                gq[to, head * HD + HALF : (head + 1) * HD] = (high_half * cos - low_half * sin).astype(bf16)
        grad_keys = mm_tn(gs_all[:count, :width], q[stack, :])
        grad_values = mm_tn(probs_all[:count, :width], gmix[stack, :])
        for side in range(2):
            for number, group in enumerate(window_groups()):
                if group[1] != kind:
                    continue
                at = key_row(side, group) - key_at
                cos, sin = group_tables(tables, chip, core, side, group)
                low_half = grad_keys[at : at + SHORT, :HALF]
                high_half = grad_keys[at : at + SHORT, HALF:]
                to = slice(number * SHORT, (number + 1) * SHORT)
                ret[side, to, :HALF] = (low_half * cos + high_half * sin).astype(bf16)
                ret[side, to, HALF:HD] = (high_half * cos - low_half * sin).astype(bf16)
                ret[side, to, HD:] = grad_values[at : at + SHORT, :].astype(bf16)
    stores.start(ret.at[0], mine_h)
    stores.start(ret.at[1], other_h)
    stores.start(gq, gq_h)
    for copy in loads[4:]:
        copy.wait()
    gnq[...] = mm_nt(gq[...], wq[...])
    stores.start(gnq, gnq_h)
    grad_gain = jnp.sum(gnq[...] * norm[:TOK, :].astype(f32), axis=0, keepdims=True)
    for step in range(8):
        side, first = step // 4, step % 4 * (SIDE // 4)
        rows = slice(first, first + SIDE // 4)
        grad_normed = mm_nt(ret[side, rows, :HD], wk[...]) + mm_nt(ret[side, rows, HD:], wv[...])
        here = norm[side * SIDE + first : side * SIDE + first + SIDE // 4, :].astype(f32)
        grad_gain = grad_gain + jnp.sum(grad_normed * here, axis=0, keepdims=True)
    gain_o[...] = grad_gain / ga[...].reshape(1, D)
    stores.wait()


def project_kernel(gain, norm_h, mine_h, other_h, gq_h, keep_h, send_h, norm, ret, gq, b, sems, out_sem):
    core = lax.axis_index("core")
    loads = copies_of((
        (norm_h.at[pl.ds(0, SIDE)], norm.at[0]), (gq_h, gq), (mine_h, ret.at[0]),
        (norm_h.at[pl.ds(SIDE, SIDE)], norm.at[1]), (other_h, ret.at[1]),
    ), sems)
    stores = Stores(out_sem)

    def put(half, at, block):
        for part in range(block.shape[1] // HALF):
            row = at + part * D
            b[half, row : row + D, :] = block[:, part * HALF : (part + 1) * HALF].astype(bf16)

    b[0, B_GAIN:, :] = jnp.zeros((B_ROWS - B_GAIN, HALF), bf16)
    b[1, B_GAIN:, :] = jnp.zeros((B_ROWS - B_GAIN, HALF), bf16)
    for part in range(D // HALF):
        b[0, B_GAIN + 16 * part : B_GAIN + 16 * part + 16, :] = jnp.broadcast_to(
            gain[:, part * HALF : (part + 1) * HALF], (16, HALF)
        ).astype(bf16)
    for copy in loads[:2]:
        copy.wait()
    for half in range(2):
        put(half, B_QUERY, mm_tn(norm[0, :TOK, :], gq[:, half * 2 * HD : (half + 1) * 2 * HD]))
    for copy in loads[2:]:
        copy.wait()
    both = mm_tn(norm[0], ret[0]) + mm_tn(norm[1], ret[1])
    for half in range(2):
        put(half, B_KV, both[:, half * HD : (half + 1) * HD])
    stores.start(b.at[1 - core], send_h)
    stores.start(b.at[core], keep_h)
    stores.wait()


def pieces_out(stores, pieces, outs):
    me = lax.axis_index("dp")
    for step, out in enumerate(outs):
        stores.start(pieces.at[lax.rem(me + step, DP)], out)


def halves_kernel(ggain, keep_h, recv_h, p0_h, p1_h, p2_h, p3_h, xz_h, x, pieces, xz, sems, out_sem):
    copies = copies_of(((keep_h, x.at[pl.ds(0, TOK)]), (recv_h, x.at[pl.ds(TOK, TOK)])), sems)
    stores = Stores(out_sem)
    for copy in copies:
        copy.wait()

    def write(at, values):
        done, rows = 0, values.shape[0]
        while done < rows:
            row = at + done
            if row < A_DP:
                piece, inner = row // A_DP_PIECE, row % A_DP_PIECE
                size = min(rows - done, A_DP_PIECE - inner)
                pieces[piece, inner : inner + size, :] = values[done : done + size, :]
            else:
                piece, inner = (row - A_DP) // A_XZ_PIECE, (row - A_DP) % A_XZ_PIECE
                size = min(rows - done, A_XZ_PIECE - inner)
                xz[piece, inner : inner + size, :] = values[done : done + size, :]
            done += size

    def put(at, block):
        rows = block.shape[0]
        for part in range(block.shape[1] // HALF):
            write(at + part * rows, block[:, part * HALF : (part + 1) * HALF].astype(bf16))

    normed = x[:, AT_NORMED:AT_OUT]
    for chunk in range(2):
        cols = slice(AT_GATE + chunk * FF_CHUNK, AT_GATE + (chunk + 1) * FF_CHUNK)
        put(A_GATE + chunk * 4 * D, mm_tn(normed, x[:, cols]))
    for chunk in range(2):
        cols = slice(AT_UP + chunk * FF_CHUNK, AT_UP + (chunk + 1) * FF_CHUNK)
        put(A_UP + chunk * 4 * D, mm_tn(normed, x[:, cols]))
        if chunk == 0:
            pieces_out(stores, pieces, (p0_h, p1_h, p2_h, p3_h))
    put(A_DOWN, mm_tn(x[:, :AT_GATE], x[:, AT_OUT:AT_BRANCH]))
    put(A_PROJ, mm_tn(x[:, AT_MIXED:AT_NORMED], x[:, AT_BRANCH:]))
    for part in range(D // HALF):
        write(A_GAIN + 16 * part, jnp.broadcast_to(
            ggain[:, part * HALF : (part + 1) * HALF], (16, HALF)
        ).astype(bf16))
    end = A_GAIN + 16 * (D // HALF)
    write(end, jnp.zeros((A_ROWS - end, HALF), bf16))
    stores.start(xz, xz_h)
    stores.wait()


def chip_sum_kernel(keep, recv, p0_h, p1_h, p2_h, p3_h, pieces, out_sem):
    stores = Stores(out_sem)
    for piece in range(DP):
        rows = slice(piece * B_PIECE, (piece + 1) * B_PIECE)
        pieces[piece] = (keep[rows, :].astype(f32) + recv[rows, :].astype(f32)).astype(bf16)
    pieces_out(stores, pieces, (p0_h, p1_h, p2_h, p3_h))
    stores.wait()


def first_sum_kernel(
    a0, a1, a2, a3, b0, b1, b2, b3, xz, out_xz, p0_h, p1_h, p2_h, p3_h, pieces, out_sem
):
    stores = Stores(out_sem)
    for piece in range(DP):
        rows = slice(piece * A_XZ_BLOCK, (piece + 1) * A_XZ_BLOCK)
        total = xz[0, rows, :].astype(f32)
        for chip in range(1, CHIPS):
            total = total + xz[chip, rows, :].astype(f32)
        pieces[piece] = total.astype(bf16)
    pieces_out(stores, pieces, (p0_h, p1_h, p2_h, p3_h))
    for chip in range(CHIPS):
        for at, size, parts in ((0, A_DP_BLOCK, (a0, a1, a2, a3)), (A_DP_BLOCK, B_BLOCK, (b0, b1, b2, b3))):
            rows = slice(chip * size, (chip + 1) * size)
            total = (parts[0][rows, :].astype(f32) + parts[1][rows, :].astype(f32)) + (
                parts[2][rows, :].astype(f32) + parts[3][rows, :].astype(f32)
            )
            out_xz[chip, at : at + size, :] = total.astype(bf16)
    stores.wait()


def second_sum_kernel(xz, c0, c1, c2, c3, copies_h, own, total, out_sem):
    stores = Stores(out_sem)
    rest = (
        (c0[...].astype(f32) + c1[...].astype(f32)) + (c2[...].astype(f32) + c3[...].astype(f32))
    ).astype(bf16)
    own[...] = rest[JOINED:, :]
    value = xz[0].astype(f32)
    for chip in range(1, CHIPS):
        value = value + xz[chip].astype(f32)
    total[: XZ_FIRST - JOINED, :] = value.astype(bf16)
    total[XZ_FIRST - JOINED :, :] = rest[:JOINED, :]
    for chip in range(CHIPS):
        stores.start(total, copies_h.at[chip])
    stores.wait()


def spread_kernel(d0, d1, d2, d3, copies_h, rows, out_sem):
    stores = Stores(out_sem)
    me = lax.axis_index("dp")
    for step, part in enumerate((d0, d1, d2, d3)):
        rows[lax.rem(me + DP - step, DP)] = part[...]
    for chip in range(CHIPS):
        stores.start(rows, copies_h.at[chip])
    stores.wait()


def unpack_kernel(
    e0_h, e1_h, e2_h, e3_h, f_h, o0_h, o1_h, o2_h, o3_h, p_h,
    gain_a_o, gain_m_o, gate_h, up_h, down_h, proj_h, query_h, key_h, value_h,
    a_dp, a_xz, b, gate, up, down, proj, query, key, value, sems, out_sem,
):
    mine, me = lax.axis_index("core"), lax.axis_index("dp")
    sides = ((mine, (e0_h, e1_h, e2_h, e3_h), f_h), (1 - mine, (o0_h, o1_h, o2_h, o3_h), p_h))
    firsts, seconds, thirds = [], [], []
    for side, parts, xz_h in sides:
        for step, part in enumerate(parts):
            dp = lax.rem(me + DP - step, DP)
            firsts.append((part.at[:, pl.ds(0, A_DP_BLOCK)], a_dp.at[side, dp]))
            seconds.append((part.at[:, pl.ds(A_DP_BLOCK, B_BLOCK)], b.at[side, dp]))
            thirds.append((part.at[:, pl.ds(XZ_FIRST - JOINED, JOINED)], a_xz.at[side, :, dp, pl.ds(0, JOINED)]))
        thirds.append((xz_h, a_xz.at[side, :, :, pl.ds(JOINED, DP_FIRST)]))
    loads = copies_of(firsts + seconds + thirds, sems)
    stores = Stores(out_sem)

    def pieces_of(core, at, rows, in_b):
        done = 0
        while done < rows:
            row = at + done
            if in_b:
                source, size = b, B_BLOCK
                index = (core, row // B_PIECE, row % B_PIECE // B_BLOCK)
            elif row < A_DP:
                source, size = a_dp, A_DP_BLOCK
                index = (core, row // A_DP_PIECE, row % A_DP_PIECE // A_DP_BLOCK)
            else:
                row = row - A_DP
                source, size = a_xz, A_XZ_BLOCK
                index = (core, row // A_XZ_PIECE, row % A_XZ_PIECE // A_XZ_BLOCK)
            inner = row % size
            size = min(rows - done, size - inner)
            yield done, size, source[index + (slice(inner, inner + size), slice(None))].astype(f32)
            done += size

    def unpack(target, at, rows, in_b, place_of, count, cores=(0, 1)):
        for core in cores:
            for part in range(count):
                row, col = place_of(core, part)
                for done, size, values in pieces_of(core, at + part * rows, rows, in_b):
                    target[row + done : row + done + size, col : col + HALF] = values

    for copy in loads[: 2 * DP]:
        copy.wait()
    unpack(gate, A_GATE, D, False, lambda core, part: (0, core * HALF_FF + part * HALF), HALF_FF // HALF)
    stores.start(gate, gate_h)
    for copy in loads[2 * DP : 4 * DP]:
        copy.wait()
    unpack(query, B_QUERY, D, True, lambda core, part: (0, core * 2 * HD + part * HALF), 4)
    stores.start(query, query_h)
    unpack(key, B_KV, D, True, lambda core, part: (0, part * HALF), 2, (0,))
    stores.start(key, key_h)
    unpack(value, B_KV, D, True, lambda core, part: (0, part * HALF), 2, (1,))
    stores.start(value, value_h)
    for copy in loads[4 * DP :]:
        copy.wait()
    unpack(up, A_UP, D, False, lambda core, part: (0, core * HALF_FF + part * HALF), HALF_FF // HALF)
    stores.start(up, up_h)
    unpack(down, A_DOWN, HALF_FF, False, lambda core, part: (core * HALF_FF, part * HALF), D // HALF)
    stores.start(down, down_h)
    unpack(proj, A_PROJ, 2 * HD, False, lambda core, part: (core * 2 * HD, part * HALF), D // HALF)
    stores.start(proj, proj_h)
    for out, at, in_b in ((gain_a_o, B_GAIN, True), (gain_m_o, A_GAIN, False)):
        for part in range(D // HALF):
            (_, _, first), = pieces_of(0, at + 16 * part, 1, in_b)
            (_, _, second), = pieces_of(1, at + 16 * part, 1, in_b)
            out[part * HALF : (part + 1) * HALF] = (first + second).reshape(HALF)
    stores.wait()


VMEM = pl.BlockSpec(memory_space=pltpu.VMEM)
SMEM = pl.BlockSpec(memory_space=pltpu.SMEM)
ANY = pl.BlockSpec(memory_space=pl.ANY)


def shape(dims, kind=bf16):
    return jax.ShapeDtypeStruct(dims, kind)


def limit(mib):
    return pltpu.CompilerParams(vmem_limit_bytes=mib * 2**20)


def cost(flops, moved):
    return pl.CostEstimate(flops=flops, bytes_accessed=moved, transcendentals=0)


def scratch(*dims, kind=bf16):
    return pltpu.VMEM(dims, kind)


def semaphores(count):
    return pltpu.SemaphoreType.DMA((count,))


def run_forward(*operands):
    return pl.pallas_call(
        forward_kernel,
        in_specs=[SMEM] + [VMEM] * 3 + [ANY] * 16,
        out_specs=[VMEM] + [ANY] * 10,
        out_shape=[
            shape((1, D), f32),
            shape((HEADS * TOK, HD)), shape((KEYS, HD)), shape((KEYS, HD)), shape((HEADS * TOK, HD)),
            shape((2 * SIDE, D)), shape((TOK, D), f32),
            shape((TOK, D)), shape((TOK, 2 * HD)), shape((TOK, ACTS)), shape((TOK, ACTS)),
        ],
        scratch_shapes=[
            scratch(2 * SIDE, D), scratch(TOK, D), scratch(D, HEADS * HD), scratch(D, HD), scratch(D, HD),
            scratch(HEADS * HD, D), scratch(D, FF), scratch(D, FF), scratch(FF, D),
            scratch(2 * SIDE, D), scratch(HEADS * TOK, HD), scratch(KEYS, HD), scratch(KEYS, HD),
            scratch(SIDE, 2 * HD, kind=f32), scratch(HEADS * LONG, KEYS_LONG, kind=f32),
            scratch(HEADS * LONG, KEYS_LONG), scratch(TOK, HEADS * HD), scratch(HEADS * TOK, HD),
            scratch(TOK, D, kind=f32), scratch(TOK, D), scratch(TOK, 2 * HD), scratch(2, TOK, ACTS),
            scratch(SHORT, KEYS_SHORT, kind=f32), scratch(LONG, KEYS_LONG, kind=f32),
            semaphores(28), semaphores(9), semaphores(14),
        ],
        compiler_params=limit(58),
        cost_estimate=cost(8 * 10**9, 3 * 10**7),
        name="forward",
    )(*operands)


def run_backward(*operands):
    return pl.pallas_call(
        backward_kernel,
        in_specs=[VMEM] * 2 + [ANY] * 8,
        out_specs=[VMEM] + [ANY] * 4,
        out_shape=[
            shape((1, D), f32), shape((SIDE, 2 * HD)), shape((SIDE, 2 * HD)), shape((TOK, HEADS * HD)),
            shape((TOK, D), f32),
        ],
        scratch_shapes=[
            scratch(HEADS * TOK, HD), scratch(KEYS, HD), scratch(KEYS, HD), scratch(HEADS * TOK, HD),
            scratch(2 * SIDE, D), scratch(D, HEADS * HD), scratch(D, HD), scratch(D, HD),
            scratch(HEADS * LONG, KEYS_LONG, kind=f32), scratch(HEADS * LONG, KEYS_LONG, kind=f32),
            scratch(HEADS * LONG, KEYS_LONG), scratch(HEADS * LONG, KEYS_LONG),
            scratch(2, SIDE, 2 * HD), scratch(TOK, HEADS * HD), scratch(TOK, D, kind=f32),
            scratch(SHORT, KEYS_SHORT, kind=f32), scratch(LONG, KEYS_LONG, kind=f32),
            semaphores(8), semaphores(4),
        ],
        compiler_params=limit(54),
        cost_estimate=cost(10**12, 10**9),
        name="backward",
    )(*operands)


def run_project(*operands):
    return pl.pallas_call(
        project_kernel,
        in_specs=[VMEM] + [ANY] * 4,
        out_specs=[ANY] * 2,
        out_shape=[shape((B_ROWS, HALF)), shape((B_ROWS, HALF))],
        scratch_shapes=[
            scratch(2, SIDE, D), scratch(2, SIDE, 2 * HD), scratch(TOK, HEADS * HD),
            scratch(2, B_ROWS, HALF), semaphores(5), semaphores(2),
        ],
        compiler_params=limit(54),
        cost_estimate=cost(10**12, 10**9),
        name="project",
    )(*operands)


def run_halves(*operands):
    return pl.pallas_call(
        halves_kernel,
        in_specs=[VMEM, ANY, ANY],
        out_specs=[ANY] * 5,
        out_shape=[shape((A_DP_PIECE, HALF))] * 4 + [shape((CHIPS, A_XZ_PIECE, HALF))],
        scratch_shapes=[
            scratch(2 * TOK, ACTS), scratch(DP, A_DP_PIECE, HALF), scratch(CHIPS, A_XZ_PIECE, HALF),
            semaphores(2), semaphores(5),
        ],
        compiler_params=limit(20),
        cost_estimate=cost(2 * 10**9, 10**7),
        name="halves",
    )(*operands)


def run_chip_sum(*operands):
    return pl.pallas_call(
        chip_sum_kernel,
        in_specs=[VMEM] * 2,
        out_specs=[ANY] * 4,
        out_shape=[shape((B_PIECE, HALF))] * 4,
        scratch_shapes=[scratch(DP, B_PIECE, HALF), semaphores(4)],
        compiler_params=limit(8),
        cost_estimate=cost(10**6, 4 * 10**6),
        name="chip_sum",
    )(*operands)


def run_first_sum(*operands):
    return pl.pallas_call(
        first_sum_kernel,
        in_specs=[VMEM] * 9,
        out_specs=[VMEM] + [ANY] * 4,
        out_shape=[shape((CHIPS, A_DP_BLOCK + B_BLOCK, HALF))] + [shape((A_XZ_BLOCK, HALF))] * 4,
        scratch_shapes=[scratch(DP, A_XZ_BLOCK, HALF), semaphores(4)],
        compiler_params=limit(12),
        cost_estimate=cost(10**6, 8 * 10**6),
        name="first_sum",
    )(*operands)


def run_second_sum(*operands):
    return pl.pallas_call(
        second_sum_kernel,
        in_specs=[VMEM] * 5,
        out_specs=[ANY, VMEM],
        out_shape=[shape((CHIPS, XZ_FIRST, HALF)), shape((DP_FIRST, HALF))],
        scratch_shapes=[scratch(XZ_FIRST, HALF), semaphores(CHIPS)],
        compiler_params=limit(4),
        cost_estimate=cost(10**6, 10**6),
        name="second_sum",
    )(*operands)


def run_spread(*operands):
    return pl.pallas_call(
        spread_kernel,
        in_specs=[VMEM] * 4,
        out_specs=ANY,
        out_shape=shape((CHIPS, DP, DP_FIRST, HALF)),
        scratch_shapes=[scratch(DP, DP_FIRST, HALF), semaphores(CHIPS)],
        compiler_params=limit(4),
        cost_estimate=cost(0, 10**6),
        name="spread",
    )(*operands)


def run_unpack(*operands):
    return pl.pallas_call(
        unpack_kernel,
        in_specs=[ANY] * 10,
        out_specs=[VMEM] * 2 + [ANY] * 7,
        out_shape=[
            shape((D,), f32), shape((D,), f32), shape((D, FF), f32), shape((D, FF), f32),
            shape((FF, D), f32), shape((HEADS * HD, D), f32), shape((D, HEADS * HD), f32),
            shape((D, HD), f32), shape((D, HD), f32),
        ],
        scratch_shapes=[
            scratch(2, DP, CHIPS, A_DP_BLOCK, HALF), scratch(2, CHIPS, DP, A_XZ_BLOCK, HALF),
            scratch(2, DP, CHIPS, B_BLOCK, HALF),
            scratch(D, FF, kind=f32), scratch(D, FF, kind=f32), scratch(FF, D, kind=f32),
            scratch(HEADS * HD, D, kind=f32), scratch(D, HEADS * HD, kind=f32), scratch(D, HD, kind=f32),
            scratch(D, HD, kind=f32), semaphores(26), semaphores(7),
        ],
        compiler_params=limit(40),
        cost_estimate=cost(0, 3 * 10**7),
        name="unpack",
    )(*operands)


def swap_cores(array):
    return lax.ppermute(array, "core", [(0, 1), (1, 0)])


def gather_dp(pieces):
    got = [pieces[0]]
    for step in range(1, DP):
        got.append(lax.ppermute(pieces[step], "dp", [(i, (i + step) % DP) for i in range(DP)]))
    return got


def shards(
    tokens, lengths, w_query, w_key, w_value, w_output, w_gate, w_up, w_down, gain_attn, gain_mlp, out_grad
):
    short_first = lengths[0, 0] == SHORT_LEN

    def to_slots(rows):
        return jnp.where(
            short_first, rows, jnp.concatenate([rows[SHORT:], rows[:SHORT]], axis=0)
        )

    slots = tokens[0]
    short_at = jnp.where(short_first, 0, LONG)

    def short_of(rows):
        return lax.dynamic_slice_in_dim(rows, short_at, SHORT, 0)

    own_short = short_of(slots)
    back = lax.ppermute(slots, "x", [(i, i + 1) for i in range(3)])
    back_short = lax.ppermute(own_short, "x", [(i, i + 2) for i in range(2)])
    here = jnp.concatenate([slots, short_of(back)], axis=0)
    there = jnp.concatenate([back, back_short], axis=0)
    ahead = lax.axis_index("z")
    rounds = [
        lax.ppermute(
            jnp.where(ahead + step < 4, here, there), "z", [(i, (i + step) % 4) for i in range(4)]
        )
        for step in range(1, 4)
    ]
    known = jnp.concatenate([slots, there], axis=0)
    window = [known, *rounds, *[swap_cores(part) for part in (known, *rounds)]]
    tables = jnp.asarray(rotary_tables())
    (
        grad_gain_mlp, q, k, v, gmix, norm, grad_resid, block_out, shared_kv, kept, sent,
    ) = run_forward(
        lengths, tables, gain_attn, gain_mlp, *window, out_grad[0],
        w_query, w_key, w_value, w_output, w_gate, w_up, w_down,
    )
    *a_pieces, a_xz = run_halves(grad_gain_mlp, kept, swap_cores(sent))
    q, a_xz = lax.optimization_barrier((q, a_xz))
    a_xz = lax.all_to_all(a_xz, CHIP, 0, 0, tiled=True)
    a_got = gather_dp(a_pieces)
    gain_part, mine, other, gq, grad_normed_q = run_backward(
        tables, gain_attn, q, k, v, gmix, norm, w_query, w_key, w_value
    )
    gq, *a_got = lax.optimization_barrier((gq, *a_got))
    b_kept, b_sent = run_project(gain_part, norm, mine, other, gq)
    b_got = gather_dp(run_chip_sum(b_kept, swap_cores(b_sent)))

    chip_sum = (mine.astype(f32) + swap_cores(other).astype(f32)).astype(bf16)
    def near(behind):
        return chip_sum[behind * TOK : (behind + 1) * TOK]

    def far(behind):
        at = (NEAR + 1) * TOK + (behind - NEAR - 1) * SHORT
        return chip_sum[at : at + SHORT]

    def padded(short):
        return jnp.pad(short, ((0, LONG), (0, 0)))

    grad_kv = near(0).astype(f32)
    for_back = near(NEAR).astype(f32)
    for_far_back = far(FAR).astype(f32)
    for step in range(1, 4):
        sent_back = jnp.concatenate([near(step), far(NEAR + step)], axis=0)
        came = lax.ppermute(sent_back, "z", [(i, (i - step) % 4) for i in range(4)]).astype(f32)
        same = ahead + step < 4
        came_near, came_far = came[:TOK], came[TOK:]
        grad_kv = grad_kv + jnp.where(same, came_near, 0.0)
        for_back = for_back + jnp.where(same, padded(came_far), came_near)
        for_far_back = for_far_back + jnp.where(same, 0.0, came_far)
    for_back, for_far_back = for_back.astype(bf16), for_far_back.astype(bf16)
    first, *c_pieces = run_first_sum(*a_got, *b_got, a_xz)
    c_got = gather_dp(c_pieces)
    first = lax.all_to_all(first, CHIP, 0, 0, tiled=True)
    copies, own_xz = run_second_sum(first, *c_got)
    copies, grad_kv, for_back, for_far_back = lax.optimization_barrier((copies, grad_kv, for_back, for_far_back))
    from_back = lax.ppermute(for_back, "x", [(i + 1, i) for i in range(3)])
    from_far_back = lax.ppermute(for_far_back, "x", [(i + 2, i) for i in range(2)])

    dp_part = lax.all_to_all(copies, CHIP, 0, 0, tiled=True)
    xz_copies = run_spread(*gather_dp([own_xz] * DP))
    dp_part, xz_copies, from_back, from_far_back = lax.optimization_barrier(
        (dp_part, xz_copies, from_back, from_far_back)
    )
    dp_parts = gather_dp([dp_part] * DP)
    xz_parts = lax.all_to_all(xz_copies, CHIP, 0, 0, tiled=True)
    parts = [*dp_parts, xz_parts]
    parts = list(lax.optimization_barrier(tuple(parts)))
    (
        total_gain_attn, total_gain_mlp, grad_gate, grad_up, grad_down, grad_proj, grad_query, grad_key, grad_value,
    ) = run_unpack(*parts, *[swap_cores(part) for part in parts])

    grad_kv = grad_kv + from_back.astype(f32) + padded(from_far_back.astype(f32))
    grad_kv = grad_kv.astype(bf16)
    grad_normed = grad_normed_q + mm_nt(grad_kv[:, :HD], w_key) + mm_nt(grad_kv[:, HD:], w_value)
    own = jnp.where(short_first, slots, jnp.concatenate([slots[LONG:], slots[:LONG]], axis=0))
    wide = own.astype(f32)
    scale = lax.rsqrt(jnp.mean(wide * wide, axis=-1, keepdims=True) + epsilon)
    unit = wide * scale
    scaled = grad_normed * gain_attn
    input_grad = to_slots(
        grad_resid + scale * (scaled - unit * jnp.mean(scaled * unit, axis=-1, keepdims=True))
    )

    return (
        block_out[None], shared_kv[None], input_grad[None],
        grad_query, grad_key, grad_value, grad_proj, grad_gate, grad_up, grad_down,
        total_gain_attn, total_gain_mlp,
    )


def solution(mesh):
    fine = Mesh(mesh.devices.reshape(4, 4, 2, 4), ALL)
    rows = P("dp", SEQ, None)
    return jax.shard_map(
        shards,
        mesh=fine,
        in_specs=(rows, P("dp", None)) + (P(),) * 9 + (rows,),
        out_specs=(rows, rows, rows) + (P(),) * 9,
        check_vma=False,
    )
```

```python
import jax
import jax.numpy as jnp
import numpy as np
from jax import lax
from jax.experimental import pallas as pl
from jax.experimental.pallas import tpu as pltpu
from jax.sharding import Mesh, PartitionSpec as P

WINDOW = 1024
SHORT_LEN = 2048
D = 640
HEADS = 4
HD = 256
HALF = 128
FF = 2048
TOK = 192
SHORT = 64
LONG = 128
CHIPS = 16
NEAR = 4
FAR = 8
SIDE = (NEAR + 1) * TOK + (FAR - NEAR) * SHORT
GROUPS = SIDE // SHORT
WINDOW_PARTS = ((0, NEAR, FAR), (1, 5), (2, 6), (3, 7))
KNOWN = 2 * TOK + SHORT
ROUND = TOK + SHORT
KEYS_SHORT = 2 * (FAR + 1) * SHORT
KEYS_LONG = 2 * (NEAR + 1) * LONG
KEYS = KEYS_SHORT + KEYS_LONG
FF_CHUNK = 512
NORM_ROWS = 304

epsilon = 1e-06
theta_base = 10000.0
masked_score = -1e30

SEQ = ("x", "z", "core")
CHIP = ("x", "z")
ALL = ("x", "z", "core", "dp")
HALF_FF = FF // 2
AT_GATE, AT_UP, AT_MIXED, AT_NORMED, AT_OUT, AT_BRANCH = 1024, 2048, 3072, 3584, 4224, 4864
ACTS = 5504
A_GATE, A_UP, A_DOWN, A_PROJ, A_GAIN, A_ROWS = 0, 5120, 10240, 15360, 17920, 18432
B_QUERY, B_KV, B_GAIN, B_ROWS = 0, 2560, 3840, 4096
DP = 4
A_DP = 7168
A_XZ = A_ROWS - A_DP
A_DP_PIECE, B_PIECE, A_XZ_PIECE = A_DP // DP, B_ROWS // DP, A_XZ // CHIPS
A_DP_BLOCK, B_BLOCK, A_XZ_BLOCK = A_DP_PIECE // CHIPS, B_PIECE // CHIPS, A_XZ_PIECE // DP
BLOCK = A_DP_BLOCK + B_BLOCK + A_XZ_BLOCK
XZ_FIRST = 192
JOINED = XZ_FIRST - A_DP_BLOCK - B_BLOCK
DP_FIRST = A_XZ_BLOCK - JOINED

bf16 = jnp.bfloat16
f32 = jnp.float32


def mm(left, right):
    return jnp.dot(left, right, preferred_element_type=f32)


def mm_tn(left, right):
    return lax.dot_general(left, right, (((0,), (0,)), ((), ())), preferred_element_type=f32)


def mm_nt(left, right):
    return lax.dot_general(left, right, (((1,), (1,)), ((), ())), preferred_element_type=f32)


def window_groups():
    groups = []
    for pieces in WINDOW_PARTS:
        for behind in pieces:
            groups.append((behind, "short", 0))
            if behind <= NEAR:
                groups += [(behind, "long", 0), (behind, "long", 1)]
    return groups


def key_row(side, group):
    behind, kind, part = group
    if kind == "short":
        return side * (KEYS_SHORT // 2) + behind * SHORT
    return KEYS_SHORT + side * (KEYS_LONG // 2) + behind * LONG + part * SHORT


def mask_bias(kind, chip, core):
    rows, width, first_key = (SHORT, KEYS_SHORT, 0) if kind == "short" else (LONG, KEYS_LONG, 0)
    half = width // 2
    column = lax.broadcasted_iota(jnp.int32, (1, width), 1)
    other = (column >= half).astype(jnp.int32)
    inner = column - other * half
    shift = 6 if kind == "short" else 7
    behind = lax.shift_right_logical(inner, shift)
    rest = inner & (rows - 1)
    key_core = core + other * (1 - 2 * core)
    key_position = (2 * (chip - behind) + key_core) * rows + rest
    query_position = (2 * chip + core) * rows + lax.broadcasted_iota(jnp.int32, (rows, 1), 0)
    distance = query_position - key_position
    allowed = (key_position >= 0) & (distance >= 0) & (distance < WINDOW)
    return jnp.where(allowed, 0.0, masked_score).astype(f32)


def group_tables(tables, chip, core, side, group):
    behind, kind, part = group
    piece = 2 * (chip - behind) + (core if side == 0 else 1 - core)
    at = jnp.maximum(piece if kind == "short" else 2 * piece + part, 0)
    cb, sb = tables[0, pl.ds(at, 1), :], tables[1, pl.ds(at, 1), :]
    cr, sr = tables[2], tables[3]
    return cb * cr - sb * sr, sb * cr + cb * sr


def rotary_tables():
    frequency = theta_base ** (-(np.arange(HALF) * 2.0 / HD))
    far = np.arange(SHORT)[:, None] * SHORT * frequency[None, :]
    near = np.arange(SHORT)[:, None] * frequency[None, :]
    return np.stack([np.cos(far), np.sin(far), np.cos(near), np.sin(near)]).astype(np.float32)


def place():
    return lax.axis_index("x") * 4 + lax.axis_index("z"), lax.axis_index("core")


def starts(lengths):
    short_first = (lengths[0, 0] == SHORT_LEN).astype(jnp.int32)
    return pl.multiple_of((1 - short_first) * LONG, SHORT), pl.multiple_of(short_first * SHORT, SHORT)


KINDS = (
    ("short", SHORT, 0, KEYS_SHORT, 0, 0),
    ("long", LONG, KEYS_SHORT, KEYS_LONG, HEADS * SHORT, SHORT),
)


def copies_of(pairs, sems, first=0):
    copies = [
        pltpu.make_async_copy(source, target, sems.at[first + number])
        for number, (source, target) in enumerate(pairs)
    ]
    for copy in copies:
        copy.start()
    return copies


class Stores:
    def __init__(self, sems):
        self.sems, self.copies = sems, []

    def start(self, source, target):
        self.copies += copies_of([(source, target)], self.sems, len(self.copies))

    def wait(self):
        for copy in self.copies:
            copy.wait()


def forward_kernel(
    lengths, tables, ga, gm, w0_h, w1_h, w2_h, w3_h, w4_h, w5_h, w6_h, w7_h, og_h, wq_h, wk_h, wv_h, wo_h, wg_h, wu_h, wd_h,
    ggain_o, q_h, k_h, v_h, gmix_h, norm_h, gres_h, bo_h, skv_h, keep_h, send_h,
    win, og, wq, wk, wv, wo, wg, wu, wd, norm, q, k, v, kv, scores_all, probs_all, mixed, gmix, gres,
    bo, skv, acts, bias_s, bias_l, out_sum, grad_sum, win_sem, sems, out_sem,
):
    chip, core = place()
    short_at, long_at = starts(lengths)
    window_loads = []
    for side, (known, *rounds) in enumerate(((w0_h, w1_h, w2_h, w3_h), (w4_h, w5_h, w6_h, w7_h))):
        base = side * SIDE
        at = base
        for source, pieces in zip((known, *rounds), WINDOW_PARTS):
            first = 0
            for behind in pieces:
                if behind <= NEAR:
                    window_loads += [
                        (source.at[pl.ds(first + short_at, SHORT)], win.at[pl.ds(at, SHORT)]),
                        (source.at[pl.ds(first + long_at, LONG)], win.at[pl.ds(at + SHORT, LONG)]),
                    ]
                    first, at = first + TOK, at + TOK
                else:
                    window_loads.append((source.at[pl.ds(first, SHORT)], win.at[pl.ds(at, SHORT)]))
                    first, at = first + SHORT, at + SHORT
    window_loads = copies_of(window_loads, win_sem)
    names = ("wk", "wv", "wq", "wo", "ogs", "ogl", "wg", "wu", "wd")
    loads = dict(zip(names, copies_of((
        (wk_h, wk), (wv_h, wv), (wq_h, wq), (wo_h, wo),
        (og_h.at[pl.ds(short_at, SHORT)], og.at[pl.ds(0, SHORT)]),
        (og_h.at[pl.ds(long_at, LONG)], og.at[pl.ds(SHORT, LONG)]),
        (wg_h, wg), (wu_h, wu), (wd_h, wd),
    ), sems)))
    stores = Stores(out_sem)
    bias_s[...] = mask_bias("short", chip, core)
    bias_l[...] = mask_bias("long", chip, core)
    gain_a = ga[...].reshape(1, D)
    gain_m = gm[...].reshape(1, D)
    for copy in window_loads:
        copy.wait()

    def normalise(step, carry):
        rows = pl.ds(pl.multiple_of(step * NORM_ROWS, 16), NORM_ROWS)
        x = win[rows, :].astype(f32)
        scale = lax.rsqrt(jnp.mean(x * x, axis=-1, keepdims=True) + epsilon)
        norm[rows, :] = (x * scale * gain_a).astype(bf16)
        return carry

    lax.fori_loop(0, 2 * SIDE // NORM_ROWS, normalise, 0)
    stores.start(norm, norm_h)
    loads["wk"].wait()
    loads["wv"].wait()
    for side in range(2):
        normed = norm[side * SIDE : (side + 1) * SIDE, :]
        kv[:, :HD] = mm(normed, wk[...])
        kv[:, HD:] = mm(normed, wv[...])
        for number, group in enumerate(window_groups()):
            rows = slice(number * SHORT, (number + 1) * SHORT)
            cos, sin = group_tables(tables, chip, core, side, group)
            low_half, high_half = kv[rows, :HALF], kv[rows, HALF:HD]
            at = key_row(side, group)
            k[at : at + SHORT, :HALF] = (low_half * cos - high_half * sin).astype(bf16)
            k[at : at + SHORT, HALF:] = (high_half * cos + low_half * sin).astype(bf16)
            v[at : at + SHORT, :] = kv[rows, HD:].astype(bf16)
            if side == 0 and number < 3:
                skv[rows, :HD] = k[at : at + SHORT, :]
                skv[rows, HD:] = v[at : at + SHORT, :]
    stores.start(k, k_h)
    stores.start(v, v_h)
    stores.start(skv.at[pl.ds(0, SHORT)], skv_h.at[pl.ds(short_at, SHORT)])
    stores.start(skv.at[pl.ds(SHORT, LONG)], skv_h.at[pl.ds(long_at, LONG)])

    loads["wq"].wait()
    query_raw = mm(norm[:TOK, :], wq[...])
    for number in range(3):
        rows = slice(number * SHORT, (number + 1) * SHORT)
        cos, sin = group_tables(tables, chip, core, 0, window_groups()[number])
        for head in range(HEADS):
            low_half = query_raw[rows, head * HD : head * HD + HALF]
            high_half = query_raw[rows, head * HD + HALF : (head + 1) * HD]
            at = head * SHORT if number == 0 else HEADS * SHORT + head * LONG + (number - 1) * SHORT
            q[at : at + SHORT, :HALF] = (low_half * cos - high_half * sin).astype(bf16) * bf16(HD**-0.5)
            q[at : at + SHORT, HALF:] = (high_half * cos + low_half * sin).astype(bf16) * bf16(HD**-0.5)
    stores.start(q, q_h)

    for kind, rows, key_at, width, query_at, row_at in KINDS:
        bias = bias_s if kind == "short" else bias_l
        count = HEADS * rows
        scores_all[:count, :width] = mm_nt(q[query_at : query_at + count, :], k[key_at : key_at + width, :])
        for head in range(HEADS):
            here = slice(head * rows, (head + 1) * rows)
            scores = scores_all[here, :width] + bias[...]
            exponent = jnp.exp(scores - jnp.max(scores, axis=-1, keepdims=True))
            share = 1.0 / jnp.sum(exponent, axis=-1, keepdims=True)
            probs_all[here, :width] = (exponent * share).astype(bf16)
        mixed_all = mm(probs_all[:count, :width], v[key_at : key_at + width, :]).astype(bf16)
        for head in range(HEADS):
            mixed[row_at : row_at + rows, head * HD : (head + 1) * HD] = mixed_all[
                head * rows : (head + 1) * rows, :
            ]

    loads["wo"].wait()
    resid = win[:TOK, :].astype(f32) + mm(mixed[...], wo[...])
    scale = lax.rsqrt(jnp.mean(resid * resid, axis=-1, keepdims=True) + epsilon)
    unit = resid * scale
    normed_mlp = (unit * gain_m).astype(bf16)
    for name in ("ogs", "ogl", "wg", "wu", "wd"):
        loads[name].wait()
    grad_out = og[...]
    for half in range(2):
        acts[half, :, AT_MIXED:AT_NORMED] = mixed[:, half * 2 * HD : (half + 1) * 2 * HD]
        acts[half, :, AT_NORMED:AT_OUT] = normed_mlp
        acts[half, :, AT_OUT:AT_BRANCH] = grad_out
    out_sum[...] = resid
    grad_sum[...] = jnp.zeros((TOK, D), f32)

    def feed_forward(chunk, carry):
        cols = pl.ds(pl.multiple_of(chunk * FF_CHUNK, FF_CHUNK), FF_CHUNK)
        gate = mm(normed_mlp, wg[:, cols])
        up = mm(normed_mlp, wu[:, cols])
        sig = jax.nn.sigmoid(gate)
        silu = gate * sig
        act = (silu * up).astype(bf16)
        grad_act = mm_nt(grad_out, wd[cols, :])
        grad_gate = (grad_act * up * sig * (1.0 + gate * (1.0 - sig))).astype(bf16)
        grad_up = (grad_act * silu).astype(bf16)
        out_sum[...] += mm(act, wd[cols, :])
        grad_sum[...] += mm_nt(grad_gate, wg[:, cols]) + mm_nt(grad_up, wu[:, cols])
        half, at = chunk // 2, chunk % 2 * FF_CHUNK
        for first, values in ((0, act), (AT_GATE, grad_gate), (AT_UP, grad_up)):
            acts[half, :, pl.ds(pl.multiple_of(first + at, FF_CHUNK), FF_CHUNK)] = values
        return carry

    lax.fori_loop(0, FF // FF_CHUNK, feed_forward, 0, unroll=2)
    block_out, grad_normed = out_sum[...], grad_sum[...]
    stores.start(acts.at[1 - core, :, pl.ds(0, AT_BRANCH)], send_h.at[:, pl.ds(0, AT_BRANCH)])
    stores.start(acts.at[core, :, pl.ds(0, AT_BRANCH)], keep_h.at[:, pl.ds(0, AT_BRANCH)])
    ggain_o[...] = jnp.sum(grad_normed * unit, axis=0, keepdims=True)
    scaled = grad_normed * gain_m
    grad_resid = grad_out.astype(f32) + scale * (
        scaled - unit * jnp.mean(scaled * unit, axis=-1, keepdims=True)
    )
    grad_branch = grad_resid.astype(bf16)
    for half in range(2):
        acts[half, :, AT_BRANCH:] = grad_branch
    rest = pl.ds(AT_BRANCH, ACTS - AT_BRANCH)
    stores.start(acts.at[1 - core, :, rest], send_h.at[:, rest])
    stores.start(acts.at[core, :, rest], keep_h.at[:, rest])
    gres[...] = grad_resid
    stores.start(gres, gres_h)
    bo[...] = block_out.astype(bf16)
    stores.start(bo.at[pl.ds(0, SHORT)], bo_h.at[pl.ds(short_at, SHORT)])
    stores.start(bo.at[pl.ds(SHORT, LONG)], bo_h.at[pl.ds(long_at, LONG)])
    grad_mixed = mm_nt(grad_branch, wo[...]).astype(bf16)
    for head in range(HEADS):
        cols = slice(head * HD, (head + 1) * HD)
        gmix[head * SHORT : (head + 1) * SHORT, :] = grad_mixed[:SHORT, cols]
        at = HEADS * SHORT + head * LONG
        gmix[at : at + LONG, :] = grad_mixed[SHORT:, cols]
    stores.start(gmix, gmix_h)
    stores.wait()


def backward_kernel(
    tables, ga, q_h, k_h, v_h, gmix_h, norm_h, wq_h, wk_h, wv_h,
    mine_h, other_h, gnq_h, keep_h, send_h,
    q, k, v, gmix, norm, wq, wk, wv, scores_all, gp_all, probs_all, gs_all, ret, gq, gnq, b, bias_s, bias_l,
    sems, out_sem,
):
    chip, core = place()
    loads = copies_of((
        (q_h, q), (k_h, k), (gmix_h, gmix), (v_h, v), (norm_h, norm), (wq_h, wq), (wk_h, wk), (wv_h, wv),
    ), sems)
    stores = Stores(out_sem)
    bias_s[...] = mask_bias("short", chip, core)
    bias_l[...] = mask_bias("long", chip, core)
    for copy in loads[:4]:
        copy.wait()
    for kind, rows, key_at, width, query_at, row_at in KINDS:
        bias = bias_s if kind == "short" else bias_l
        keys = k[key_at : key_at + width, :]
        count = HEADS * rows
        stack = slice(query_at, query_at + count)
        scores_all[:count, :width] = mm_nt(q[stack, :], keys)
        gp_all[:count, :width] = mm_nt(gmix[stack, :], v[key_at : key_at + width, :])
        for head in range(HEADS):
            here = slice(head * rows, (head + 1) * rows)
            scores = scores_all[here, :width] + bias[...]
            exponent = jnp.exp(scores - jnp.max(scores, axis=-1, keepdims=True))
            probs = exponent * (1.0 / jnp.sum(exponent, axis=-1, keepdims=True))
            probs_all[here, :width] = probs.astype(bf16)
            grad_probs = gp_all[here, :width]
            inner = jnp.sum(probs * grad_probs, axis=-1, keepdims=True)
            gs_all[here, :width] = (probs * (grad_probs - inner)).astype(bf16)
        grad_queries = mm(gs_all[:count, :width], keys) * (HD**-0.5)
        for head in range(HEADS):
            for part in range(rows // SHORT):
                number = 0 if kind == "short" else 1 + part
                cos, sin = group_tables(tables, chip, core, 0, window_groups()[number])
                at = head * rows + part * SHORT
                low_half = grad_queries[at : at + SHORT, :HALF]
                high_half = grad_queries[at : at + SHORT, HALF:]
                to = slice(row_at + part * SHORT, row_at + (part + 1) * SHORT)
                gq[to, head * HD : head * HD + HALF] = (low_half * cos + high_half * sin).astype(bf16)
                gq[to, head * HD + HALF : (head + 1) * HD] = (high_half * cos - low_half * sin).astype(bf16)
        grad_keys = mm_tn(gs_all[:count, :width], q[stack, :])
        grad_values = mm_tn(probs_all[:count, :width], gmix[stack, :])
        for side in range(2):
            for number, group in enumerate(window_groups()):
                if group[1] != kind:
                    continue
                at = key_row(side, group) - key_at
                cos, sin = group_tables(tables, chip, core, side, group)
                low_half = grad_keys[at : at + SHORT, :HALF]
                high_half = grad_keys[at : at + SHORT, HALF:]
                to = slice(number * SHORT, (number + 1) * SHORT)
                ret[side, to, :HALF] = (low_half * cos + high_half * sin).astype(bf16)
                ret[side, to, HALF:HD] = (high_half * cos - low_half * sin).astype(bf16)
                ret[side, to, HD:] = grad_values[at : at + SHORT, :].astype(bf16)
    stores.start(ret.at[0], mine_h)
    stores.start(ret.at[1], other_h)
    for copy in loads[4:]:
        copy.wait()
    gnq[...] = mm_nt(gq[...], wq[...])
    stores.start(gnq, gnq_h)
    grad_gain = jnp.sum(gnq[...] * norm[:TOK, :].astype(f32), axis=0, keepdims=True)
    for step in range(8):
        side, first = step // 4, step % 4 * (SIDE // 4)
        rows = slice(first, first + SIDE // 4)
        grad_normed = mm_nt(ret[side, rows, :HD], wk[...]) + mm_nt(ret[side, rows, HD:], wv[...])
        here = norm[side * SIDE + first : side * SIDE + first + SIDE // 4, :].astype(f32)
        grad_gain = grad_gain + jnp.sum(grad_normed * here, axis=0, keepdims=True)
    grad_gain = grad_gain / ga[...].reshape(1, D)

    def put(half, at, block):
        for part in range(block.shape[1] // HALF):
            row = at + part * D
            b[half, row : row + D, :] = block[:, part * HALF : (part + 1) * HALF].astype(bf16)

    b[0, B_GAIN:, :] = jnp.zeros((B_ROWS - B_GAIN, HALF), bf16)
    b[1, B_GAIN:, :] = jnp.zeros((B_ROWS - B_GAIN, HALF), bf16)
    for part in range(D // HALF):
        b[0, B_GAIN + 16 * part : B_GAIN + 16 * part + 16, :] = jnp.broadcast_to(
            grad_gain[:, part * HALF : (part + 1) * HALF], (16, HALF)
        ).astype(bf16)
    for half in range(2):
        put(half, B_QUERY, mm_tn(norm[:TOK, :], gq[:, half * 2 * HD : (half + 1) * 2 * HD]))
    both = mm_tn(norm[:SIDE, :], ret[0]) + mm_tn(norm[SIDE:, :], ret[1])
    for half in range(2):
        put(half, B_KV, both[:, half * HD : (half + 1) * HD])
    stores.start(b.at[1 - core], send_h)
    stores.start(b.at[core], keep_h)
    stores.wait()


def pieces_out(stores, pieces, outs):
    me = lax.axis_index("dp")
    for step, out in enumerate(outs):
        stores.start(pieces.at[lax.rem(me + step, DP)], out)


def halves_kernel(ggain, keep_h, recv_h, p0_h, p1_h, p2_h, p3_h, xz_h, x, pieces, xz, sems, out_sem):
    copies = copies_of(((keep_h, x.at[pl.ds(0, TOK)]), (recv_h, x.at[pl.ds(TOK, TOK)])), sems)
    stores = Stores(out_sem)
    for copy in copies:
        copy.wait()

    def write(at, values):
        done, rows = 0, values.shape[0]
        while done < rows:
            row = at + done
            if row < A_DP:
                piece, inner = row // A_DP_PIECE, row % A_DP_PIECE
                size = min(rows - done, A_DP_PIECE - inner)
                pieces[piece, inner : inner + size, :] = values[done : done + size, :]
            else:
                piece, inner = (row - A_DP) // A_XZ_PIECE, (row - A_DP) % A_XZ_PIECE
                size = min(rows - done, A_XZ_PIECE - inner)
                xz[piece, inner : inner + size, :] = values[done : done + size, :]
            done += size

    def put(at, block):
        rows = block.shape[0]
        for part in range(block.shape[1] // HALF):
            write(at + part * rows, block[:, part * HALF : (part + 1) * HALF].astype(bf16))

    normed = x[:, AT_NORMED:AT_OUT]
    for chunk in range(2):
        cols = slice(AT_GATE + chunk * FF_CHUNK, AT_GATE + (chunk + 1) * FF_CHUNK)
        put(A_GATE + chunk * 4 * D, mm_tn(normed, x[:, cols]))
    for chunk in range(2):
        cols = slice(AT_UP + chunk * FF_CHUNK, AT_UP + (chunk + 1) * FF_CHUNK)
        put(A_UP + chunk * 4 * D, mm_tn(normed, x[:, cols]))
        if chunk == 0:
            pieces_out(stores, pieces, (p0_h, p1_h, p2_h, p3_h))
    put(A_DOWN, mm_tn(x[:, :AT_GATE], x[:, AT_OUT:AT_BRANCH]))
    put(A_PROJ, mm_tn(x[:, AT_MIXED:AT_NORMED], x[:, AT_BRANCH:]))
    for part in range(D // HALF):
        write(A_GAIN + 16 * part, jnp.broadcast_to(
            ggain[:, part * HALF : (part + 1) * HALF], (16, HALF)
        ).astype(bf16))
    end = A_GAIN + 16 * (D // HALF)
    write(end, jnp.zeros((A_ROWS - end, HALF), bf16))
    stores.start(xz, xz_h)
    stores.wait()


def chip_sum_kernel(keep, recv, p0_h, p1_h, p2_h, p3_h, pieces, out_sem):
    stores = Stores(out_sem)
    for piece in range(DP):
        rows = slice(piece * B_PIECE, (piece + 1) * B_PIECE)
        pieces[piece] = (keep[rows, :].astype(f32) + recv[rows, :].astype(f32)).astype(bf16)
    pieces_out(stores, pieces, (p0_h, p1_h, p2_h, p3_h))
    stores.wait()


def first_sum_kernel(
    a0, a1, a2, a3, b0, b1, b2, b3, xz, out_xz, p0_h, p1_h, p2_h, p3_h, pieces, out_sem
):
    stores = Stores(out_sem)
    for piece in range(DP):
        rows = slice(piece * A_XZ_BLOCK, (piece + 1) * A_XZ_BLOCK)
        total = xz[0, rows, :].astype(f32)
        for chip in range(1, CHIPS):
            total = total + xz[chip, rows, :].astype(f32)
        pieces[piece] = total.astype(bf16)
    pieces_out(stores, pieces, (p0_h, p1_h, p2_h, p3_h))
    for chip in range(CHIPS):
        for at, size, parts in ((0, A_DP_BLOCK, (a0, a1, a2, a3)), (A_DP_BLOCK, B_BLOCK, (b0, b1, b2, b3))):
            rows = slice(chip * size, (chip + 1) * size)
            total = (parts[0][rows, :].astype(f32) + parts[1][rows, :].astype(f32)) + (
                parts[2][rows, :].astype(f32) + parts[3][rows, :].astype(f32)
            )
            out_xz[chip, at : at + size, :] = total.astype(bf16)
    stores.wait()


def second_sum_kernel(xz, c0, c1, c2, c3, copies_h, own, total, out_sem):
    stores = Stores(out_sem)
    rest = (
        (c0[...].astype(f32) + c1[...].astype(f32)) + (c2[...].astype(f32) + c3[...].astype(f32))
    ).astype(bf16)
    own[...] = rest[JOINED:, :]
    value = xz[0].astype(f32)
    for chip in range(1, CHIPS):
        value = value + xz[chip].astype(f32)
    total[: XZ_FIRST - JOINED, :] = value.astype(bf16)
    total[XZ_FIRST - JOINED :, :] = rest[:JOINED, :]
    for chip in range(CHIPS):
        stores.start(total, copies_h.at[chip])
    stores.wait()


def spread_kernel(d0, d1, d2, d3, copies_h, rows, out_sem):
    stores = Stores(out_sem)
    me = lax.axis_index("dp")
    for step, part in enumerate((d0, d1, d2, d3)):
        rows[lax.rem(me + DP - step, DP)] = part[...]
    for chip in range(CHIPS):
        stores.start(rows, copies_h.at[chip])
    stores.wait()


def window_sum_kernel(mine, other, known, r1, r2, r3):
    at = 0
    for out in (known, r1, r2, r3):
        rows = slice(at, at + out.shape[0])
        out[...] = (mine[rows, :].astype(f32) + other[rows, :].astype(f32)).astype(bf16)
        at += out.shape[0]


def turn_back_kernel(known, c1, c2, c3, own, back, far_back):
    ahead = lax.axis_index("z")
    own_sum = known[:TOK, :].astype(f32)
    back_sum = known[TOK : 2 * TOK, :].astype(f32)
    far_sum = known[2 * TOK :, :].astype(f32)
    for step, came in enumerate((c1, c2, c3), 1):
        same = (ahead + step < 4).astype(f32)
        near, far = came[:TOK, :].astype(f32), came[TOK:, :].astype(f32)
        own_sum = own_sum + near * same
        back_sum = back_sum + near * (1.0 - same)
        back_sum = jnp.concatenate([back_sum[:SHORT, :] + far * same, back_sum[SHORT:, :]], axis=0)
        far_sum = far_sum + far * (1.0 - same)
    own[...] = own_sum
    back[...] = back_sum.astype(bf16)
    far_back[...] = far_sum.astype(bf16)


def token_grad_kernel(lengths, ga, own, back, far_back, gnq, gres, tokens_h, wk, wv, out_h, x, out, sems):
    short_at, long_at = starts(lengths)
    loads = copies_of((
        (tokens_h.at[pl.ds(short_at, SHORT)], x.at[pl.ds(0, SHORT)]),
        (tokens_h.at[pl.ds(long_at, LONG)], x.at[pl.ds(SHORT, LONG)]),
    ), sems)
    total = own[...] + back[...].astype(f32)
    total = jnp.concatenate([total[:SHORT, :] + far_back[...].astype(f32), total[SHORT:, :]], axis=0).astype(bf16)
    grad_normed = gnq[...] + mm_nt(total[:, :HD], wk[...]) + mm_nt(total[:, HD:], wv[...])
    for copy in loads:
        copy.wait()
    wide = x[...].astype(f32)
    scale = lax.rsqrt(jnp.mean(wide * wide, axis=-1, keepdims=True) + epsilon)
    unit = wide * scale
    scaled = grad_normed * ga[...].reshape(1, D)
    out[...] = gres[...] + scale * (scaled - unit * jnp.mean(scaled * unit, axis=-1, keepdims=True))
    stores = copies_of((
        (out.at[pl.ds(0, SHORT)], out_h.at[pl.ds(short_at, SHORT)]),
        (out.at[pl.ds(SHORT, LONG)], out_h.at[pl.ds(long_at, LONG)]),
    ), sems, 2)
    for copy in stores:
        copy.wait()


def unpack_kernel(
    e0_h, e1_h, e2_h, e3_h, f_h, o0_h, o1_h, o2_h, o3_h, p_h,
    gain_a_o, gain_m_o, gate_h, up_h, down_h, proj_h, query_h, key_h, value_h,
    a_dp, a_xz, b, gate, up, down, proj, query, key, value, sems, out_sem,
):
    mine, me = lax.axis_index("core"), lax.axis_index("dp")
    sides = ((mine, (e0_h, e1_h, e2_h, e3_h), f_h), (1 - mine, (o0_h, o1_h, o2_h, o3_h), p_h))
    firsts, seconds, thirds = [], [], []
    for side, parts, xz_h in sides:
        for step, part in enumerate(parts):
            dp = lax.rem(me + DP - step, DP)
            firsts.append((part.at[:, pl.ds(0, A_DP_BLOCK)], a_dp.at[side, dp]))
            seconds.append((part.at[:, pl.ds(A_DP_BLOCK, B_BLOCK)], b.at[side, dp]))
            thirds.append((part.at[:, pl.ds(XZ_FIRST - JOINED, JOINED)], a_xz.at[side, :, dp, pl.ds(0, JOINED)]))
        thirds.append((xz_h, a_xz.at[side, :, :, pl.ds(JOINED, DP_FIRST)]))
    loads = copies_of(firsts + seconds + thirds, sems)
    stores = Stores(out_sem)

    def pieces_of(core, at, rows, in_b):
        done = 0
        while done < rows:
            row = at + done
            if in_b:
                source, size = b, B_BLOCK
                index = (core, row // B_PIECE, row % B_PIECE // B_BLOCK)
            elif row < A_DP:
                source, size = a_dp, A_DP_BLOCK
                index = (core, row // A_DP_PIECE, row % A_DP_PIECE // A_DP_BLOCK)
            else:
                row = row - A_DP
                source, size = a_xz, A_XZ_BLOCK
                index = (core, row // A_XZ_PIECE, row % A_XZ_PIECE // A_XZ_BLOCK)
            inner = row % size
            size = min(rows - done, size - inner)
            yield done, size, source[index + (slice(inner, inner + size), slice(None))].astype(f32)
            done += size

    def unpack(target, at, rows, in_b, place_of, count, cores=(0, 1)):
        for core in cores:
            for part in range(count):
                row, col = place_of(core, part)
                for done, size, values in pieces_of(core, at + part * rows, rows, in_b):
                    target[row + done : row + done + size, col : col + HALF] = values

    for copy in loads[: 2 * DP]:
        copy.wait()
    unpack(gate, A_GATE, D, False, lambda core, part: (0, core * HALF_FF + part * HALF), HALF_FF // HALF)
    stores.start(gate, gate_h)
    for copy in loads[2 * DP : 4 * DP]:
        copy.wait()
    unpack(query, B_QUERY, D, True, lambda core, part: (0, core * 2 * HD + part * HALF), 4)
    stores.start(query, query_h)
    unpack(key, B_KV, D, True, lambda core, part: (0, part * HALF), 2, (0,))
    stores.start(key, key_h)
    unpack(value, B_KV, D, True, lambda core, part: (0, part * HALF), 2, (1,))
    stores.start(value, value_h)
    for copy in loads[4 * DP :]:
        copy.wait()
    unpack(up, A_UP, D, False, lambda core, part: (0, core * HALF_FF + part * HALF), HALF_FF // HALF)
    stores.start(up, up_h)
    unpack(down, A_DOWN, HALF_FF, False, lambda core, part: (core * HALF_FF, part * HALF), D // HALF)
    stores.start(down, down_h)
    unpack(proj, A_PROJ, 2 * HD, False, lambda core, part: (core * 2 * HD, part * HALF), D // HALF)
    stores.start(proj, proj_h)
    for out, at, in_b in ((gain_a_o, B_GAIN, True), (gain_m_o, A_GAIN, False)):
        for part in range(D // HALF):
            (_, _, first), = pieces_of(0, at + 16 * part, 1, in_b)
            (_, _, second), = pieces_of(1, at + 16 * part, 1, in_b)
            out[part * HALF : (part + 1) * HALF] = (first + second).reshape(HALF)
    stores.wait()


VMEM = pl.BlockSpec(memory_space=pltpu.VMEM)
SMEM = pl.BlockSpec(memory_space=pltpu.SMEM)
ANY = pl.BlockSpec(memory_space=pl.ANY)


def shape(dims, kind=bf16):
    return jax.ShapeDtypeStruct(dims, kind)


def limit(mib):
    return pltpu.CompilerParams(vmem_limit_bytes=mib * 2**20)


def cost(flops, moved):
    return pl.CostEstimate(flops=flops, bytes_accessed=moved, transcendentals=0)


def scratch(*dims, kind=bf16):
    return pltpu.VMEM(dims, kind)


def semaphores(count):
    return pltpu.SemaphoreType.DMA((count,))


def run_forward(*operands):
    return pl.pallas_call(
        forward_kernel,
        in_specs=[SMEM] + [VMEM] * 3 + [ANY] * 16,
        out_specs=[VMEM] + [ANY] * 10,
        out_shape=[
            shape((1, D), f32),
            shape((HEADS * TOK, HD)), shape((KEYS, HD)), shape((KEYS, HD)), shape((HEADS * TOK, HD)),
            shape((2 * SIDE, D)), shape((TOK, D), f32),
            shape((TOK, D)), shape((TOK, 2 * HD)), shape((TOK, ACTS)), shape((TOK, ACTS)),
        ],
        scratch_shapes=[
            scratch(2 * SIDE, D), scratch(TOK, D), scratch(D, HEADS * HD), scratch(D, HD), scratch(D, HD),
            scratch(HEADS * HD, D), scratch(D, FF), scratch(D, FF), scratch(FF, D),
            scratch(2 * SIDE, D), scratch(HEADS * TOK, HD), scratch(KEYS, HD), scratch(KEYS, HD),
            scratch(SIDE, 2 * HD, kind=f32), scratch(HEADS * LONG, KEYS_LONG, kind=f32),
            scratch(HEADS * LONG, KEYS_LONG), scratch(TOK, HEADS * HD), scratch(HEADS * TOK, HD),
            scratch(TOK, D, kind=f32), scratch(TOK, D), scratch(TOK, 2 * HD), scratch(2, TOK, ACTS),
            scratch(SHORT, KEYS_SHORT, kind=f32), scratch(LONG, KEYS_LONG, kind=f32),
            scratch(TOK, D, kind=f32), scratch(TOK, D, kind=f32),
            semaphores(28), semaphores(9), semaphores(14),
        ],
        compiler_params=limit(58),
        cost_estimate=cost(8 * 10**9, 3 * 10**7),
        name="forward",
    )(*operands)


def run_backward(*operands):
    return pl.pallas_call(
        backward_kernel,
        in_specs=[VMEM] * 2 + [ANY] * 8,
        out_specs=[ANY] * 5,
        out_shape=[
            shape((SIDE, 2 * HD)), shape((SIDE, 2 * HD)), shape((TOK, D), f32),
            shape((B_ROWS, HALF)), shape((B_ROWS, HALF)),
        ],
        scratch_shapes=[
            scratch(HEADS * TOK, HD), scratch(KEYS, HD), scratch(KEYS, HD), scratch(HEADS * TOK, HD),
            scratch(2 * SIDE, D), scratch(D, HEADS * HD), scratch(D, HD), scratch(D, HD),
            scratch(HEADS * LONG, KEYS_LONG, kind=f32), scratch(HEADS * LONG, KEYS_LONG, kind=f32),
            scratch(HEADS * LONG, KEYS_LONG), scratch(HEADS * LONG, KEYS_LONG),
            scratch(2, SIDE, 2 * HD), scratch(TOK, HEADS * HD), scratch(TOK, D, kind=f32),
            scratch(2, B_ROWS, HALF),
            scratch(SHORT, KEYS_SHORT, kind=f32), scratch(LONG, KEYS_LONG, kind=f32),
            semaphores(8), semaphores(5),
        ],
        compiler_params=limit(54),
        cost_estimate=cost(10**12, 10**9),
        name="backward",
    )(*operands)


def run_halves(*operands):
    return pl.pallas_call(
        halves_kernel,
        in_specs=[VMEM, ANY, ANY],
        out_specs=[ANY] * 5,
        out_shape=[shape((A_DP_PIECE, HALF))] * 4 + [shape((CHIPS, A_XZ_PIECE, HALF))],
        scratch_shapes=[
            scratch(2 * TOK, ACTS), scratch(DP, A_DP_PIECE, HALF), scratch(CHIPS, A_XZ_PIECE, HALF),
            semaphores(2), semaphores(5),
        ],
        compiler_params=limit(20),
        cost_estimate=cost(2 * 10**9, 10**7),
        name="halves",
    )(*operands)


def run_chip_sum(*operands):
    return pl.pallas_call(
        chip_sum_kernel,
        in_specs=[VMEM] * 2,
        out_specs=[ANY] * 4,
        out_shape=[shape((B_PIECE, HALF))] * 4,
        scratch_shapes=[scratch(DP, B_PIECE, HALF), semaphores(4)],
        compiler_params=limit(8),
        cost_estimate=cost(0, 0),
        name="chip_sum",
    )(*operands)


def run_first_sum(*operands):
    return pl.pallas_call(
        first_sum_kernel,
        in_specs=[VMEM] * 9,
        out_specs=[VMEM] + [ANY] * 4,
        out_shape=[shape((CHIPS, A_DP_BLOCK + B_BLOCK, HALF))] + [shape((A_XZ_BLOCK, HALF))] * 4,
        scratch_shapes=[scratch(DP, A_XZ_BLOCK, HALF), semaphores(4)],
        compiler_params=limit(12),
        cost_estimate=cost(10**6, 8 * 10**6),
        name="first_sum",
    )(*operands)


def run_second_sum(*operands):
    return pl.pallas_call(
        second_sum_kernel,
        in_specs=[VMEM] * 5,
        out_specs=[ANY, VMEM],
        out_shape=[shape((CHIPS, XZ_FIRST, HALF)), shape((DP_FIRST, HALF))],
        scratch_shapes=[scratch(XZ_FIRST, HALF), semaphores(CHIPS)],
        compiler_params=limit(4),
        cost_estimate=cost(10**6, 10**6),
        name="second_sum",
    )(*operands)


def run_spread(*operands):
    return pl.pallas_call(
        spread_kernel,
        in_specs=[VMEM] * 4,
        out_specs=ANY,
        out_shape=shape((CHIPS, DP, DP_FIRST, HALF)),
        scratch_shapes=[scratch(DP, DP_FIRST, HALF), semaphores(CHIPS)],
        compiler_params=limit(4),
        cost_estimate=cost(0, 10**6),
        name="spread",
    )(*operands)


def run_unpack(*operands):
    return pl.pallas_call(
        unpack_kernel,
        in_specs=[ANY] * 10,
        out_specs=[VMEM] * 2 + [ANY] * 7,
        out_shape=[
            shape((D,), f32), shape((D,), f32), shape((D, FF), f32), shape((D, FF), f32),
            shape((FF, D), f32), shape((HEADS * HD, D), f32), shape((D, HEADS * HD), f32),
            shape((D, HD), f32), shape((D, HD), f32),
        ],
        scratch_shapes=[
            scratch(2, DP, CHIPS, A_DP_BLOCK, HALF), scratch(2, CHIPS, DP, A_XZ_BLOCK, HALF),
            scratch(2, DP, CHIPS, B_BLOCK, HALF),
            scratch(D, FF, kind=f32), scratch(D, FF, kind=f32), scratch(FF, D, kind=f32),
            scratch(HEADS * HD, D, kind=f32), scratch(D, HEADS * HD, kind=f32), scratch(D, HD, kind=f32),
            scratch(D, HD, kind=f32), semaphores(26), semaphores(7),
        ],
        compiler_params=limit(40),
        cost_estimate=cost(0, 3 * 10**7),
        name="unpack",
    )(*operands)


def run_window_sum(*operands):
    return pl.pallas_call(
        window_sum_kernel,
        in_specs=[VMEM] * 2,
        out_specs=[VMEM] * 4,
        out_shape=[shape((KNOWN, 2 * HD)), *[shape((ROUND, 2 * HD))] * 3],
        compiler_params=limit(8),
        cost_estimate=cost(0, 10**6),
        name="window_sum",
    )(*operands)


def run_turn_back(*operands):
    return pl.pallas_call(
        turn_back_kernel,
        in_specs=[VMEM] * 4,
        out_specs=[VMEM] * 3,
        out_shape=[shape((TOK, 2 * HD), f32), shape((TOK, 2 * HD)), shape((SHORT, 2 * HD))],
        compiler_params=limit(8),
        cost_estimate=cost(10**12, 10**9),
        name="turn_back",
    )(*operands)


def run_token_grad(*operands):
    return pl.pallas_call(
        token_grad_kernel,
        in_specs=[SMEM] + [VMEM] * 6 + [ANY] + [VMEM] * 2,
        out_specs=ANY,
        out_shape=shape((TOK, D), f32),
        scratch_shapes=[scratch(TOK, D), scratch(TOK, D, kind=f32), semaphores(4)],
        compiler_params=limit(12),
        cost_estimate=cost(10**6, 10**6),
        name="token_grad",
    )(*operands)


def swap_cores(array):
    return lax.ppermute(array, "core", [(0, 1), (1, 0)])


def gather_dp(pieces):
    got = [pieces[0]]
    for step in range(1, DP):
        got.append(lax.ppermute(pieces[step], "dp", [(i, (i + step) % DP) for i in range(DP)]))
    return got


def shards(
    tokens, lengths, w_query, w_key, w_value, w_output, w_gate, w_up, w_down, gain_attn, gain_mlp, out_grad
):
    short_first = lengths[0, 0] == SHORT_LEN

    slots = tokens[0]
    short_at = jnp.where(short_first, 0, LONG)

    def short_of(rows):
        return lax.dynamic_slice_in_dim(rows, short_at, SHORT, 0)

    own_short = short_of(slots)
    back = lax.ppermute(slots, "x", [(i, i + 1) for i in range(3)])
    back_short = lax.ppermute(own_short, "x", [(i, i + 2) for i in range(2)])
    here = jnp.concatenate([slots, short_of(back)], axis=0)
    there = jnp.concatenate([back, back_short], axis=0)
    ahead = lax.axis_index("z")
    rounds = [
        lax.ppermute(
            jnp.where(ahead + step < 4, here, there), "z", [(i, (i + step) % 4) for i in range(4)]
        )
        for step in range(1, 4)
    ]
    known = jnp.concatenate([slots, there], axis=0)
    window = [known, *rounds, *[swap_cores(part) for part in (known, *rounds)]]
    tables = jnp.asarray(rotary_tables())
    (
        grad_gain_mlp, q, k, v, gmix, norm, grad_resid, block_out, shared_kv, kept, sent,
    ) = run_forward(
        lengths, tables, gain_attn, gain_mlp, *window, out_grad[0],
        w_query, w_key, w_value, w_output, w_gate, w_up, w_down,
    )
    *a_pieces, a_xz = run_halves(grad_gain_mlp, kept, swap_cores(sent))
    q, a_xz = lax.optimization_barrier((q, a_xz))
    a_xz = lax.all_to_all(a_xz, CHIP, 0, 0, tiled=True)
    a_got = gather_dp(a_pieces)
    mine, other, grad_normed_q, b_kept, b_sent = run_backward(
        tables, gain_attn, q, k, v, gmix, norm, w_query, w_key, w_value
    )
    b_kept, b_sent, *a_got = lax.optimization_barrier((b_kept, b_sent, *a_got))
    b_pieces = run_chip_sum(b_kept, swap_cores(b_sent))
    b_got = gather_dp(b_pieces)

    other = swap_cores(other)
    b_got[1], other = lax.optimization_barrier((b_got[1], other))
    known_back, *round_back = run_window_sum(mine, other)
    came = [
        lax.ppermute(rows, "z", [(i, (i - step) % 4) for i in range(4)]) for step, rows in enumerate(round_back, 1)
    ]
    first, *c_pieces = run_first_sum(*a_got, *b_got, a_xz)
    c_got = gather_dp(c_pieces)
    first = lax.all_to_all(first, CHIP, 0, 0, tiled=True)
    own_back, for_back, for_far_back = run_turn_back(known_back, *came)
    copies, own_xz = run_second_sum(first, *c_got)
    copies, for_back, for_far_back = lax.optimization_barrier((copies, for_back, for_far_back))
    dp_part = lax.all_to_all(copies, CHIP, 0, 0, tiled=True)
    xz_copies = run_spread(*gather_dp([own_xz] * DP))
    dp_part, xz_copies = lax.optimization_barrier((dp_part, xz_copies))
    dp_parts = gather_dp([dp_part] * DP)
    xz_parts = lax.all_to_all(xz_copies, CHIP, 0, 0, tiled=True)
    parts = [*dp_parts, xz_parts]
    from_back = lax.ppermute(for_back, "x", [(i + 1, i) for i in range(3)])
    from_far_back = lax.ppermute(for_far_back, "x", [(i + 2, i) for i in range(2)])
    *parts, from_back, from_far_back = lax.optimization_barrier((*parts, from_back, from_far_back))
    (
        total_gain_attn, total_gain_mlp, grad_gate, grad_up, grad_down, grad_proj, grad_query, grad_key, grad_value,
    ) = run_unpack(*parts, *[swap_cores(part) for part in parts])

    input_grad = run_token_grad(
        lengths, gain_attn, own_back, from_back, from_far_back, grad_normed_q, grad_resid, slots, w_key, w_value
    )
    return (
        block_out[None], shared_kv[None], input_grad[None],
        grad_query, grad_key, grad_value, grad_proj, grad_gate, grad_up, grad_down,
        total_gain_attn, total_gain_mlp,
    )


def solution(mesh):
    fine = Mesh(mesh.devices.reshape(4, 4, 2, 4), ALL)
    rows = P("dp", SEQ, None)
    return jax.shard_map(
        shards,
        mesh=fine,
        in_specs=(rows, P("dp", None)) + (P(),) * 9 + (rows,),
        out_specs=(rows, rows, rows) + (P(),) * 9,
        check_vma=False,
    )
```

```python
import jax
import jax.numpy as jnp
import numpy as np
from jax import lax
from jax.experimental import pallas as pl
from jax.experimental.pallas import tpu as pltpu
from jax.sharding import Mesh, PartitionSpec as P

WINDOW = 1024
SHORT_LEN = 2048
D = 640
HEADS = 4
HD = 256
HALF = 128
FF = 2048
TOK = 192
SHORT = 64
LONG = 128
CHIPS = 16
NEAR = 4
FAR = 8
SIDE = (NEAR + 1) * TOK + (FAR - NEAR) * SHORT
GROUPS = SIDE // SHORT
WINDOW_PARTS = ((0, NEAR, FAR), (1, 5), (2, 6), (3, 7))
KNOWN = 2 * TOK + SHORT
ROUND = TOK + SHORT
KEYS_SHORT = 2 * (FAR + 1) * SHORT
KEYS_LONG = 2 * (NEAR + 1) * LONG
KEYS = KEYS_SHORT + KEYS_LONG
FF_CHUNK = 512
NORM_ROWS = 304

epsilon = 1e-06
theta_base = 10000.0
masked_score = -1e30

SEQ = ("x", "z", "core")
CHIP = ("x", "z")
ALL = ("x", "z", "core", "dp")
HALF_FF = FF // 2
AT_GATE, AT_UP, AT_MIXED, AT_NORMED, AT_OUT, AT_BRANCH = 1024, 2048, 3072, 3584, 4224, 4864
ACTS = 5504
A_GATE, A_UP, A_DOWN, A_PROJ, A_GAIN, A_ROWS = 0, 5120, 10240, 15360, 17920, 18432
B_QUERY, B_KV, B_GAIN, B_ROWS = 0, 2560, 3840, 4096
DP = 4
A_DP = 7168
A_XZ = A_ROWS - A_DP
A_DP_PIECE, B_PIECE, A_XZ_PIECE = A_DP // DP, B_ROWS // DP, A_XZ // CHIPS
A_DP_BLOCK, B_BLOCK, A_XZ_BLOCK = A_DP_PIECE // CHIPS, B_PIECE // CHIPS, A_XZ_PIECE // DP
BLOCK = A_DP_BLOCK + B_BLOCK + A_XZ_BLOCK
XZ_FIRST = 192
JOINED = XZ_FIRST - A_DP_BLOCK - B_BLOCK
DP_FIRST = A_XZ_BLOCK - JOINED

bf16 = jnp.bfloat16
f32 = jnp.float32


def mm(left, right):
    return jnp.dot(left, right, preferred_element_type=f32)


def mm_tn(left, right):
    return lax.dot_general(left, right, (((0,), (0,)), ((), ())), preferred_element_type=f32)


def mm_nt(left, right):
    return lax.dot_general(left, right, (((1,), (1,)), ((), ())), preferred_element_type=f32)


def window_groups():
    groups = []
    for pieces in WINDOW_PARTS:
        for behind in pieces:
            groups.append((behind, "short", 0))
            if behind <= NEAR:
                groups += [(behind, "long", 0), (behind, "long", 1)]
    return groups


def key_row(side, group):
    behind, kind, part = group
    if kind == "short":
        return side * (KEYS_SHORT // 2) + behind * SHORT
    return KEYS_SHORT + side * (KEYS_LONG // 2) + behind * LONG + part * SHORT


def mask_bias(kind, chip, core):
    rows, width, first_key = (SHORT, KEYS_SHORT, 0) if kind == "short" else (LONG, KEYS_LONG, 0)
    half = width // 2
    column = lax.broadcasted_iota(jnp.int32, (1, width), 1)
    other = (column >= half).astype(jnp.int32)
    inner = column - other * half
    shift = 6 if kind == "short" else 7
    behind = lax.shift_right_logical(inner, shift)
    rest = inner & (rows - 1)
    key_core = core + other * (1 - 2 * core)
    key_position = (2 * (chip - behind) + key_core) * rows + rest
    query_position = (2 * chip + core) * rows + lax.broadcasted_iota(jnp.int32, (rows, 1), 0)
    distance = query_position - key_position
    allowed = (key_position >= 0) & (distance >= 0) & (distance < WINDOW)
    return jnp.where(allowed, 0.0, masked_score).astype(f32)


def group_tables(tables, chip, core, side, group):
    behind, kind, part = group
    piece = 2 * (chip - behind) + (core if side == 0 else 1 - core)
    at = jnp.maximum(piece if kind == "short" else 2 * piece + part, 0)
    cb, sb = tables[0, pl.ds(at, 1), :], tables[1, pl.ds(at, 1), :]
    cr, sr = tables[2], tables[3]
    return cb * cr - sb * sr, sb * cr + cb * sr


def rotary_tables():
    frequency = theta_base ** (-(np.arange(HALF) * 2.0 / HD))
    far = np.arange(SHORT)[:, None] * SHORT * frequency[None, :]
    near = np.arange(SHORT)[:, None] * frequency[None, :]
    return np.stack([np.cos(far), np.sin(far), np.cos(near), np.sin(near)]).astype(np.float32)


def place():
    return lax.axis_index("x") * 4 + lax.axis_index("z"), lax.axis_index("core")


def starts(lengths):
    short_first = (lengths[0, 0] == SHORT_LEN).astype(jnp.int32)
    return pl.multiple_of((1 - short_first) * LONG, SHORT), pl.multiple_of(short_first * SHORT, SHORT)


KINDS = (
    ("short", SHORT, 0, KEYS_SHORT, 0, 0),
    ("long", LONG, KEYS_SHORT, KEYS_LONG, HEADS * SHORT, SHORT),
)


def copies_of(pairs, sems, first=0):
    copies = [
        pltpu.make_async_copy(source, target, sems.at[first + number])
        for number, (source, target) in enumerate(pairs)
    ]
    for copy in copies:
        copy.start()
    return copies


class Stores:
    def __init__(self, sems):
        self.sems, self.copies = sems, []

    def start(self, source, target):
        self.copies += copies_of([(source, target)], self.sems, len(self.copies))

    def wait(self):
        for copy in self.copies:
            copy.wait()


def forward_kernel(
    lengths, tables, ga, gm, w0_h, w1_h, w2_h, w3_h, w4_h, w5_h, w6_h, w7_h, og_h, wq_h, wk_h, wv_h, wo_h, wg_h, wu_h, wd_h,
    ggain_o, q_h, k_h, v_h, gmix_h, norm_h, gres_h, bo_h, skv_h, keep_h, send_h,
    win, og, wq, wk, wv, wo, wg, wu, wd, norm, q, k, v, kv, scores_all, probs_all, mixed, gmix, gres,
    bo, skv, acts, bias_s, bias_l, out_sum, grad_sum, win_sem, sems, out_sem,
):
    chip, core = place()
    short_at, long_at = starts(lengths)
    window_loads = []
    for side, (known, *rounds) in enumerate(((w0_h, w1_h, w2_h, w3_h), (w4_h, w5_h, w6_h, w7_h))):
        base = side * SIDE
        at = base
        for source, pieces in zip((known, *rounds), WINDOW_PARTS):
            first = 0
            for behind in pieces:
                if behind <= NEAR:
                    window_loads += [
                        (source.at[pl.ds(first + short_at, SHORT)], win.at[pl.ds(at, SHORT)]),
                        (source.at[pl.ds(first + long_at, LONG)], win.at[pl.ds(at + SHORT, LONG)]),
                    ]
                    first, at = first + TOK, at + TOK
                else:
                    window_loads.append((source.at[pl.ds(first, SHORT)], win.at[pl.ds(at, SHORT)]))
                    first, at = first + SHORT, at + SHORT
    window_loads = copies_of(window_loads, win_sem)
    names = ("wk", "wv", "wq", "wo", "ogs", "ogl", "wg", "wu", "wd")
    loads = dict(zip(names, copies_of((
        (wk_h, wk), (wv_h, wv), (wq_h, wq), (wo_h, wo),
        (og_h.at[pl.ds(short_at, SHORT)], og.at[pl.ds(0, SHORT)]),
        (og_h.at[pl.ds(long_at, LONG)], og.at[pl.ds(SHORT, LONG)]),
        (wg_h, wg), (wu_h, wu), (wd_h, wd),
    ), sems)))
    stores = Stores(out_sem)
    bias_s[...] = mask_bias("short", chip, core)
    bias_l[...] = mask_bias("long", chip, core)
    gain_a = ga[...].reshape(1, D)
    gain_m = gm[...].reshape(1, D)
    for copy in window_loads:
        copy.wait()

    def normalise(step, carry):
        rows = pl.ds(pl.multiple_of(step * NORM_ROWS, 16), NORM_ROWS)
        x = win[rows, :].astype(f32)
        scale = lax.rsqrt(jnp.mean(x * x, axis=-1, keepdims=True) + epsilon)
        norm[rows, :] = (x * scale * gain_a).astype(bf16)
        return carry

    lax.fori_loop(0, 2 * SIDE // NORM_ROWS, normalise, 0)
    stores.start(norm, norm_h)
    loads["wk"].wait()
    loads["wv"].wait()
    for side in range(2):
        normed = norm[side * SIDE : (side + 1) * SIDE, :]
        kv[:, :HD] = mm(normed, wk[...])
        kv[:, HD:] = mm(normed, wv[...])
        for number, group in enumerate(window_groups()):
            rows = slice(number * SHORT, (number + 1) * SHORT)
            cos, sin = group_tables(tables, chip, core, side, group)
            low_half, high_half = kv[rows, :HALF], kv[rows, HALF:HD]
            at = key_row(side, group)
            k[at : at + SHORT, :HALF] = (low_half * cos - high_half * sin).astype(bf16)
            k[at : at + SHORT, HALF:] = (high_half * cos + low_half * sin).astype(bf16)
            v[at : at + SHORT, :] = kv[rows, HD:].astype(bf16)
            if side == 0 and number < 3:
                skv[rows, :HD] = k[at : at + SHORT, :]
                skv[rows, HD:] = v[at : at + SHORT, :]
    stores.start(k, k_h)
    stores.start(v, v_h)
    stores.start(skv.at[pl.ds(0, SHORT)], skv_h.at[pl.ds(short_at, SHORT)])
    stores.start(skv.at[pl.ds(SHORT, LONG)], skv_h.at[pl.ds(long_at, LONG)])

    loads["wq"].wait()
    query_raw = mm(norm[:TOK, :], wq[...])
    for number in range(3):
        rows = slice(number * SHORT, (number + 1) * SHORT)
        cos, sin = group_tables(tables, chip, core, 0, window_groups()[number])
        for head in range(HEADS):
            low_half = query_raw[rows, head * HD : head * HD + HALF]
            high_half = query_raw[rows, head * HD + HALF : (head + 1) * HD]
            at = head * SHORT if number == 0 else HEADS * SHORT + head * LONG + (number - 1) * SHORT
            q[at : at + SHORT, :HALF] = (low_half * cos - high_half * sin).astype(bf16) * bf16(HD**-0.5)
            q[at : at + SHORT, HALF:] = (high_half * cos + low_half * sin).astype(bf16) * bf16(HD**-0.5)
    stores.start(q, q_h)

    for kind, rows, key_at, width, query_at, row_at in KINDS:
        bias = bias_s if kind == "short" else bias_l
        count = HEADS * rows
        scores_all[:count, :width] = mm_nt(q[query_at : query_at + count, :], k[key_at : key_at + width, :])
        for head in range(HEADS):
            here = slice(head * rows, (head + 1) * rows)
            scores = scores_all[here, :width] + bias[...]
            exponent = jnp.exp(scores - jnp.max(scores, axis=-1, keepdims=True))
            share = 1.0 / jnp.sum(exponent, axis=-1, keepdims=True)
            probs_all[here, :width] = (exponent * share).astype(bf16)
        mixed_all = mm(probs_all[:count, :width], v[key_at : key_at + width, :]).astype(bf16)
        for head in range(HEADS):
            mixed[row_at : row_at + rows, head * HD : (head + 1) * HD] = mixed_all[
                head * rows : (head + 1) * rows, :
            ]

    loads["wo"].wait()
    resid = win[:TOK, :].astype(f32) + mm(mixed[...], wo[...])
    scale = lax.rsqrt(jnp.mean(resid * resid, axis=-1, keepdims=True) + epsilon)
    unit = resid * scale
    normed_mlp = (unit * gain_m).astype(bf16)
    for name in ("ogs", "ogl", "wg", "wu", "wd"):
        loads[name].wait()
    grad_out = og[...]
    for half in range(2):
        acts[half, :, AT_MIXED:AT_NORMED] = mixed[:, half * 2 * HD : (half + 1) * 2 * HD]
        acts[half, :, AT_NORMED:AT_OUT] = normed_mlp
        acts[half, :, AT_OUT:AT_BRANCH] = grad_out
    out_sum[...] = resid
    grad_sum[...] = jnp.zeros((TOK, D), f32)

    def feed_forward(chunk, carry):
        cols = pl.ds(pl.multiple_of(chunk * FF_CHUNK, FF_CHUNK), FF_CHUNK)
        gate = mm(normed_mlp, wg[:, cols])
        up = mm(normed_mlp, wu[:, cols])
        sig = jax.nn.sigmoid(gate)
        silu = gate * sig
        act = (silu * up).astype(bf16)
        grad_act = mm_nt(grad_out, wd[cols, :])
        grad_gate = (grad_act * up * sig * (1.0 + gate * (1.0 - sig))).astype(bf16)
        grad_up = (grad_act * silu).astype(bf16)
        out_sum[...] += mm(act, wd[cols, :])
        grad_sum[...] += mm_nt(grad_gate, wg[:, cols]) + mm_nt(grad_up, wu[:, cols])
        half, at = chunk // 2, chunk % 2 * FF_CHUNK
        for first, values in ((0, act), (AT_GATE, grad_gate), (AT_UP, grad_up)):
            acts[half, :, pl.ds(pl.multiple_of(first + at, FF_CHUNK), FF_CHUNK)] = values
        return carry

    lax.fori_loop(0, FF // FF_CHUNK, feed_forward, 0, unroll=1)
    block_out, grad_normed = out_sum[...], grad_sum[...]
    stores.start(acts.at[1 - core, :, pl.ds(0, AT_BRANCH)], send_h.at[:, pl.ds(0, AT_BRANCH)])
    stores.start(acts.at[core, :, pl.ds(0, AT_BRANCH)], keep_h.at[:, pl.ds(0, AT_BRANCH)])
    ggain_o[...] = jnp.sum(grad_normed * unit, axis=0, keepdims=True)
    scaled = grad_normed * gain_m
    grad_resid = grad_out.astype(f32) + scale * (
        scaled - unit * jnp.mean(scaled * unit, axis=-1, keepdims=True)
    )
    grad_branch = grad_resid.astype(bf16)
    for half in range(2):
        acts[half, :, AT_BRANCH:] = grad_branch
    rest = pl.ds(AT_BRANCH, ACTS - AT_BRANCH)
    stores.start(acts.at[1 - core, :, rest], send_h.at[:, rest])
    stores.start(acts.at[core, :, rest], keep_h.at[:, rest])
    gres[...] = grad_resid
    stores.start(gres, gres_h)
    bo[...] = block_out.astype(bf16)
    stores.start(bo.at[pl.ds(0, SHORT)], bo_h.at[pl.ds(short_at, SHORT)])
    stores.start(bo.at[pl.ds(SHORT, LONG)], bo_h.at[pl.ds(long_at, LONG)])
    grad_mixed = mm_nt(grad_branch, wo[...]).astype(bf16)
    for head in range(HEADS):
        cols = slice(head * HD, (head + 1) * HD)
        gmix[head * SHORT : (head + 1) * SHORT, :] = grad_mixed[:SHORT, cols]
        at = HEADS * SHORT + head * LONG
        gmix[at : at + LONG, :] = grad_mixed[SHORT:, cols]
    stores.start(gmix, gmix_h)
    stores.wait()


def backward_kernel(
    tables, ga, q_h, k_h, v_h, gmix_h, norm_h, wq_h, wk_h, wv_h,
    mine_h, other_h, gnq_h, keep_h, send_h,
    q, k, v, gmix, norm, wq, wk, wv, scores_all, gp_all, probs_all, gs_all, ret, gq, gnq, b, bias_s, bias_l,
    sems, out_sem,
):
    chip, core = place()
    loads = copies_of((
        (q_h, q), (k_h, k), (gmix_h, gmix), (v_h, v), (norm_h, norm), (wq_h, wq), (wk_h, wk), (wv_h, wv),
    ), sems)
    stores = Stores(out_sem)
    bias_s[...] = mask_bias("short", chip, core)
    bias_l[...] = mask_bias("long", chip, core)
    for copy in loads[:4]:
        copy.wait()
    for kind, rows, key_at, width, query_at, row_at in KINDS:
        bias = bias_s if kind == "short" else bias_l
        keys = k[key_at : key_at + width, :]
        count = HEADS * rows
        stack = slice(query_at, query_at + count)
        scores_all[:count, :width] = mm_nt(q[stack, :], keys)
        gp_all[:count, :width] = mm_nt(gmix[stack, :], v[key_at : key_at + width, :])
        for head in range(HEADS):
            here = slice(head * rows, (head + 1) * rows)
            scores = scores_all[here, :width] + bias[...]
            exponent = jnp.exp(scores - jnp.max(scores, axis=-1, keepdims=True))
            probs = exponent * (1.0 / jnp.sum(exponent, axis=-1, keepdims=True))
            probs_all[here, :width] = probs.astype(bf16)
            grad_probs = gp_all[here, :width]
            inner = jnp.sum(probs * grad_probs, axis=-1, keepdims=True)
            gs_all[here, :width] = (probs * (grad_probs - inner)).astype(bf16)
        grad_queries = mm(gs_all[:count, :width], keys) * (HD**-0.5)
        for head in range(HEADS):
            for part in range(rows // SHORT):
                number = 0 if kind == "short" else 1 + part
                cos, sin = group_tables(tables, chip, core, 0, window_groups()[number])
                at = head * rows + part * SHORT
                low_half = grad_queries[at : at + SHORT, :HALF]
                high_half = grad_queries[at : at + SHORT, HALF:]
                to = slice(row_at + part * SHORT, row_at + (part + 1) * SHORT)
                gq[to, head * HD : head * HD + HALF] = (low_half * cos + high_half * sin).astype(bf16)
                gq[to, head * HD + HALF : (head + 1) * HD] = (high_half * cos - low_half * sin).astype(bf16)
        grad_keys = mm_tn(gs_all[:count, :width], q[stack, :])
        grad_values = mm_tn(probs_all[:count, :width], gmix[stack, :])
        for side in range(2):
            for number, group in enumerate(window_groups()):
                if group[1] != kind:
                    continue
                at = key_row(side, group) - key_at
                cos, sin = group_tables(tables, chip, core, side, group)
                low_half = grad_keys[at : at + SHORT, :HALF]
                high_half = grad_keys[at : at + SHORT, HALF:]
                to = slice(number * SHORT, (number + 1) * SHORT)
                ret[side, to, :HALF] = (low_half * cos + high_half * sin).astype(bf16)
                ret[side, to, HALF:HD] = (high_half * cos - low_half * sin).astype(bf16)
                ret[side, to, HD:] = grad_values[at : at + SHORT, :].astype(bf16)
    stores.start(ret.at[0], mine_h)
    stores.start(ret.at[1], other_h)
    for copy in loads[4:]:
        copy.wait()
    gnq[...] = mm_nt(gq[...], wq[...])
    stores.start(gnq, gnq_h)
    grad_gain = jnp.sum(gnq[...] * norm[:TOK, :].astype(f32), axis=0, keepdims=True)

    def gain_part(step, total):
        side, first = step // 4, pl.multiple_of(step % 4 * (SIDE // 4), 16)
        rows = pl.ds(first, SIDE // 4)
        grad_normed = mm_nt(ret[side, rows, :HD], wk[...]) + mm_nt(ret[side, rows, HD:], wv[...])
        here = norm[pl.ds(pl.multiple_of(side * SIDE + first, 16), SIDE // 4), :].astype(f32)
        return total + jnp.sum(grad_normed * here, axis=0, keepdims=True)

    grad_gain = lax.fori_loop(0, 8, gain_part, grad_gain, unroll=2)
    grad_gain = grad_gain / ga[...].reshape(1, D)

    def put(half, at, block):
        for part in range(block.shape[1] // HALF):
            row = at + part * D
            b[half, row : row + D, :] = block[:, part * HALF : (part + 1) * HALF].astype(bf16)

    b[0, B_GAIN:, :] = jnp.zeros((B_ROWS - B_GAIN, HALF), bf16)
    b[1, B_GAIN:, :] = jnp.zeros((B_ROWS - B_GAIN, HALF), bf16)
    for part in range(D // HALF):
        b[0, B_GAIN + 16 * part : B_GAIN + 16 * part + 16, :] = jnp.broadcast_to(
            grad_gain[:, part * HALF : (part + 1) * HALF], (16, HALF)
        ).astype(bf16)
    for half in range(2):
        put(half, B_QUERY, mm_tn(norm[:TOK, :], gq[:, half * 2 * HD : (half + 1) * 2 * HD]))
    both = mm_tn(norm[:SIDE, :], ret[0]) + mm_tn(norm[SIDE:, :], ret[1])
    for half in range(2):
        put(half, B_KV, both[:, half * HD : (half + 1) * HD])
    stores.start(b.at[1 - core], send_h)
    stores.start(b.at[core], keep_h)
    stores.wait()


def pieces_out(stores, pieces, outs):
    me = lax.axis_index("dp")
    for step, out in enumerate(outs):
        stores.start(pieces.at[lax.rem(me + step, DP)], out)


def halves_kernel(ggain, keep_h, recv_h, p0_h, p1_h, p2_h, p3_h, xz_h, x, pieces, xz, sems, out_sem):
    copies = copies_of(((keep_h, x.at[pl.ds(0, TOK)]), (recv_h, x.at[pl.ds(TOK, TOK)])), sems)
    stores = Stores(out_sem)
    for copy in copies:
        copy.wait()

    def write(at, values):
        done, rows = 0, values.shape[0]
        while done < rows:
            row = at + done
            if row < A_DP:
                piece, inner = row // A_DP_PIECE, row % A_DP_PIECE
                size = min(rows - done, A_DP_PIECE - inner)
                pieces[piece, inner : inner + size, :] = values[done : done + size, :]
            else:
                piece, inner = (row - A_DP) // A_XZ_PIECE, (row - A_DP) % A_XZ_PIECE
                size = min(rows - done, A_XZ_PIECE - inner)
                xz[piece, inner : inner + size, :] = values[done : done + size, :]
            done += size

    def put(at, block):
        rows = block.shape[0]
        for part in range(block.shape[1] // HALF):
            write(at + part * rows, block[:, part * HALF : (part + 1) * HALF].astype(bf16))

    normed = x[:, AT_NORMED:AT_OUT]
    for chunk in range(2):
        cols = slice(AT_GATE + chunk * FF_CHUNK, AT_GATE + (chunk + 1) * FF_CHUNK)
        put(A_GATE + chunk * 4 * D, mm_tn(normed, x[:, cols]))
    for chunk in range(2):
        cols = slice(AT_UP + chunk * FF_CHUNK, AT_UP + (chunk + 1) * FF_CHUNK)
        put(A_UP + chunk * 4 * D, mm_tn(normed, x[:, cols]))
        if chunk == 0:
            pieces_out(stores, pieces, (p0_h, p1_h, p2_h, p3_h))
    put(A_DOWN, mm_tn(x[:, :AT_GATE], x[:, AT_OUT:AT_BRANCH]))
    put(A_PROJ, mm_tn(x[:, AT_MIXED:AT_NORMED], x[:, AT_BRANCH:]))
    for part in range(D // HALF):
        write(A_GAIN + 16 * part, jnp.broadcast_to(
            ggain[:, part * HALF : (part + 1) * HALF], (16, HALF)
        ).astype(bf16))
    end = A_GAIN + 16 * (D // HALF)
    write(end, jnp.zeros((A_ROWS - end, HALF), bf16))
    stores.start(xz, xz_h)
    stores.wait()


def chip_sum_kernel(keep, recv, p0_h, p1_h, p2_h, p3_h, pieces, out_sem):
    stores = Stores(out_sem)
    for piece in range(DP):
        rows = slice(piece * B_PIECE, (piece + 1) * B_PIECE)
        pieces[piece] = (keep[rows, :].astype(f32) + recv[rows, :].astype(f32)).astype(bf16)
    pieces_out(stores, pieces, (p0_h, p1_h, p2_h, p3_h))
    stores.wait()


def first_sum_kernel(
    a0, a1, a2, a3, b0, b1, b2, b3, xz, out_xz, p0_h, p1_h, p2_h, p3_h, pieces, out_sem
):
    stores = Stores(out_sem)
    for piece in range(DP):
        rows = slice(piece * A_XZ_BLOCK, (piece + 1) * A_XZ_BLOCK)
        total = xz[0, rows, :].astype(f32)
        for chip in range(1, CHIPS):
            total = total + xz[chip, rows, :].astype(f32)
        pieces[piece] = total.astype(bf16)
    pieces_out(stores, pieces, (p0_h, p1_h, p2_h, p3_h))
    for chip in range(CHIPS):
        for at, size, parts in ((0, A_DP_BLOCK, (a0, a1, a2, a3)), (A_DP_BLOCK, B_BLOCK, (b0, b1, b2, b3))):
            rows = slice(chip * size, (chip + 1) * size)
            total = (parts[0][rows, :].astype(f32) + parts[1][rows, :].astype(f32)) + (
                parts[2][rows, :].astype(f32) + parts[3][rows, :].astype(f32)
            )
            out_xz[chip, at : at + size, :] = total.astype(bf16)
    stores.wait()


def second_sum_kernel(xz, c0, c1, c2, c3, copies_h, own, total, out_sem):
    stores = Stores(out_sem)
    rest = (
        (c0[...].astype(f32) + c1[...].astype(f32)) + (c2[...].astype(f32) + c3[...].astype(f32))
    ).astype(bf16)
    own[...] = rest[JOINED:, :]
    value = xz[0].astype(f32)
    for chip in range(1, CHIPS):
        value = value + xz[chip].astype(f32)
    total[: XZ_FIRST - JOINED, :] = value.astype(bf16)
    total[XZ_FIRST - JOINED :, :] = rest[:JOINED, :]
    for chip in range(CHIPS):
        stores.start(total, copies_h.at[chip])
    stores.wait()


def spread_kernel(d0, d1, d2, d3, copies_h, rows, out_sem):
    stores = Stores(out_sem)
    me = lax.axis_index("dp")
    for step, part in enumerate((d0, d1, d2, d3)):
        rows[lax.rem(me + DP - step, DP)] = part[...]
    for chip in range(CHIPS):
        stores.start(rows, copies_h.at[chip])
    stores.wait()


def window_sum_kernel(mine, other, known, r1, r2, r3):
    at = 0
    for out in (known, r1, r2, r3):
        rows = slice(at, at + out.shape[0])
        out[...] = (mine[rows, :].astype(f32) + other[rows, :].astype(f32)).astype(bf16)
        at += out.shape[0]


def turn_back_kernel(known, c1, c2, c3, own, back, far_back):
    ahead = lax.axis_index("z")
    own_sum = known[:TOK, :].astype(f32)
    back_sum = known[TOK : 2 * TOK, :].astype(f32)
    far_sum = known[2 * TOK :, :].astype(f32)
    for step, came in enumerate((c1, c2, c3), 1):
        same = (ahead + step < 4).astype(f32)
        near, far = came[:TOK, :].astype(f32), came[TOK:, :].astype(f32)
        own_sum = own_sum + near * same
        back_sum = back_sum + near * (1.0 - same)
        back_sum = jnp.concatenate([back_sum[:SHORT, :] + far * same, back_sum[SHORT:, :]], axis=0)
        far_sum = far_sum + far * (1.0 - same)
    own[...] = own_sum
    back[...] = back_sum.astype(bf16)
    far_back[...] = far_sum.astype(bf16)


def token_grad_kernel(lengths, ga, own, back, far_back, gnq, gres, tokens_h, wk, wv, out_h, x, out, sems):
    short_at, long_at = starts(lengths)
    loads = copies_of((
        (tokens_h.at[pl.ds(short_at, SHORT)], x.at[pl.ds(0, SHORT)]),
        (tokens_h.at[pl.ds(long_at, LONG)], x.at[pl.ds(SHORT, LONG)]),
    ), sems)
    total = own[...] + back[...].astype(f32)
    total = jnp.concatenate([total[:SHORT, :] + far_back[...].astype(f32), total[SHORT:, :]], axis=0).astype(bf16)
    grad_normed = gnq[...] + mm_nt(total[:, :HD], wk[...]) + mm_nt(total[:, HD:], wv[...])
    for copy in loads:
        copy.wait()
    wide = x[...].astype(f32)
    scale = lax.rsqrt(jnp.mean(wide * wide, axis=-1, keepdims=True) + epsilon)
    unit = wide * scale
    scaled = grad_normed * ga[...].reshape(1, D)
    out[...] = gres[...] + scale * (scaled - unit * jnp.mean(scaled * unit, axis=-1, keepdims=True))
    stores = copies_of((
        (out.at[pl.ds(0, SHORT)], out_h.at[pl.ds(short_at, SHORT)]),
        (out.at[pl.ds(SHORT, LONG)], out_h.at[pl.ds(long_at, LONG)]),
    ), sems, 2)
    for copy in stores:
        copy.wait()


def unpack_kernel(
    e0_h, e1_h, e2_h, e3_h, f_h, o0_h, o1_h, o2_h, o3_h, p_h,
    gain_a_o, gain_m_o, gate_h, up_h, down_h, proj_h, query_h, key_h, value_h,
    a_dp, a_xz, b, gate, up, down, proj, query, key, value, sems, out_sem,
):
    mine, me = lax.axis_index("core"), lax.axis_index("dp")
    sides = ((mine, (e0_h, e1_h, e2_h, e3_h), f_h), (1 - mine, (o0_h, o1_h, o2_h, o3_h), p_h))
    firsts, seconds, thirds = [], [], []
    for side, parts, xz_h in sides:
        for step, part in enumerate(parts):
            dp = lax.rem(me + DP - step, DP)
            firsts.append((part.at[:, pl.ds(0, A_DP_BLOCK)], a_dp.at[side, dp]))
            seconds.append((part.at[:, pl.ds(A_DP_BLOCK, B_BLOCK)], b.at[side, dp]))
            thirds.append((part.at[:, pl.ds(XZ_FIRST - JOINED, JOINED)], a_xz.at[side, :, dp, pl.ds(0, JOINED)]))
        thirds.append((xz_h, a_xz.at[side, :, :, pl.ds(JOINED, DP_FIRST)]))
    loads = copies_of(firsts + seconds + thirds, sems)
    stores = Stores(out_sem)

    def pieces_of(core, at, rows, in_b):
        done = 0
        while done < rows:
            row = at + done
            if in_b:
                source, size = b, B_BLOCK
                index = (core, row // B_PIECE, row % B_PIECE // B_BLOCK)
            elif row < A_DP:
                source, size = a_dp, A_DP_BLOCK
                index = (core, row // A_DP_PIECE, row % A_DP_PIECE // A_DP_BLOCK)
            else:
                row = row - A_DP
                source, size = a_xz, A_XZ_BLOCK
                index = (core, row // A_XZ_PIECE, row % A_XZ_PIECE // A_XZ_BLOCK)
            inner = row % size
            size = min(rows - done, size - inner)
            yield done, size, source[index + (slice(inner, inner + size), slice(None))].astype(f32)
            done += size

    def unpack(target, at, rows, in_b, place_of, count, cores=(0, 1)):
        for core in cores:
            for part in range(count):
                row, col = place_of(core, part)
                for done, size, values in pieces_of(core, at + part * rows, rows, in_b):
                    target[row + done : row + done + size, col : col + HALF] = values

    for copy in loads[: 2 * DP]:
        copy.wait()
    unpack(gate, A_GATE, D, False, lambda core, part: (0, core * HALF_FF + part * HALF), HALF_FF // HALF)
    stores.start(gate, gate_h)
    for copy in loads[2 * DP : 4 * DP]:
        copy.wait()
    unpack(query, B_QUERY, D, True, lambda core, part: (0, core * 2 * HD + part * HALF), 4)
    stores.start(query, query_h)
    unpack(key, B_KV, D, True, lambda core, part: (0, part * HALF), 2, (0,))
    stores.start(key, key_h)
    unpack(value, B_KV, D, True, lambda core, part: (0, part * HALF), 2, (1,))
    stores.start(value, value_h)
    for copy in loads[4 * DP :]:
        copy.wait()
    unpack(up, A_UP, D, False, lambda core, part: (0, core * HALF_FF + part * HALF), HALF_FF // HALF)
    stores.start(up, up_h)
    unpack(down, A_DOWN, HALF_FF, False, lambda core, part: (core * HALF_FF, part * HALF), D // HALF)
    stores.start(down, down_h)
    unpack(proj, A_PROJ, 2 * HD, False, lambda core, part: (core * 2 * HD, part * HALF), D // HALF)
    stores.start(proj, proj_h)
    for out, at, in_b in ((gain_a_o, B_GAIN, True), (gain_m_o, A_GAIN, False)):
        for part in range(D // HALF):
            (_, _, first), = pieces_of(0, at + 16 * part, 1, in_b)
            (_, _, second), = pieces_of(1, at + 16 * part, 1, in_b)
            out[part * HALF : (part + 1) * HALF] = (first + second).reshape(HALF)
    stores.wait()


VMEM = pl.BlockSpec(memory_space=pltpu.VMEM)
SMEM = pl.BlockSpec(memory_space=pltpu.SMEM)
ANY = pl.BlockSpec(memory_space=pl.ANY)


def shape(dims, kind=bf16):
    return jax.ShapeDtypeStruct(dims, kind)


def limit(mib):
    return pltpu.CompilerParams(vmem_limit_bytes=mib * 2**20)


def cost(flops, moved):
    return pl.CostEstimate(flops=flops, bytes_accessed=moved, transcendentals=0)


def scratch(*dims, kind=bf16):
    return pltpu.VMEM(dims, kind)


def semaphores(count):
    return pltpu.SemaphoreType.DMA((count,))


def run_forward(*operands):
    return pl.pallas_call(
        forward_kernel,
        in_specs=[SMEM] + [VMEM] * 3 + [ANY] * 16,
        out_specs=[VMEM] + [ANY] * 10,
        out_shape=[
            shape((1, D), f32),
            shape((HEADS * TOK, HD)), shape((KEYS, HD)), shape((KEYS, HD)), shape((HEADS * TOK, HD)),
            shape((2 * SIDE, D)), shape((TOK, D), f32),
            shape((TOK, D)), shape((TOK, 2 * HD)), shape((TOK, ACTS)), shape((TOK, ACTS)),
        ],
        scratch_shapes=[
            scratch(2 * SIDE, D), scratch(TOK, D), scratch(D, HEADS * HD), scratch(D, HD), scratch(D, HD),
            scratch(HEADS * HD, D), scratch(D, FF), scratch(D, FF), scratch(FF, D),
            scratch(2 * SIDE, D), scratch(HEADS * TOK, HD), scratch(KEYS, HD), scratch(KEYS, HD),
            scratch(SIDE, 2 * HD, kind=f32), scratch(HEADS * LONG, KEYS_LONG, kind=f32),
            scratch(HEADS * LONG, KEYS_LONG), scratch(TOK, HEADS * HD), scratch(HEADS * TOK, HD),
            scratch(TOK, D, kind=f32), scratch(TOK, D), scratch(TOK, 2 * HD), scratch(2, TOK, ACTS),
            scratch(SHORT, KEYS_SHORT, kind=f32), scratch(LONG, KEYS_LONG, kind=f32),
            scratch(TOK, D, kind=f32), scratch(TOK, D, kind=f32),
            semaphores(28), semaphores(9), semaphores(14),
        ],
        compiler_params=limit(58),
        cost_estimate=cost(8 * 10**9, 3 * 10**7),
        name="forward",
    )(*operands)


def run_backward(*operands):
    return pl.pallas_call(
        backward_kernel,
        in_specs=[VMEM] * 2 + [ANY] * 8,
        out_specs=[ANY] * 5,
        out_shape=[
            shape((SIDE, 2 * HD)), shape((SIDE, 2 * HD)), shape((TOK, D), f32),
            shape((B_ROWS, HALF)), shape((B_ROWS, HALF)),
        ],
        scratch_shapes=[
            scratch(HEADS * TOK, HD), scratch(KEYS, HD), scratch(KEYS, HD), scratch(HEADS * TOK, HD),
            scratch(2 * SIDE, D), scratch(D, HEADS * HD), scratch(D, HD), scratch(D, HD),
            scratch(HEADS * LONG, KEYS_LONG, kind=f32), scratch(HEADS * LONG, KEYS_LONG, kind=f32),
            scratch(HEADS * LONG, KEYS_LONG), scratch(HEADS * LONG, KEYS_LONG),
            scratch(2, SIDE, 2 * HD), scratch(TOK, HEADS * HD), scratch(TOK, D, kind=f32),
            scratch(2, B_ROWS, HALF),
            scratch(SHORT, KEYS_SHORT, kind=f32), scratch(LONG, KEYS_LONG, kind=f32),
            semaphores(8), semaphores(5),
        ],
        compiler_params=limit(54),
        cost_estimate=cost(10**12, 10**9),
        name="backward",
    )(*operands)


def run_halves(*operands):
    return pl.pallas_call(
        halves_kernel,
        in_specs=[VMEM, ANY, ANY],
        out_specs=[ANY] * 5,
        out_shape=[shape((A_DP_PIECE, HALF))] * 4 + [shape((CHIPS, A_XZ_PIECE, HALF))],
        scratch_shapes=[
            scratch(2 * TOK, ACTS), scratch(DP, A_DP_PIECE, HALF), scratch(CHIPS, A_XZ_PIECE, HALF),
            semaphores(2), semaphores(5),
        ],
        compiler_params=limit(20),
        cost_estimate=cost(2 * 10**9, 10**7),
        name="halves",
    )(*operands)


def run_chip_sum(*operands):
    return pl.pallas_call(
        chip_sum_kernel,
        in_specs=[VMEM] * 2,
        out_specs=[ANY] * 4,
        out_shape=[shape((B_PIECE, HALF))] * 4,
        scratch_shapes=[scratch(DP, B_PIECE, HALF), semaphores(4)],
        compiler_params=limit(8),
        cost_estimate=cost(0, 0),
        name="chip_sum",
    )(*operands)


def run_first_sum(*operands):
    return pl.pallas_call(
        first_sum_kernel,
        in_specs=[VMEM] * 9,
        out_specs=[VMEM] + [ANY] * 4,
        out_shape=[shape((CHIPS, A_DP_BLOCK + B_BLOCK, HALF))] + [shape((A_XZ_BLOCK, HALF))] * 4,
        scratch_shapes=[scratch(DP, A_XZ_BLOCK, HALF), semaphores(4)],
        compiler_params=limit(12),
        cost_estimate=cost(10**6, 8 * 10**6),
        name="first_sum",
    )(*operands)


def run_second_sum(*operands):
    return pl.pallas_call(
        second_sum_kernel,
        in_specs=[VMEM] * 5,
        out_specs=[ANY, VMEM],
        out_shape=[shape((CHIPS, XZ_FIRST, HALF)), shape((DP_FIRST, HALF))],
        scratch_shapes=[scratch(XZ_FIRST, HALF), semaphores(CHIPS)],
        compiler_params=limit(4),
        cost_estimate=cost(10**6, 10**6),
        name="second_sum",
    )(*operands)


def run_spread(*operands):
    return pl.pallas_call(
        spread_kernel,
        in_specs=[VMEM] * 4,
        out_specs=ANY,
        out_shape=shape((CHIPS, DP, DP_FIRST, HALF)),
        scratch_shapes=[scratch(DP, DP_FIRST, HALF), semaphores(CHIPS)],
        compiler_params=limit(4),
        cost_estimate=cost(0, 10**6),
        name="spread",
    )(*operands)


def run_unpack(*operands):
    return pl.pallas_call(
        unpack_kernel,
        in_specs=[ANY] * 10,
        out_specs=[VMEM] * 2 + [ANY] * 7,
        out_shape=[
            shape((D,), f32), shape((D,), f32), shape((D, FF), f32), shape((D, FF), f32),
            shape((FF, D), f32), shape((HEADS * HD, D), f32), shape((D, HEADS * HD), f32),
            shape((D, HD), f32), shape((D, HD), f32),
        ],
        scratch_shapes=[
            scratch(2, DP, CHIPS, A_DP_BLOCK, HALF), scratch(2, CHIPS, DP, A_XZ_BLOCK, HALF),
            scratch(2, DP, CHIPS, B_BLOCK, HALF),
            scratch(D, FF, kind=f32), scratch(D, FF, kind=f32), scratch(FF, D, kind=f32),
            scratch(HEADS * HD, D, kind=f32), scratch(D, HEADS * HD, kind=f32), scratch(D, HD, kind=f32),
            scratch(D, HD, kind=f32), semaphores(26), semaphores(7),
        ],
        compiler_params=limit(40),
        cost_estimate=cost(0, 3 * 10**7),
        name="unpack",
    )(*operands)


def run_window_sum(*operands):
    return pl.pallas_call(
        window_sum_kernel,
        in_specs=[VMEM] * 2,
        out_specs=[VMEM] * 4,
        out_shape=[shape((KNOWN, 2 * HD)), *[shape((ROUND, 2 * HD))] * 3],
        compiler_params=limit(8),
        cost_estimate=cost(0, 10**6),
        name="window_sum",
    )(*operands)


def run_turn_back(*operands):
    return pl.pallas_call(
        turn_back_kernel,
        in_specs=[VMEM] * 4,
        out_specs=[VMEM] * 3,
        out_shape=[shape((TOK, 2 * HD), f32), shape((TOK, 2 * HD)), shape((SHORT, 2 * HD))],
        compiler_params=limit(8),
        cost_estimate=cost(10**12, 10**9),
        name="turn_back",
    )(*operands)


def run_token_grad(*operands):
    return pl.pallas_call(
        token_grad_kernel,
        in_specs=[SMEM] + [VMEM] * 6 + [ANY] + [VMEM] * 2,
        out_specs=ANY,
        out_shape=shape((TOK, D), f32),
        scratch_shapes=[scratch(TOK, D), scratch(TOK, D, kind=f32), semaphores(4)],
        compiler_params=limit(12),
        cost_estimate=cost(10**6, 10**6),
        name="token_grad",
    )(*operands)


def swap_cores(array):
    return lax.ppermute(array, "core", [(0, 1), (1, 0)])


def gather_dp(pieces):
    got = [pieces[0]]
    for step in range(1, DP):
        got.append(lax.ppermute(pieces[step], "dp", [(i, (i + step) % DP) for i in range(DP)]))
    return got


def shards(
    tokens, lengths, w_query, w_key, w_value, w_output, w_gate, w_up, w_down, gain_attn, gain_mlp, out_grad
):
    short_first = lengths[0, 0] == SHORT_LEN

    slots = tokens[0]
    short_at = jnp.where(short_first, 0, LONG)

    def short_of(rows):
        return lax.dynamic_slice_in_dim(rows, short_at, SHORT, 0)

    own_short = short_of(slots)
    back = lax.ppermute(slots, "x", [(i, i + 1) for i in range(3)])
    back_short = lax.ppermute(own_short, "x", [(i, i + 2) for i in range(2)])
    here = jnp.concatenate([slots, short_of(back)], axis=0)
    there = jnp.concatenate([back, back_short], axis=0)
    ahead = lax.axis_index("z")
    rounds = [
        lax.ppermute(
            jnp.where(ahead + step < 4, here, there), "z", [(i, (i + step) % 4) for i in range(4)]
        )
        for step in range(1, 4)
    ]
    known = jnp.concatenate([slots, there], axis=0)
    window = [known, *rounds, *[swap_cores(part) for part in (known, *rounds)]]
    tables = jnp.asarray(rotary_tables())
    (
        grad_gain_mlp, q, k, v, gmix, norm, grad_resid, block_out, shared_kv, kept, sent,
    ) = run_forward(
        lengths, tables, gain_attn, gain_mlp, *window, out_grad[0],
        w_query, w_key, w_value, w_output, w_gate, w_up, w_down,
    )
    *a_pieces, a_xz = run_halves(grad_gain_mlp, kept, swap_cores(sent))
    q, a_xz = lax.optimization_barrier((q, a_xz))
    a_xz = lax.all_to_all(a_xz, CHIP, 0, 0, tiled=True)
    a_got = gather_dp(a_pieces)
    mine, other, grad_normed_q, b_kept, b_sent = run_backward(
        tables, gain_attn, q, k, v, gmix, norm, w_query, w_key, w_value
    )
    b_kept, b_sent, *a_got = lax.optimization_barrier((b_kept, b_sent, *a_got))
    b_pieces = run_chip_sum(b_kept, swap_cores(b_sent))
    b_got = gather_dp(b_pieces)

    other = swap_cores(other)
    b_got[1], other = lax.optimization_barrier((b_got[1], other))
    known_back, *round_back = run_window_sum(mine, other)
    came = [
        lax.ppermute(rows, "z", [(i, (i - step) % 4) for i in range(4)]) for step, rows in enumerate(round_back, 1)
    ]
    first, *c_pieces = run_first_sum(*a_got, *b_got, a_xz)
    c_got = gather_dp(c_pieces)
    first = lax.all_to_all(first, CHIP, 0, 0, tiled=True)
    own_back, for_back, for_far_back = run_turn_back(known_back, *came)
    copies, own_xz = run_second_sum(first, *c_got)
    copies, for_back, for_far_back = lax.optimization_barrier((copies, for_back, for_far_back))
    dp_part = lax.all_to_all(copies, CHIP, 0, 0, tiled=True)
    xz_copies = run_spread(*gather_dp([own_xz] * DP))
    dp_part, xz_copies = lax.optimization_barrier((dp_part, xz_copies))
    dp_parts = gather_dp([dp_part] * DP)
    xz_parts = lax.all_to_all(xz_copies, CHIP, 0, 0, tiled=True)
    parts = [*dp_parts, xz_parts]
    from_back = lax.ppermute(for_back, "x", [(i + 1, i) for i in range(3)])
    from_far_back = lax.ppermute(for_far_back, "x", [(i + 2, i) for i in range(2)])
    *parts, from_back, from_far_back = lax.optimization_barrier((*parts, from_back, from_far_back))
    (
        total_gain_attn, total_gain_mlp, grad_gate, grad_up, grad_down, grad_proj, grad_query, grad_key, grad_value,
    ) = run_unpack(*parts, *[swap_cores(part) for part in parts])

    input_grad = run_token_grad(
        lengths, gain_attn, own_back, from_back, from_far_back, grad_normed_q, grad_resid, slots, w_key, w_value
    )
    return (
        block_out[None], shared_kv[None], input_grad[None],
        grad_query, grad_key, grad_value, grad_proj, grad_gate, grad_up, grad_down,
        total_gain_attn, total_gain_mlp,
    )


def solution(mesh):
    fine = Mesh(mesh.devices.reshape(4, 4, 2, 4), ALL)
    rows = P("dp", SEQ, None)
    return jax.shard_map(
        shards,
        mesh=fine,
        in_specs=(rows, P("dp", None)) + (P(),) * 9 + (rows,),
        out_specs=(rows, rows, rows) + (P(),) * 9,
        check_vma=False,
    )
```

```python
import jax
import jax.numpy as jnp
import numpy as np
from jax import lax
from jax.experimental import pallas as pl
from jax.experimental.pallas import tpu as pltpu
from jax.sharding import Mesh, PartitionSpec as P

WINDOW = 1024
SHORT_LEN = 2048
D = 640
HEADS = 4
HD = 256
HALF = 128
FF = 2048
TOK = 192
SHORT = 64
LONG = 128
CHIPS = 16
NEAR = 4
FAR = 8
SIDE = (NEAR + 1) * TOK + (FAR - NEAR) * SHORT
GROUPS = SIDE // SHORT
WINDOW_PARTS = ((0, NEAR, FAR), (1, 5), (2, 6), (3, 7))
KNOWN = 2 * TOK + SHORT
ROUND = TOK + SHORT
KEYS_SHORT = 2 * (FAR + 1) * SHORT
KEYS_LONG = 2 * (NEAR + 1) * LONG
KEYS = KEYS_SHORT + KEYS_LONG
FF_CHUNK = 512
NORM_ROWS = 304

epsilon = 1e-06
theta_base = 10000.0
masked_score = -1e30

SEQ = ("x", "z", "core")
CHIP = ("x", "z")
ALL = ("x", "z", "core", "dp")
HALF_FF = FF // 2
AT_GATE, AT_UP, AT_MIXED, AT_NORMED, AT_OUT, AT_BRANCH = 1024, 2048, 3072, 3584, 4224, 4864
ACTS = 5504
A_GATE, A_UP, A_DOWN, A_PROJ, A_GAIN, A_ROWS = 0, 5120, 10240, 15360, 17920, 18432
B_QUERY, B_KV, B_GAIN, B_ROWS = 0, 2560, 3840, 4096
DP = 4
A_DP = 6144
A_XZ = A_ROWS - A_DP
A_DP_PIECE, B_PIECE, A_XZ_PIECE = A_DP // DP, B_ROWS // DP, A_XZ // CHIPS
A_DP_BLOCK, B_BLOCK, A_XZ_BLOCK = A_DP_PIECE // CHIPS, B_PIECE // CHIPS, A_XZ_PIECE // DP
BLOCK = A_DP_BLOCK + B_BLOCK + A_XZ_BLOCK
XZ_FIRST = 192
JOINED = XZ_FIRST - A_DP_BLOCK - B_BLOCK
DP_FIRST = A_XZ_BLOCK - JOINED

bf16 = jnp.bfloat16
f32 = jnp.float32


def mm(left, right):
    return jnp.dot(left, right, preferred_element_type=f32)


def mm_tn(left, right):
    return lax.dot_general(left, right, (((0,), (0,)), ((), ())), preferred_element_type=f32)


def mm_nt(left, right):
    return lax.dot_general(left, right, (((1,), (1,)), ((), ())), preferred_element_type=f32)


def window_groups():
    groups = []
    for pieces in WINDOW_PARTS:
        for behind in pieces:
            groups.append((behind, "short", 0))
            if behind <= NEAR:
                groups += [(behind, "long", 0), (behind, "long", 1)]
    return groups


def key_row(side, group):
    behind, kind, part = group
    if kind == "short":
        return side * (KEYS_SHORT // 2) + behind * SHORT
    return KEYS_SHORT + side * (KEYS_LONG // 2) + behind * LONG + part * SHORT


def mask_bias(kind, chip, core):
    rows, width, first_key = (SHORT, KEYS_SHORT, 0) if kind == "short" else (LONG, KEYS_LONG, 0)
    half = width // 2
    column = lax.broadcasted_iota(jnp.int32, (1, width), 1)
    other = (column >= half).astype(jnp.int32)
    inner = column - other * half
    shift = 6 if kind == "short" else 7
    behind = lax.shift_right_logical(inner, shift)
    rest = inner & (rows - 1)
    key_core = core + other * (1 - 2 * core)
    key_position = (2 * (chip - behind) + key_core) * rows + rest
    query_position = (2 * chip + core) * rows + lax.broadcasted_iota(jnp.int32, (rows, 1), 0)
    distance = query_position - key_position
    allowed = (key_position >= 0) & (distance >= 0) & (distance < WINDOW)
    return jnp.where(allowed, 0.0, masked_score).astype(f32)


def group_tables(tables, chip, core, side, group):
    behind, kind, part = group
    piece = 2 * (chip - behind) + (core if side == 0 else 1 - core)
    at = jnp.maximum(piece if kind == "short" else 2 * piece + part, 0)
    cb, sb = tables[0, pl.ds(at, 1), :], tables[1, pl.ds(at, 1), :]
    cr, sr = tables[2], tables[3]
    return cb * cr - sb * sr, sb * cr + cb * sr


def rotary_tables():
    frequency = theta_base ** (-(np.arange(HALF) * 2.0 / HD))
    far = np.arange(SHORT)[:, None] * SHORT * frequency[None, :]
    near = np.arange(SHORT)[:, None] * frequency[None, :]
    return np.stack([np.cos(far), np.sin(far), np.cos(near), np.sin(near)]).astype(np.float32)


def place():
    return lax.axis_index("x") * 4 + lax.axis_index("z"), lax.axis_index("core")


def starts(lengths):
    short_first = (lengths[0, 0] == SHORT_LEN).astype(jnp.int32)
    return pl.multiple_of((1 - short_first) * LONG, SHORT), pl.multiple_of(short_first * SHORT, SHORT)


KINDS = (
    ("short", SHORT, 0, KEYS_SHORT, 0, 0),
    ("long", LONG, KEYS_SHORT, KEYS_LONG, HEADS * SHORT, SHORT),
)


def copies_of(pairs, sems, first=0):
    copies = [
        pltpu.make_async_copy(source, target, sems.at[first + number])
        for number, (source, target) in enumerate(pairs)
    ]
    for copy in copies:
        copy.start()
    return copies


class Stores:
    def __init__(self, sems):
        self.sems, self.copies = sems, []

    def start(self, source, target):
        self.copies += copies_of([(source, target)], self.sems, len(self.copies))

    def wait(self):
        for copy in self.copies:
            copy.wait()


def forward_kernel(
    lengths, tables, ga, gm, w0_h, w1_h, w2_h, w3_h, w4_h, w5_h, w6_h, w7_h, og_h, wq_h, wk_h, wv_h, wo_h, wg_h, wu_h, wd_h,
    ggain_o, q_h, k_h, v_h, gmix_h, norm_h, gres_h, bo_h, skv_h, keep_h, send_h,
    win, og, wq, wk, wv, wo, wg, wu, wd, norm, q, k, v, kv, scores_all, probs_all, mixed, gmix, gres,
    bo, skv, acts, bias_s, bias_l, out_sum, grad_sum, win_sem, sems, out_sem,
):
    chip, core = place()
    short_at, long_at = starts(lengths)
    window_loads = []
    for side, (known, *rounds) in enumerate(((w0_h, w1_h, w2_h, w3_h), (w4_h, w5_h, w6_h, w7_h))):
        base = side * SIDE
        at = base
        for source, pieces in zip((known, *rounds), WINDOW_PARTS):
            first = 0
            for behind in pieces:
                if behind <= NEAR:
                    window_loads += [
                        (source.at[pl.ds(first + short_at, SHORT)], win.at[pl.ds(at, SHORT)]),
                        (source.at[pl.ds(first + long_at, LONG)], win.at[pl.ds(at + SHORT, LONG)]),
                    ]
                    first, at = first + TOK, at + TOK
                else:
                    window_loads.append((source.at[pl.ds(first, SHORT)], win.at[pl.ds(at, SHORT)]))
                    first, at = first + SHORT, at + SHORT
    window_loads = copies_of(window_loads, win_sem)
    names = ("wk", "wv", "wq", "wo", "ogs", "ogl", "wg", "wu", "wd")
    loads = dict(zip(names, copies_of((
        (wk_h, wk), (wv_h, wv), (wq_h, wq), (wo_h, wo),
        (og_h.at[pl.ds(short_at, SHORT)], og.at[pl.ds(0, SHORT)]),
        (og_h.at[pl.ds(long_at, LONG)], og.at[pl.ds(SHORT, LONG)]),
        (wg_h, wg), (wu_h, wu), (wd_h, wd),
    ), sems)))
    stores = Stores(out_sem)
    bias_s[...] = mask_bias("short", chip, core)
    bias_l[...] = mask_bias("long", chip, core)
    gain_a = ga[...].reshape(1, D)
    gain_m = gm[...].reshape(1, D)
    for copy in window_loads:
        copy.wait()

    def normalise(step, carry):
        rows = pl.ds(pl.multiple_of(step * NORM_ROWS, 16), NORM_ROWS)
        x = win[rows, :].astype(f32)
        scale = lax.rsqrt(jnp.mean(x * x, axis=-1, keepdims=True) + epsilon)
        norm[rows, :] = (x * scale * gain_a).astype(bf16)
        return carry

    lax.fori_loop(0, 2 * SIDE // NORM_ROWS, normalise, 0)
    stores.start(norm, norm_h)
    loads["wk"].wait()
    loads["wv"].wait()
    for side in range(2):
        normed = norm[side * SIDE : (side + 1) * SIDE, :]
        kv[:, :HD] = mm(normed, wk[...])
        kv[:, HD:] = mm(normed, wv[...])
        for number, group in enumerate(window_groups()):
            rows = slice(number * SHORT, (number + 1) * SHORT)
            cos, sin = group_tables(tables, chip, core, side, group)
            low_half, high_half = kv[rows, :HALF], kv[rows, HALF:HD]
            at = key_row(side, group)
            k[at : at + SHORT, :HALF] = (low_half * cos - high_half * sin).astype(bf16)
            k[at : at + SHORT, HALF:] = (high_half * cos + low_half * sin).astype(bf16)
            v[at : at + SHORT, :] = kv[rows, HD:].astype(bf16)
            if side == 0 and number < 3:
                skv[rows, :HD] = k[at : at + SHORT, :]
                skv[rows, HD:] = v[at : at + SHORT, :]
    stores.start(k, k_h)
    stores.start(v, v_h)
    stores.start(skv.at[pl.ds(0, SHORT)], skv_h.at[pl.ds(short_at, SHORT)])
    stores.start(skv.at[pl.ds(SHORT, LONG)], skv_h.at[pl.ds(long_at, LONG)])

    loads["wq"].wait()
    query_raw = mm(norm[:TOK, :], wq[...])
    for number in range(3):
        rows = slice(number * SHORT, (number + 1) * SHORT)
        cos, sin = group_tables(tables, chip, core, 0, window_groups()[number])
        for head in range(HEADS):
            low_half = query_raw[rows, head * HD : head * HD + HALF]
            high_half = query_raw[rows, head * HD + HALF : (head + 1) * HD]
            at = head * SHORT if number == 0 else HEADS * SHORT + head * LONG + (number - 1) * SHORT
            q[at : at + SHORT, :HALF] = (low_half * cos - high_half * sin).astype(bf16) * bf16(HD**-0.5)
            q[at : at + SHORT, HALF:] = (high_half * cos + low_half * sin).astype(bf16) * bf16(HD**-0.5)
    stores.start(q, q_h)

    for kind, rows, key_at, width, query_at, row_at in KINDS:
        bias = bias_s if kind == "short" else bias_l
        count = HEADS * rows
        scores_all[:count, :width] = mm_nt(q[query_at : query_at + count, :], k[key_at : key_at + width, :])
        for head in range(HEADS):
            here = slice(head * rows, (head + 1) * rows)
            scores = scores_all[here, :width] + bias[...]
            exponent = jnp.exp(scores - jnp.max(scores, axis=-1, keepdims=True))
            share = 1.0 / jnp.sum(exponent, axis=-1, keepdims=True)
            probs_all[here, :width] = (exponent * share).astype(bf16)
        mixed_all = mm(probs_all[:count, :width], v[key_at : key_at + width, :]).astype(bf16)
        for head in range(HEADS):
            mixed[row_at : row_at + rows, head * HD : (head + 1) * HD] = mixed_all[
                head * rows : (head + 1) * rows, :
            ]

    loads["wo"].wait()
    resid = win[:TOK, :].astype(f32) + mm(mixed[...], wo[...])
    scale = lax.rsqrt(jnp.mean(resid * resid, axis=-1, keepdims=True) + epsilon)
    unit = resid * scale
    normed_mlp = (unit * gain_m).astype(bf16)
    for name in ("ogs", "ogl", "wg", "wu", "wd"):
        loads[name].wait()
    grad_out = og[...]
    for half in range(2):
        acts[half, :, AT_MIXED:AT_NORMED] = mixed[:, half * 2 * HD : (half + 1) * 2 * HD]
        acts[half, :, AT_NORMED:AT_OUT] = normed_mlp
        acts[half, :, AT_OUT:AT_BRANCH] = grad_out
    out_sum[...] = resid
    grad_sum[...] = jnp.zeros((TOK, D), f32)

    def feed_forward(chunk, carry):
        cols = pl.ds(pl.multiple_of(chunk * FF_CHUNK, FF_CHUNK), FF_CHUNK)
        gate = mm(normed_mlp, wg[:, cols])
        up = mm(normed_mlp, wu[:, cols])
        sig = jax.nn.sigmoid(gate)
        silu = gate * sig
        act = (silu * up).astype(bf16)
        grad_act = mm_nt(grad_out, wd[cols, :])
        grad_gate = (grad_act * up * sig * (1.0 + gate * (1.0 - sig))).astype(bf16)
        grad_up = (grad_act * silu).astype(bf16)
        out_sum[...] += mm(act, wd[cols, :])
        grad_sum[...] += mm_nt(grad_gate, wg[:, cols]) + mm_nt(grad_up, wu[:, cols])
        half, at = chunk // 2, chunk % 2 * FF_CHUNK
        for first, values in ((0, act), (AT_GATE, grad_gate), (AT_UP, grad_up)):
            acts[half, :, pl.ds(pl.multiple_of(first + at, FF_CHUNK), FF_CHUNK)] = values
        return carry

    lax.fori_loop(0, FF // FF_CHUNK, feed_forward, 0, unroll=1)
    block_out, grad_normed = out_sum[...], grad_sum[...]
    stores.start(acts.at[1 - core, :, pl.ds(0, AT_BRANCH)], send_h.at[:, pl.ds(0, AT_BRANCH)])
    stores.start(acts.at[core, :, pl.ds(0, AT_BRANCH)], keep_h.at[:, pl.ds(0, AT_BRANCH)])
    ggain_o[...] = jnp.sum(grad_normed * unit, axis=0, keepdims=True)
    scaled = grad_normed * gain_m
    grad_resid = grad_out.astype(f32) + scale * (
        scaled - unit * jnp.mean(scaled * unit, axis=-1, keepdims=True)
    )
    grad_branch = grad_resid.astype(bf16)
    for half in range(2):
        acts[half, :, AT_BRANCH:] = grad_branch
    rest = pl.ds(AT_BRANCH, ACTS - AT_BRANCH)
    stores.start(acts.at[1 - core, :, rest], send_h.at[:, rest])
    stores.start(acts.at[core, :, rest], keep_h.at[:, rest])
    gres[...] = grad_resid
    stores.start(gres, gres_h)
    bo[...] = block_out.astype(bf16)
    stores.start(bo.at[pl.ds(0, SHORT)], bo_h.at[pl.ds(short_at, SHORT)])
    stores.start(bo.at[pl.ds(SHORT, LONG)], bo_h.at[pl.ds(long_at, LONG)])
    grad_mixed = mm_nt(grad_branch, wo[...]).astype(bf16)
    for head in range(HEADS):
        cols = slice(head * HD, (head + 1) * HD)
        gmix[head * SHORT : (head + 1) * SHORT, :] = grad_mixed[:SHORT, cols]
        at = HEADS * SHORT + head * LONG
        gmix[at : at + LONG, :] = grad_mixed[SHORT:, cols]
    stores.start(gmix, gmix_h)
    stores.wait()


def backward_kernel(
    tables, ga, q_h, k_h, v_h, gmix_h, norm_h, wq_h, wk_h, wv_h,
    mine_h, other_h, gnq_h, keep_h, send_h,
    q, k, v, gmix, norm, wq, wk, wv, scores_all, gp_all, probs_all, gs_all, ret, gq, gnq, b, bias_s, bias_l,
    sems, out_sem,
):
    chip, core = place()
    loads = copies_of((
        (q_h, q), (k_h, k), (gmix_h, gmix), (v_h, v), (norm_h, norm), (wq_h, wq), (wk_h, wk), (wv_h, wv),
    ), sems)
    stores = Stores(out_sem)
    bias_s[...] = mask_bias("short", chip, core)
    bias_l[...] = mask_bias("long", chip, core)
    for copy in loads[:4]:
        copy.wait()
    for kind, rows, key_at, width, query_at, row_at in KINDS:
        bias = bias_s if kind == "short" else bias_l
        keys = k[key_at : key_at + width, :]
        count = HEADS * rows
        stack = slice(query_at, query_at + count)
        scores_all[:count, :width] = mm_nt(q[stack, :], keys)
        gp_all[:count, :width] = mm_nt(gmix[stack, :], v[key_at : key_at + width, :])
        for head in range(HEADS):
            here = slice(head * rows, (head + 1) * rows)
            scores = scores_all[here, :width] + bias[...]
            exponent = jnp.exp(scores - jnp.max(scores, axis=-1, keepdims=True))
            probs = exponent * (1.0 / jnp.sum(exponent, axis=-1, keepdims=True))
            probs_all[here, :width] = probs.astype(bf16)
            grad_probs = gp_all[here, :width]
            inner = jnp.sum(probs * grad_probs, axis=-1, keepdims=True)
            gs_all[here, :width] = (probs * (grad_probs - inner)).astype(bf16)
        grad_queries = mm(gs_all[:count, :width], keys) * (HD**-0.5)
        for head in range(HEADS):
            for part in range(rows // SHORT):
                number = 0 if kind == "short" else 1 + part
                cos, sin = group_tables(tables, chip, core, 0, window_groups()[number])
                at = head * rows + part * SHORT
                low_half = grad_queries[at : at + SHORT, :HALF]
                high_half = grad_queries[at : at + SHORT, HALF:]
                to = slice(row_at + part * SHORT, row_at + (part + 1) * SHORT)
                gq[to, head * HD : head * HD + HALF] = (low_half * cos + high_half * sin).astype(bf16)
                gq[to, head * HD + HALF : (head + 1) * HD] = (high_half * cos - low_half * sin).astype(bf16)
        grad_keys = mm_tn(gs_all[:count, :width], q[stack, :])
        grad_values = mm_tn(probs_all[:count, :width], gmix[stack, :])
        for side in range(2):
            for number, group in enumerate(window_groups()):
                if group[1] != kind:
                    continue
                at = key_row(side, group) - key_at
                cos, sin = group_tables(tables, chip, core, side, group)
                low_half = grad_keys[at : at + SHORT, :HALF]
                high_half = grad_keys[at : at + SHORT, HALF:]
                to = slice(number * SHORT, (number + 1) * SHORT)
                ret[side, to, :HALF] = (low_half * cos + high_half * sin).astype(bf16)
                ret[side, to, HALF:HD] = (high_half * cos - low_half * sin).astype(bf16)
                ret[side, to, HD:] = grad_values[at : at + SHORT, :].astype(bf16)
    stores.start(ret.at[0], mine_h)
    stores.start(ret.at[1], other_h)
    for copy in loads[4:]:
        copy.wait()
    gnq[...] = mm_nt(gq[...], wq[...])
    stores.start(gnq, gnq_h)
    grad_gain = jnp.sum(gnq[...] * norm[:TOK, :].astype(f32), axis=0, keepdims=True)

    def gain_part(step, total):
        side, first = step // 4, pl.multiple_of(step % 4 * (SIDE // 4), 16)
        rows = pl.ds(first, SIDE // 4)
        grad_normed = mm_nt(ret[side, rows, :HD], wk[...]) + mm_nt(ret[side, rows, HD:], wv[...])
        here = norm[pl.ds(pl.multiple_of(side * SIDE + first, 16), SIDE // 4), :].astype(f32)
        return total + jnp.sum(grad_normed * here, axis=0, keepdims=True)

    grad_gain = lax.fori_loop(0, 8, gain_part, grad_gain, unroll=2)
    grad_gain = grad_gain / ga[...].reshape(1, D)

    def put(half, at, block):
        for part in range(block.shape[1] // HALF):
            row = at + part * D
            b[half, row : row + D, :] = block[:, part * HALF : (part + 1) * HALF].astype(bf16)

    b[0, B_GAIN:, :] = jnp.zeros((B_ROWS - B_GAIN, HALF), bf16)
    b[1, B_GAIN:, :] = jnp.zeros((B_ROWS - B_GAIN, HALF), bf16)
    for part in range(D // HALF):
        b[0, B_GAIN + 16 * part : B_GAIN + 16 * part + 16, :] = jnp.broadcast_to(
            grad_gain[:, part * HALF : (part + 1) * HALF], (16, HALF)
        ).astype(bf16)
    for half in range(2):
        put(half, B_QUERY, mm_tn(norm[:TOK, :], gq[:, half * 2 * HD : (half + 1) * 2 * HD]))
    both = mm_tn(norm[:SIDE, :], ret[0]) + mm_tn(norm[SIDE:, :], ret[1])
    for half in range(2):
        put(half, B_KV, both[:, half * HD : (half + 1) * HD])
    stores.start(b.at[1 - core], send_h)
    stores.start(b.at[core], keep_h)
    stores.wait()


def pieces_out(stores, pieces, outs):
    me = lax.axis_index("dp")
    for step, out in enumerate(outs):
        stores.start(pieces.at[lax.rem(me + step, DP)], out)


def halves_kernel(ggain, keep_h, recv_h, p0_h, p1_h, p2_h, p3_h, xz_h, x, pieces, xz, sems, out_sem):
    copies = copies_of(((keep_h, x.at[pl.ds(0, TOK)]), (recv_h, x.at[pl.ds(TOK, TOK)])), sems)
    stores = Stores(out_sem)
    for copy in copies:
        copy.wait()

    def write(at, values):
        done, rows = 0, values.shape[0]
        while done < rows:
            row = at + done
            if row < A_DP:
                piece, inner = row // A_DP_PIECE, row % A_DP_PIECE
                size = min(rows - done, A_DP_PIECE - inner)
                pieces[piece, inner : inner + size, :] = values[done : done + size, :]
            else:
                piece, inner = (row - A_DP) // A_XZ_PIECE, (row - A_DP) % A_XZ_PIECE
                size = min(rows - done, A_XZ_PIECE - inner)
                xz[piece, inner : inner + size, :] = values[done : done + size, :]
            done += size

    def put(at, block):
        rows = block.shape[0]
        for part in range(block.shape[1] // HALF):
            write(at + part * rows, block[:, part * HALF : (part + 1) * HALF].astype(bf16))

    normed = x[:, AT_NORMED:AT_OUT]
    for chunk in range(2):
        cols = slice(AT_GATE + chunk * FF_CHUNK, AT_GATE + (chunk + 1) * FF_CHUNK)
        put(A_GATE + chunk * 4 * D, mm_tn(normed, x[:, cols]))
    for chunk in range(2):
        cols = slice(AT_UP + chunk * FF_CHUNK, AT_UP + (chunk + 1) * FF_CHUNK)
        put(A_UP + chunk * 4 * D, mm_tn(normed, x[:, cols]))
        if chunk == 0:
            pieces_out(stores, pieces, (p0_h, p1_h, p2_h, p3_h))
    put(A_DOWN, mm_tn(x[:, :AT_GATE], x[:, AT_OUT:AT_BRANCH]))
    put(A_PROJ, mm_tn(x[:, AT_MIXED:AT_NORMED], x[:, AT_BRANCH:]))
    for part in range(D // HALF):
        write(A_GAIN + 16 * part, jnp.broadcast_to(
            ggain[:, part * HALF : (part + 1) * HALF], (16, HALF)
        ).astype(bf16))
    end = A_GAIN + 16 * (D // HALF)
    write(end, jnp.zeros((A_ROWS - end, HALF), bf16))
    stores.start(xz, xz_h)
    stores.wait()


def chip_sum_kernel(keep, recv, p0_h, p1_h, p2_h, p3_h, pieces, out_sem):
    stores = Stores(out_sem)
    for piece in range(DP):
        rows = slice(piece * B_PIECE, (piece + 1) * B_PIECE)
        pieces[piece] = (keep[rows, :].astype(f32) + recv[rows, :].astype(f32)).astype(bf16)
    pieces_out(stores, pieces, (p0_h, p1_h, p2_h, p3_h))
    stores.wait()


def first_sum_kernel(
    a0, a1, a2, a3, b0, b1, b2, b3, xz, out_xz, p0_h, p1_h, p2_h, p3_h, pieces, out_sem
):
    stores = Stores(out_sem)
    for piece in range(DP):
        rows = slice(piece * A_XZ_BLOCK, (piece + 1) * A_XZ_BLOCK)
        total = xz[0, rows, :].astype(f32)
        for chip in range(1, CHIPS):
            total = total + xz[chip, rows, :].astype(f32)
        pieces[piece] = total.astype(bf16)
    pieces_out(stores, pieces, (p0_h, p1_h, p2_h, p3_h))
    for chip in range(CHIPS):
        for at, size, parts in ((0, A_DP_BLOCK, (a0, a1, a2, a3)), (A_DP_BLOCK, B_BLOCK, (b0, b1, b2, b3))):
            rows = slice(chip * size, (chip + 1) * size)
            total = (parts[0][rows, :].astype(f32) + parts[1][rows, :].astype(f32)) + (
                parts[2][rows, :].astype(f32) + parts[3][rows, :].astype(f32)
            )
            out_xz[chip, at : at + size, :] = total.astype(bf16)
    stores.wait()


def second_sum_kernel(xz, c0, c1, c2, c3, copies_h, own, total, out_sem):
    stores = Stores(out_sem)
    rest = (
        (c0[...].astype(f32) + c1[...].astype(f32)) + (c2[...].astype(f32) + c3[...].astype(f32))
    ).astype(bf16)
    own[...] = rest[JOINED:, :]
    value = xz[0].astype(f32)
    for chip in range(1, CHIPS):
        value = value + xz[chip].astype(f32)
    total[: XZ_FIRST - JOINED, :] = value.astype(bf16)
    total[XZ_FIRST - JOINED :, :] = rest[:JOINED, :]
    for chip in range(CHIPS):
        stores.start(total, copies_h.at[chip])
    stores.wait()


def spread_kernel(d0, d1, d2, d3, copies_h, rows, out_sem):
    stores = Stores(out_sem)
    me = lax.axis_index("dp")
    for step, part in enumerate((d0, d1, d2, d3)):
        rows[lax.rem(me + DP - step, DP)] = part[...]
    for chip in range(CHIPS):
        stores.start(rows, copies_h.at[chip])
    stores.wait()


def window_sum_kernel(mine, other, known, r1, r2, r3):
    at = 0
    for out in (known, r1, r2, r3):
        rows = slice(at, at + out.shape[0])
        out[...] = (mine[rows, :].astype(f32) + other[rows, :].astype(f32)).astype(bf16)
        at += out.shape[0]


def turn_back_kernel(known, c1, c2, c3, own, back, far_back):
    ahead = lax.axis_index("z")
    own_sum = known[:TOK, :].astype(f32)
    back_sum = known[TOK : 2 * TOK, :].astype(f32)
    far_sum = known[2 * TOK :, :].astype(f32)
    for step, came in enumerate((c1, c2, c3), 1):
        same = (ahead + step < 4).astype(f32)
        near, far = came[:TOK, :].astype(f32), came[TOK:, :].astype(f32)
        own_sum = own_sum + near * same
        back_sum = back_sum + near * (1.0 - same)
        back_sum = jnp.concatenate([back_sum[:SHORT, :] + far * same, back_sum[SHORT:, :]], axis=0)
        far_sum = far_sum + far * (1.0 - same)
    own[...] = own_sum
    back[...] = back_sum.astype(bf16)
    far_back[...] = far_sum.astype(bf16)


def token_grad_kernel(lengths, ga, own, back, far_back, gnq, gres, tokens_h, wk, wv, out_h, x, out, sems):
    short_at, long_at = starts(lengths)
    loads = copies_of((
        (tokens_h.at[pl.ds(short_at, SHORT)], x.at[pl.ds(0, SHORT)]),
        (tokens_h.at[pl.ds(long_at, LONG)], x.at[pl.ds(SHORT, LONG)]),
    ), sems)
    total = own[...] + back[...].astype(f32)
    total = jnp.concatenate([total[:SHORT, :] + far_back[...].astype(f32), total[SHORT:, :]], axis=0).astype(bf16)
    grad_normed = gnq[...] + mm_nt(total[:, :HD], wk[...]) + mm_nt(total[:, HD:], wv[...])
    for copy in loads:
        copy.wait()
    wide = x[...].astype(f32)
    scale = lax.rsqrt(jnp.mean(wide * wide, axis=-1, keepdims=True) + epsilon)
    unit = wide * scale
    scaled = grad_normed * ga[...].reshape(1, D)
    out[...] = gres[...] + scale * (scaled - unit * jnp.mean(scaled * unit, axis=-1, keepdims=True))
    stores = copies_of((
        (out.at[pl.ds(0, SHORT)], out_h.at[pl.ds(short_at, SHORT)]),
        (out.at[pl.ds(SHORT, LONG)], out_h.at[pl.ds(long_at, LONG)]),
    ), sems, 2)
    for copy in stores:
        copy.wait()


def unpack_kernel(
    e0_h, e1_h, e2_h, e3_h, f_h, o0_h, o1_h, o2_h, o3_h, p_h,
    gain_a_o, gain_m_o, gate_h, up_h, down_h, proj_h, query_h, key_h, value_h,
    a_dp, a_xz, b, gate, up, down, proj, query, key, value, sems, out_sem,
):
    mine, me = lax.axis_index("core"), lax.axis_index("dp")
    sides = ((mine, (e0_h, e1_h, e2_h, e3_h), f_h), (1 - mine, (o0_h, o1_h, o2_h, o3_h), p_h))
    firsts, seconds, thirds = [], [], []
    for side, parts, xz_h in sides:
        for step, part in enumerate(parts):
            dp = lax.rem(me + DP - step, DP)
            firsts.append((part.at[:, pl.ds(0, A_DP_BLOCK)], a_dp.at[side, dp]))
            seconds.append((part.at[:, pl.ds(A_DP_BLOCK, B_BLOCK)], b.at[side, dp]))
            thirds.append((part.at[:, pl.ds(XZ_FIRST - JOINED, JOINED)], a_xz.at[side, :, dp, pl.ds(0, JOINED)]))
        thirds.append((xz_h, a_xz.at[side, :, :, pl.ds(JOINED, DP_FIRST)]))
    loads = copies_of(firsts + seconds + thirds, sems)
    stores = Stores(out_sem)

    def pieces_of(core, at, rows, in_b):
        done = 0
        while done < rows:
            row = at + done
            if in_b:
                source, size = b, B_BLOCK
                index = (core, row // B_PIECE, row % B_PIECE // B_BLOCK)
            elif row < A_DP:
                source, size = a_dp, A_DP_BLOCK
                index = (core, row // A_DP_PIECE, row % A_DP_PIECE // A_DP_BLOCK)
            else:
                row = row - A_DP
                source, size = a_xz, A_XZ_BLOCK
                index = (core, row // A_XZ_PIECE, row % A_XZ_PIECE // A_XZ_BLOCK)
            inner = row % size
            size = min(rows - done, size - inner)
            yield done, size, source[index + (slice(inner, inner + size), slice(None))].astype(f32)
            done += size

    def unpack(target, at, rows, in_b, place_of, count, cores=(0, 1)):
        for core in cores:
            for part in range(count):
                row, col = place_of(core, part)
                for done, size, values in pieces_of(core, at + part * rows, rows, in_b):
                    target[row + done : row + done + size, col : col + HALF] = values

    for copy in loads[: 2 * DP]:
        copy.wait()
    unpack(gate, A_GATE, D, False, lambda core, part: (0, core * HALF_FF + part * HALF), HALF_FF // HALF)
    stores.start(gate, gate_h)
    for copy in loads[2 * DP : 4 * DP]:
        copy.wait()
    unpack(query, B_QUERY, D, True, lambda core, part: (0, core * 2 * HD + part * HALF), 4)
    stores.start(query, query_h)
    unpack(key, B_KV, D, True, lambda core, part: (0, part * HALF), 2, (0,))
    stores.start(key, key_h)
    unpack(value, B_KV, D, True, lambda core, part: (0, part * HALF), 2, (1,))
    stores.start(value, value_h)
    for copy in loads[4 * DP :]:
        copy.wait()
    unpack(up, A_UP, D, False, lambda core, part: (0, core * HALF_FF + part * HALF), HALF_FF // HALF)
    stores.start(up, up_h)
    unpack(down, A_DOWN, HALF_FF, False, lambda core, part: (core * HALF_FF, part * HALF), D // HALF)
    stores.start(down, down_h)
    unpack(proj, A_PROJ, 2 * HD, False, lambda core, part: (core * 2 * HD, part * HALF), D // HALF)
    stores.start(proj, proj_h)
    for out, at, in_b in ((gain_a_o, B_GAIN, True), (gain_m_o, A_GAIN, False)):
        for part in range(D // HALF):
            (_, _, first), = pieces_of(0, at + 16 * part, 1, in_b)
            (_, _, second), = pieces_of(1, at + 16 * part, 1, in_b)
            out[part * HALF : (part + 1) * HALF] = (first + second).reshape(HALF)
    stores.wait()


VMEM = pl.BlockSpec(memory_space=pltpu.VMEM)
SMEM = pl.BlockSpec(memory_space=pltpu.SMEM)
ANY = pl.BlockSpec(memory_space=pl.ANY)


def shape(dims, kind=bf16):
    return jax.ShapeDtypeStruct(dims, kind)


def limit(mib):
    return pltpu.CompilerParams(vmem_limit_bytes=mib * 2**20)


def cost(flops, moved):
    return pl.CostEstimate(flops=flops, bytes_accessed=moved, transcendentals=0)


def scratch(*dims, kind=bf16):
    return pltpu.VMEM(dims, kind)


def semaphores(count):
    return pltpu.SemaphoreType.DMA((count,))


def run_forward(*operands):
    return pl.pallas_call(
        forward_kernel,
        in_specs=[SMEM] + [VMEM] * 3 + [ANY] * 16,
        out_specs=[VMEM] + [ANY] * 10,
        out_shape=[
            shape((1, D), f32),
            shape((HEADS * TOK, HD)), shape((KEYS, HD)), shape((KEYS, HD)), shape((HEADS * TOK, HD)),
            shape((2 * SIDE, D)), shape((TOK, D), f32),
            shape((TOK, D)), shape((TOK, 2 * HD)), shape((TOK, ACTS)), shape((TOK, ACTS)),
        ],
        scratch_shapes=[
            scratch(2 * SIDE, D), scratch(TOK, D), scratch(D, HEADS * HD), scratch(D, HD), scratch(D, HD),
            scratch(HEADS * HD, D), scratch(D, FF), scratch(D, FF), scratch(FF, D),
            scratch(2 * SIDE, D), scratch(HEADS * TOK, HD), scratch(KEYS, HD), scratch(KEYS, HD),
            scratch(SIDE, 2 * HD, kind=f32), scratch(HEADS * LONG, KEYS_LONG, kind=f32),
            scratch(HEADS * LONG, KEYS_LONG), scratch(TOK, HEADS * HD), scratch(HEADS * TOK, HD),
            scratch(TOK, D, kind=f32), scratch(TOK, D), scratch(TOK, 2 * HD), scratch(2, TOK, ACTS),
            scratch(SHORT, KEYS_SHORT, kind=f32), scratch(LONG, KEYS_LONG, kind=f32),
            scratch(TOK, D, kind=f32), scratch(TOK, D, kind=f32),
            semaphores(28), semaphores(9), semaphores(14),
        ],
        compiler_params=limit(58),
        cost_estimate=cost(8 * 10**9, 3 * 10**7),
        name="forward",
    )(*operands)


def run_backward(*operands):
    return pl.pallas_call(
        backward_kernel,
        in_specs=[VMEM] * 2 + [ANY] * 8,
        out_specs=[ANY] * 5,
        out_shape=[
            shape((SIDE, 2 * HD)), shape((SIDE, 2 * HD)), shape((TOK, D), f32),
            shape((B_ROWS, HALF)), shape((B_ROWS, HALF)),
        ],
        scratch_shapes=[
            scratch(HEADS * TOK, HD), scratch(KEYS, HD), scratch(KEYS, HD), scratch(HEADS * TOK, HD),
            scratch(2 * SIDE, D), scratch(D, HEADS * HD), scratch(D, HD), scratch(D, HD),
            scratch(HEADS * LONG, KEYS_LONG, kind=f32), scratch(HEADS * LONG, KEYS_LONG, kind=f32),
            scratch(HEADS * LONG, KEYS_LONG), scratch(HEADS * LONG, KEYS_LONG),
            scratch(2, SIDE, 2 * HD), scratch(TOK, HEADS * HD), scratch(TOK, D, kind=f32),
            scratch(2, B_ROWS, HALF),
            scratch(SHORT, KEYS_SHORT, kind=f32), scratch(LONG, KEYS_LONG, kind=f32),
            semaphores(8), semaphores(5),
        ],
        compiler_params=limit(54),
        cost_estimate=cost(10**12, 10**9),
        name="backward",
    )(*operands)


def run_halves(*operands):
    return pl.pallas_call(
        halves_kernel,
        in_specs=[VMEM, ANY, ANY],
        out_specs=[ANY] * 5,
        out_shape=[shape((A_DP_PIECE, HALF))] * 4 + [shape((CHIPS, A_XZ_PIECE, HALF))],
        scratch_shapes=[
            scratch(2 * TOK, ACTS), scratch(DP, A_DP_PIECE, HALF), scratch(CHIPS, A_XZ_PIECE, HALF),
            semaphores(2), semaphores(5),
        ],
        compiler_params=limit(20),
        cost_estimate=cost(2 * 10**9, 10**7),
        name="halves",
    )(*operands)


def run_chip_sum(*operands):
    return pl.pallas_call(
        chip_sum_kernel,
        in_specs=[VMEM] * 2,
        out_specs=[ANY] * 4,
        out_shape=[shape((B_PIECE, HALF))] * 4,
        scratch_shapes=[scratch(DP, B_PIECE, HALF), semaphores(4)],
        compiler_params=limit(8),
        cost_estimate=cost(0, 0),
        name="chip_sum",
    )(*operands)


def run_first_sum(*operands):
    return pl.pallas_call(
        first_sum_kernel,
        in_specs=[VMEM] * 9,
        out_specs=[VMEM] + [ANY] * 4,
        out_shape=[shape((CHIPS, A_DP_BLOCK + B_BLOCK, HALF))] + [shape((A_XZ_BLOCK, HALF))] * 4,
        scratch_shapes=[scratch(DP, A_XZ_BLOCK, HALF), semaphores(4)],
        compiler_params=limit(12),
        cost_estimate=cost(10**6, 8 * 10**6),
        name="first_sum",
    )(*operands)


def run_second_sum(*operands):
    return pl.pallas_call(
        second_sum_kernel,
        in_specs=[VMEM] * 5,
        out_specs=[ANY, VMEM],
        out_shape=[shape((CHIPS, XZ_FIRST, HALF)), shape((DP_FIRST, HALF))],
        scratch_shapes=[scratch(XZ_FIRST, HALF), semaphores(CHIPS)],
        compiler_params=limit(4),
        cost_estimate=cost(10**6, 10**6),
        name="second_sum",
    )(*operands)


def run_spread(*operands):
    return pl.pallas_call(
        spread_kernel,
        in_specs=[VMEM] * 4,
        out_specs=ANY,
        out_shape=shape((CHIPS, DP, DP_FIRST, HALF)),
        scratch_shapes=[scratch(DP, DP_FIRST, HALF), semaphores(CHIPS)],
        compiler_params=limit(4),
        cost_estimate=cost(0, 10**6),
        name="spread",
    )(*operands)


def run_unpack(*operands):
    return pl.pallas_call(
        unpack_kernel,
        in_specs=[ANY] * 10,
        out_specs=[VMEM] * 2 + [ANY] * 7,
        out_shape=[
            shape((D,), f32), shape((D,), f32), shape((D, FF), f32), shape((D, FF), f32),
            shape((FF, D), f32), shape((HEADS * HD, D), f32), shape((D, HEADS * HD), f32),
            shape((D, HD), f32), shape((D, HD), f32),
        ],
        scratch_shapes=[
            scratch(2, DP, CHIPS, A_DP_BLOCK, HALF), scratch(2, CHIPS, DP, A_XZ_BLOCK, HALF),
            scratch(2, DP, CHIPS, B_BLOCK, HALF),
            scratch(D, FF, kind=f32), scratch(D, FF, kind=f32), scratch(FF, D, kind=f32),
            scratch(HEADS * HD, D, kind=f32), scratch(D, HEADS * HD, kind=f32), scratch(D, HD, kind=f32),
            scratch(D, HD, kind=f32), semaphores(26), semaphores(7),
        ],
        compiler_params=limit(40),
        cost_estimate=cost(0, 3 * 10**7),
        name="unpack",
    )(*operands)


def run_window_sum(*operands):
    return pl.pallas_call(
        window_sum_kernel,
        in_specs=[VMEM] * 2,
        out_specs=[VMEM] * 4,
        out_shape=[shape((KNOWN, 2 * HD)), *[shape((ROUND, 2 * HD))] * 3],
        compiler_params=limit(8),
        cost_estimate=cost(0, 10**6),
        name="window_sum",
    )(*operands)


def run_turn_back(*operands):
    return pl.pallas_call(
        turn_back_kernel,
        in_specs=[VMEM] * 4,
        out_specs=[VMEM] * 3,
        out_shape=[shape((TOK, 2 * HD), f32), shape((TOK, 2 * HD)), shape((SHORT, 2 * HD))],
        compiler_params=limit(8),
        cost_estimate=cost(10**12, 10**9),
        name="turn_back",
    )(*operands)


def run_token_grad(*operands):
    return pl.pallas_call(
        token_grad_kernel,
        in_specs=[SMEM] + [VMEM] * 6 + [ANY] + [VMEM] * 2,
        out_specs=ANY,
        out_shape=shape((TOK, D), f32),
        scratch_shapes=[scratch(TOK, D), scratch(TOK, D, kind=f32), semaphores(4)],
        compiler_params=limit(12),
        cost_estimate=cost(10**6, 10**6),
        name="token_grad",
    )(*operands)


def swap_cores(array):
    return lax.ppermute(array, "core", [(0, 1), (1, 0)])


def gather_dp(pieces):
    got = [pieces[0]]
    for step in range(1, DP):
        got.append(lax.ppermute(pieces[step], "dp", [(i, (i + step) % DP) for i in range(DP)]))
    return got


def shards(
    tokens, lengths, w_query, w_key, w_value, w_output, w_gate, w_up, w_down, gain_attn, gain_mlp, out_grad
):
    short_first = lengths[0, 0] == SHORT_LEN

    slots = tokens[0]
    short_at = jnp.where(short_first, 0, LONG)

    def short_of(rows):
        return lax.dynamic_slice_in_dim(rows, short_at, SHORT, 0)

    own_short = short_of(slots)
    back = lax.ppermute(slots, "x", [(i, i + 1) for i in range(3)])
    back_short = lax.ppermute(own_short, "x", [(i, i + 2) for i in range(2)])
    here = jnp.concatenate([slots, short_of(back)], axis=0)
    there = jnp.concatenate([back, back_short], axis=0)
    ahead = lax.axis_index("z")
    rounds = [
        lax.ppermute(
            jnp.where(ahead + step < 4, here, there), "z", [(i, (i + step) % 4) for i in range(4)]
        )
        for step in range(1, 4)
    ]
    known = jnp.concatenate([slots, there], axis=0)
    window = [known, *rounds, *[swap_cores(part) for part in (known, *rounds)]]
    tables = jnp.asarray(rotary_tables())
    (
        grad_gain_mlp, q, k, v, gmix, norm, grad_resid, block_out, shared_kv, kept, sent,
    ) = run_forward(
        lengths, tables, gain_attn, gain_mlp, *window, out_grad[0],
        w_query, w_key, w_value, w_output, w_gate, w_up, w_down,
    )
    *a_pieces, a_xz = run_halves(grad_gain_mlp, kept, swap_cores(sent))
    q, a_xz = lax.optimization_barrier((q, a_xz))
    a_xz = lax.all_to_all(a_xz, CHIP, 0, 0, tiled=True)
    a_got = gather_dp(a_pieces)
    mine, other, grad_normed_q, b_kept, b_sent = run_backward(
        tables, gain_attn, q, k, v, gmix, norm, w_query, w_key, w_value
    )
    b_kept, b_sent, *a_got = lax.optimization_barrier((b_kept, b_sent, *a_got))
    b_pieces = run_chip_sum(b_kept, swap_cores(b_sent))
    b_got = gather_dp(b_pieces)

    other = swap_cores(other)
    b_got[1], other = lax.optimization_barrier((b_got[1], other))
    known_back, *round_back = run_window_sum(mine, other)
    came = [
        lax.ppermute(rows, "z", [(i, (i - step) % 4) for i in range(4)]) for step, rows in enumerate(round_back, 1)
    ]
    first, *c_pieces = run_first_sum(*a_got, *b_got, a_xz)
    c_got = gather_dp(c_pieces)
    first = lax.all_to_all(first, CHIP, 0, 0, tiled=True)
    own_back, for_back, for_far_back = run_turn_back(known_back, *came)
    copies, own_xz = run_second_sum(first, *c_got)
    copies, for_back, for_far_back = lax.optimization_barrier((copies, for_back, for_far_back))
    dp_part = lax.all_to_all(copies, CHIP, 0, 0, tiled=True)
    xz_copies = run_spread(*gather_dp([own_xz] * DP))
    dp_part, xz_copies = lax.optimization_barrier((dp_part, xz_copies))
    dp_parts = gather_dp([dp_part] * DP)
    xz_parts = lax.all_to_all(xz_copies, CHIP, 0, 0, tiled=True)
    parts = [*dp_parts, xz_parts]
    from_back = lax.ppermute(for_back, "x", [(i + 1, i) for i in range(3)])
    from_far_back = lax.ppermute(for_far_back, "x", [(i + 2, i) for i in range(2)])
    *parts, from_back, from_far_back = lax.optimization_barrier((*parts, from_back, from_far_back))
    (
        total_gain_attn, total_gain_mlp, grad_gate, grad_up, grad_down, grad_proj, grad_query, grad_key, grad_value,
    ) = run_unpack(*parts, *[swap_cores(part) for part in parts])

    input_grad = run_token_grad(
        lengths, gain_attn, own_back, from_back, from_far_back, grad_normed_q, grad_resid, slots, w_key, w_value
    )
    return (
        block_out[None], shared_kv[None], input_grad[None],
        grad_query, grad_key, grad_value, grad_proj, grad_gate, grad_up, grad_down,
        total_gain_attn, total_gain_mlp,
    )


def solution(mesh):
    fine = Mesh(mesh.devices.reshape(4, 4, 2, 4), ALL)
    rows = P("dp", SEQ, None)
    return jax.shard_map(
        shards,
        mesh=fine,
        in_specs=(rows, P("dp", None)) + (P(),) * 9 + (rows,),
        out_specs=(rows, rows, rows) + (P(),) * 9,
        check_vma=False,
    )
```
